128 devices in a mesh: row: 4 (over z), ctx: 4 (over y_lo, core), head: 8 (over y_hi, x).
Axes of the slice: x: 4, y: 4 (y_hi: 2, y_lo: 2; y = y_hi * 2 + y_lo), z: 4, core: 2. Of those that a mesh axis runs over, the one named last changes fastest.
Arguments:
- tokens: bfloat16 [4, 4096, 1536], P('row', ('ctx', 'head')), may hold values from -6 to 6
- doc_lengths: int32 [4, 8], P('row'), may hold values from 1 to 3392, as said below
- w_query: bfloat16 [1536, 1536], P(('row', 'ctx')), may hold values from -0.15625 to 0.15625
- w_key: bfloat16 [1536, 768], P(('row', 'ctx')), may hold values from -0.15625 to 0.15625
- w_value: bfloat16 [1536, 768], P(('row', 'ctx')), may hold values from -0.15625 to 0.15625
- w_output: bfloat16 [1536, 1536], P(('row', 'ctx')), may hold values from -2.5 to 2.5
- w_gate: bfloat16 [1536, 4096], P(('row', 'ctx')), may hold values from -0.15625 to 0.15625
- w_up: bfloat16 [1536, 4096], P(('row', 'ctx')), may hold values from -0.15625 to 0.15625
- w_down: bfloat16 [4096, 1536], P(('row', 'ctx')), may hold values from -0.09375 to 0.09375
- gain_attn: bfloat16 [1536], P(('row', 'ctx')), may hold values from 0.25 to 1.75
- gain_mlp: bfloat16 [1536], P(('row', 'ctx')), may hold values from 0.25 to 1.75
- cotangent: bfloat16 [4, 4096, 1536], P('row', ('ctx', 'head')), may hold values from -6 to 6
Outputs:
- layer_out: bfloat16 [4, 4096, 1536], P('row', ('ctx', 'head'))
- tokens_grad: bfloat16 [4, 4096, 1536], P('row', ('ctx', 'head'))
- grad_query: float32 [1536, 1536], P(('row', 'ctx'))
- grad_key: float32 [1536, 768], P(('row', 'ctx'))
- grad_value: float32 [1536, 768], P(('row', 'ctx'))
- grad_output: float32 [1536, 1536], P(('row', 'ctx'))
- grad_gate: float32 [1536, 4096], P(('row', 'ctx'))
- grad_up: float32 [1536, 4096], P(('row', 'ctx'))
- grad_down: float32 [4096, 1536], P(('row', 'ctx'))
- grad_gain_attn: float32 [1536], P(('row', 'ctx'))
- grad_gain_mlp: float32 [1536], P(('row', 'ctx'))
The draws below stay inside these ranges and needn't reach their ends.
Inputs may be any that keep to these rules, and one draw needn't show every extreme that they name: `doc_lengths`: each row's 8 document lengths, in order from position 0; their sum is less than 4096, and the positions after it are padding. In every row one document has the largest length and another has length 1.
All inputs are finite; a program needn't handle non-finite values.
Results may differ from the reference program's by a relative error of at most 0.025.
Values may be sent and summed in bfloat16 or wider, within the bound.
A program may use at most 256 MiB of HBM per device.

```python
import jax
import jax.numpy as jnp
import numpy as np
from jax import lax

D = 1536
HEADS = 16
KV = 8
HD = 96
FF = 4096
NDOC = 8
SEQ = 4096
ROWS = 4
N_CTX = 4


def draw_doc_lengths(key, part):
    key = jax.random.fold_in(key, 11)
    portion = SEQ // N_CTX
    small_top = max(3, portion // (2 * NDOC) + 1)
    tail = max(1, portion // 4)
    longest_len = SEQ - (NDOC - 1) * (small_top - 1) - tail
    key_small, key_long = jax.random.split(key, 2)
    shorts = jax.random.randint(key_small, (ROWS, NDOC), 1, small_top)
    longest = jax.random.randint(key_long, (ROWS, 1), 0, NDOC)
    positions = jnp.arange(NDOC)[None, :]
    chosen = positions == longest
    single = positions == (longest + 1) % NDOC
    return jnp.where(chosen, longest_len, jnp.where(single, 1, shorts)).astype(jnp.int32)


def block_levels(rng, dims, cuts, smallest, top_value):
    factor_of, own = 1.0, jax.random.fold_in(rng, 6)
    for position, shards_of in cuts:
        draws = jnp.exp(jax.random.uniform(jax.random.fold_in(own, position), (shards_of,), jnp.float32, smallest / len(cuts), top_value / len(cuts)))
        factor_of = factor_of * jnp.repeat(draws, dims[position] // shards_of).reshape([-1 if axis == position else 1 for axis in range(len(dims))])
    return factor_of


def gaussian(key, extent, width, bound, shards=(), held_as=jnp.bfloat16):
    values = width * jax.random.normal(key, extent, jnp.float32)
    if shards:
        values = values * block_levels(key, extent, shards, -0.22, 0.18)
    return jnp.clip(values, -bound, bound).astype(held_as)


def setup_inputs(seed: int = 0) -> dict:
    arg_keys = jax.random.split(jax.random.key(seed), 13)
    tokens = gaussian(arg_keys[0], (ROWS, SEQ, D), 1.0, 6.0, ((0, 4), (1, 32)))
    doc_lengths = draw_doc_lengths(jax.random.fold_in(arg_keys[12], 71), 0)
    w_query = gaussian(arg_keys[2], (D, D), D ** -0.5, 0.15625, ((0, 16),))
    w_key = gaussian(arg_keys[3], (D, KV * HD), D ** -0.5, 0.15625, ((0, 16),))
    w_value = gaussian(arg_keys[4], (D, KV * HD), D ** -0.5, 0.15625, ((0, 16),))
    w_output = gaussian(arg_keys[5], (D, D), (max(1, D * 16 // SEQ)) ** -0.5, 2.5, ((0, 16),))
    w_gate = gaussian(arg_keys[6], (D, FF), D ** -0.5, 0.15625, ((0, 16),))
    w_up = gaussian(arg_keys[7], (D, FF), D ** -0.5, 0.15625, ((0, 16),))
    w_down = gaussian(arg_keys[8], (FF, D), FF ** -0.5, 0.09375, ((0, 16),))
    gain_attn = jnp.clip(1.0 + 0.15 * jax.random.normal(arg_keys[9], (D,), jnp.float32), 0.25, 1.75).astype(jnp.bfloat16)
    gain_mlp = jnp.clip(1.0 + 0.15 * jax.random.normal(arg_keys[10], (D,), jnp.float32), 0.25, 1.75).astype(jnp.bfloat16)
    cotangent = gaussian(arg_keys[11], (ROWS, SEQ, D), 1.0, 6.0, ((0, 4), (1, 32)))
    return {"tokens": tokens, "doc_lengths": doc_lengths, "w_query": w_query, "w_key": w_key, "w_value": w_value, "w_output": w_output, "w_gate": w_gate, "w_up": w_up, "w_down": w_down, "gain_attn": gain_attn, "gain_mlp": gain_mlp, "cotangent": cotangent}


@jax.custom_vjp
def low(v):
    return lax.optimization_barrier(v.astype(jnp.bfloat16)).astype(jnp.float32)

@jax.custom_vjp
def low_back(v):
    return v

def low_keep(v):
    return (low(v), None)

def low_pass(kept, grad):
    return (grad,)

def back_keep(v):
    return (v, None)

def back_low(kept, grad):
    return (low(grad),)
low.defvjp(low_keep, low_pass)
low_back.defvjp(back_keep, back_low)
NORM_EPS = 1e-05
HIGHEST = lax.Precision.HIGHEST

def frequency_table(head_width):
    halfway = head_width // 2
    base_freq = 500000.0 ** (-np.arange(halfway) * 2.0 / head_width)
    wavelength = 2.0 * np.pi / base_freq
    smooth = (8192.0 / wavelength - 1.0) / 3.0
    middle = (1.0 - smooth) * base_freq / 32.0 + smooth * base_freq
    freq_table = np.where(wavelength > 8192.0, base_freq / 32.0, np.where(wavelength < 2048.0, base_freq, middle))
    return freq_table.astype(np.float32)

def doc_layout(lengths, places):
    doc_count = lengths.shape[0]
    doc_ends = jnp.cumsum(lengths).astype(jnp.int32)
    starts = (doc_ends - lengths).astype(jnp.int32)
    segment = lax.optimization_barrier(jnp.sum((places[:, None] >= doc_ends[None, :]).astype(jnp.int32), axis=1)).astype(jnp.int32)
    chosen = segment[:, None] == jnp.arange(doc_count, dtype=jnp.int32)[None, :]
    offset = lax.optimization_barrier(jnp.sum(jnp.where(chosen, starts[None, :], 0), axis=1)) + jnp.where(segment == doc_count, doc_ends[doc_count - 1], 0)
    return (segment, (places - offset).astype(jnp.int32))

def rope_angles(offsets):
    frequency = jnp.asarray(frequency_table(HD))
    angles = offsets.astype(jnp.float32)[:, None] * frequency[None, :]
    return (jnp.cos(angles), jnp.sin(angles))

def rotate(vectors, cosine, sine_part):
    halfway = vectors.shape[-1] // 2
    first_half = vectors[..., :halfway]
    second = vectors[..., halfway:]
    cos_b = cosine[:, None, :]
    sin_b = sine_part[:, None, :]
    return jnp.concatenate([first_half * cos_b - second * sin_b, second * cos_b + first_half * sin_b], axis=-1)

def matmul(left_side, right_side):
    return jnp.dot(left_side, right_side, precision=HIGHEST)

def layer_row(inputs, lengths, w_query, w_key, w_value, w_output, w_gate, w_up, w_down, gain_attn, gain_mlp):
    seq_len = inputs.shape[0]
    places = jnp.arange(seq_len, dtype=jnp.int32)
    segment, offsets = doc_layout(lengths, places)
    valid = (segment < lengths.shape[0]).astype(inputs.dtype)
    cosine, sine_part = rope_angles(offsets)
    norm_attn = inputs * lax.rsqrt(lax.optimization_barrier(jnp.mean(inputs * inputs, axis=1, keepdims=True)) + NORM_EPS)
    h_attn = low(norm_attn * gain_attn)
    queries = low_back(matmul(h_attn, w_query)).reshape(seq_len, HEADS, HD)
    keyset = low_back(matmul(h_attn, w_key)).reshape(seq_len, KV, HD)
    values = low(low_back(matmul(h_attn, w_value))).reshape(seq_len, KV, HD)
    queries = low(rotate(queries, cosine, sine_part))
    keyset = low(rotate(keyset, cosine, sine_part))
    grouped = queries.reshape(seq_len, KV, HEADS // KV, HD).transpose(1, 2, 0, 3)
    allowed = (segment[:, None] == segment[None, :]) & (places[None, :] <= places[:, None])

    def one_group(operands):
        group_q, group_k, group_v = operands
        scores = low_back(jnp.einsum('pqd,kd->pqk', group_q, group_k, precision=HIGHEST) * HD ** (-0.5))
        scores = jnp.where(allowed[None], scores, -jnp.inf)
        shifted = jnp.exp(scores - lax.optimization_barrier(jnp.max(scores, axis=2, keepdims=True)))
        probs_full = shifted / lax.optimization_barrier(jnp.sum(shifted, axis=2, keepdims=True))
        return jnp.einsum('pqk,kd->pqd', low(probs_full), group_v, precision=HIGHEST)
    attended = lax.map(jax.checkpoint(one_group), (grouped, keyset.transpose(1, 0, 2), values.transpose(1, 0, 2)))
    attended = attended.transpose(2, 0, 1, 3).reshape(seq_len, HEADS * HD) * valid[:, None]
    attn_low = low(low_back(attended))
    resid = inputs + low_back(matmul(attn_low, w_output))
    norm_mlp = resid * lax.rsqrt(lax.optimization_barrier(jnp.mean(resid * resid, axis=1, keepdims=True)) + NORM_EPS)
    h_mlp = low(norm_mlp * gain_mlp)
    gate_pre = low_back(matmul(h_mlp, w_gate))
    up_pre = low_back(matmul(h_mlp, w_up))
    hidden = low(jax.nn.silu(gate_pre) * up_pre)
    return resid + low_back(matmul(hidden, w_down))

def reference(tokens, doc_lengths, w_query, w_key, w_value, w_output, w_gate, w_up, w_down, gain_attn, gain_mlp, cotangent):
    floats = [weight_item.astype(jnp.float32) for weight_item in (w_query, w_key, w_value, w_output, w_gate, w_up, w_down, gain_attn, gain_mlp)]

    def forward(inputs, *params):

        def one_row(operands):
            row_input, row_lengths = operands
            return layer_row(row_input, row_lengths, *params)
        return lax.map(jax.checkpoint(one_row), (inputs, doc_lengths))
    result, pullback = jax.vjp(forward, tokens.astype(jnp.float32), *floats)
    gradients = pullback(cotangent.astype(jnp.float32))
    return (result.astype(jnp.bfloat16), gradients[0].astype(jnp.bfloat16), gradients[1], gradients[2], gradients[3], gradients[4], gradients[5], gradients[6], gradients[7], gradients[8], gradients[9])
```

```python
from functools import partial

import jax
import jax.numpy as jnp
import numpy as np
from jax import lax
from jax.experimental import pallas as pl
from jax.experimental.pallas import tpu as pltpu
from jax.sharding import Mesh
from jax.sharding import PartitionSpec as P

HEADS = 16
KV = 8
HD = 96
NORM_EPS = 1e-05
LOG2E = 1.4426950408889634
LN2 = 0.6931471805599453
SCALE = HD ** (-0.5)
BF = jnp.bfloat16
F32 = jnp.float32
AXES = ("z", "yl", "c", "yh", "x")
GROUP = ("yl", "c", "yh")
MESH = pl.DeviceIdType.MESH
TOK = 128
NT = 8
NX = 4


def frequency_table(head_width):
    halfway = head_width // 2
    base_freq = 500000.0 ** (-np.arange(halfway) * 2.0 / head_width)
    wavelength = 2.0 * np.pi / base_freq
    smooth = (8192.0 / wavelength - 1.0) / 3.0
    middle = (1.0 - smooth) * base_freq / 32.0 + smooth * base_freq
    freq_table = np.where(
        wavelength > 8192.0, base_freq / 32.0, np.where(wavelength < 2048.0, base_freq, middle)
    )
    return freq_table.astype(np.float32)


def doc_layout(lengths, places):
    doc_count = lengths.shape[0]
    doc_ends = jnp.cumsum(lengths)
    starts = doc_ends - lengths
    segment = jnp.sum((places[:, None] >= doc_ends[None, :]).astype(jnp.int32), axis=1)
    chosen = segment[:, None] == jnp.arange(doc_count, dtype=jnp.int32)[None, :]
    offset = jnp.sum(jnp.where(chosen, starts[None, :], 0), axis=1) + jnp.where(
        segment == doc_count, doc_ends[doc_count - 1], 0
    )
    return (segment, offset)


def mm(a, b):
    return jnp.dot(a, b, preferred_element_type=F32)


def mm_nt(a, b):
    return lax.dot_general(a, b, (((1,), (1,)), ((), ())), preferred_element_type=F32)


def mm_tn(a, b):
    return lax.dot_general(a, b, (((0,), (0,)), ((), ())), preferred_element_type=F32)


class Place:
    def __init__(self):
        self.yl = lax.axis_index("yl")
        self.c = lax.axis_index("c")
        self.yh = lax.axis_index("yh")
        self.y = self.yh * 2 + self.yl
        self.t = self.rank(0, self.c)

    def rank(self, k, c):
        y = lax.rem(self.y + (k + 4), 4)
        return lax.rem(y, 2) * 4 + c * 2 + y // 2

    def ring(self, k):
        y = lax.rem(self.y + (k + 4), 4)
        return {"yh": y // 2, "yl": lax.rem(y, 2)}

    def sibling(self):
        return {"c": 1 - self.c}

    def greet(self):
        barrier = pltpu.get_barrier_semaphore()
        for who in (self.ring(1), self.ring(-1), self.sibling()):
            pl.semaphore_signal(barrier, inc=1, device_id=who, device_id_type=MESH)
        pl.semaphore_wait(barrier, 3)


class Sent:
    def __init__(self, copy):
        self.copy, self.arrived = copy, False

    def wait_recv(self):
        if not self.arrived:
            self.copy.wait_recv()
        self.arrived = True

    def wait_send(self):
        self.copy.wait_send()


class Copies:
    def __init__(self, send_sem, recv_sem):
        self.send_sem, self.recv_sem, self.n, self.all = send_sem, recv_sem, 0, []

    def __call__(self, src, dst, who):
        i = self.n
        self.n += 1
        copy = pltpu.make_async_remote_copy(
            src_ref=src,
            dst_ref=dst,
            send_sem=self.send_sem.at[i],
            recv_sem=self.recv_sem.at[i],
            device_id=who,
            device_id_type=MESH,
        )
        copy.start()
        sent = Sent(copy)
        self.all.append(sent)
        return sent

    def finish(self):
        for sent in self.all:
            sent.wait_recv()
        for sent in self.all:
            sent.wait_send()


def gather_begin(me, send, own, out):
    return [
        send(own, out.at[me.t], me.ring(1)),
        send(own, out.at[me.t], me.ring(-1)),
        send(own, out.at[me.t], me.sibling()),
    ]


def gather_rest(me, send, out, begun):
    down, up, mine = begun
    half = out.shape[1] // 2
    below, above, far = me.rank(-1, me.c), me.rank(1, me.c), me.rank(2, me.c)
    down.wait_recv()
    part = out.at[below, pl.ds(0, half)]
    on_down = send(part, part, me.ring(1))
    sib_below = send(out.at[below], out.at[below], me.sibling())
    up.wait_recv()
    part = out.at[above, pl.ds(half, half)]
    on_up = send(part, part, me.ring(-1))
    sib_above = send(out.at[above], out.at[above], me.sibling())
    on_down.wait_recv()
    on_up.wait_recv()
    sib_far = send(out.at[far], out.at[far], me.sibling())
    for copy in (mine, sib_below, sib_above, sib_far):
        copy.wait_recv()


def gather_kernel(own, out, send_sem, recv_sem, local_sem):
    me = Place()
    me.greet()
    send = Copies(send_sem, recv_sem)
    begun = gather_begin(me, send, own, out)
    local = pltpu.make_async_copy(own, out.at[me.t], local_sem)
    local.start()
    gather_rest(me, send, out, begun)
    local.wait()
    send.finish()


ANY = pl.BlockSpec(memory_space=pl.ANY)


def gather_group(own, name, number):
    rows, width = own.shape
    return pl.pallas_call(
        gather_kernel,
        out_shape=jax.ShapeDtypeStruct((NT, rows, width), own.dtype),
        in_specs=[ANY],
        out_specs=ANY,
        scratch_shapes=[
            pltpu.SemaphoreType.DMA((8,)),
            pltpu.SemaphoreType.DMA((8,)),
            pltpu.SemaphoreType.DMA,
        ],
        compiler_params=pltpu.CompilerParams(collective_id=number, has_side_effects=True),
        name=name,
    )(own)


def scatter_kernel(part, out, sib, far_a, far_b, near_a, near_b, mid, send_sem, recv_sem):
    me = Place()
    me.greet()
    send = Copies(send_sem, recv_sem)
    half = TOK // 2
    lo, hi = pl.ds(0, half), pl.ds(half, half)
    other = 1 - me.c
    from_sib = {}
    for k in (2, 1, 3, 0):
        from_sib[k] = send(part.at[me.rank(k, other)], sib.at[k], me.sibling())

    def both(k, rows):
        return part[me.rank(k, me.c), rows].astype(F32) + sib[k, rows].astype(F32)

    from_sib[2].wait_recv()
    mid[2] = both(2, slice(None)).astype(BF)
    far_up = send(mid.at[2, lo], far_a, me.ring(1))
    far_down = send(mid.at[2, hi], far_b, me.ring(-1))
    from_sib[1].wait_recv()
    mid[1, half:] = both(1, slice(half, TOK)).astype(BF)
    up_hi = send(mid.at[1, hi], near_a.at[hi], me.ring(1))
    from_sib[3].wait_recv()
    mid[3, :half] = both(3, slice(0, half)).astype(BF)
    down_lo = send(mid.at[3, lo], near_b.at[lo], me.ring(-1))
    far_up.wait_recv()
    mid[1, :half] = (both(1, slice(0, half)) + far_a[...].astype(F32)).astype(BF)
    up_lo = send(mid.at[1, lo], near_a.at[lo], me.ring(1))
    far_down.wait_recv()
    mid[3, half:] = (both(3, slice(half, TOK)) + far_b[...].astype(F32)).astype(BF)
    down_hi = send(mid.at[3, hi], near_b.at[hi], me.ring(-1))
    from_sib[0].wait_recv()
    total = both(0, slice(None))
    for copy in (up_hi, up_lo, down_lo, down_hi):
        copy.wait_recv()
    out[...] = total + near_a[...].astype(F32) + near_b[...].astype(F32)
    send.finish()


VM = pl.BlockSpec(memory_space=pltpu.VMEM)


def scatter_group(part, name, number):
    _, rows, width = part.shape
    half = rows // 2
    return pl.pallas_call(
        scatter_kernel,
        out_shape=jax.ShapeDtypeStruct((rows, width), F32),
        in_specs=[VM],
        out_specs=VM,
        scratch_shapes=[
            pltpu.VMEM((4, rows, width), BF),
            pltpu.VMEM((half, width), BF),
            pltpu.VMEM((half, width), BF),
            pltpu.VMEM((rows, width), BF),
            pltpu.VMEM((rows, width), BF),
            pltpu.VMEM((4, rows, width), BF),
            pltpu.SemaphoreType.DMA((10,)),
            pltpu.SemaphoreType.DMA((10,)),
        ],
        compiler_params=pltpu.CompilerParams(
            collective_id=number, has_side_effects=True, vmem_limit_bytes=40 * 2**20
        ),
        name=name,
    )(part)


def first_kernel(
    tok, wqkv, wgu, wo, tok_all, qkv, gu, oh, tmp_qkv, tmp_gu, send_sem, recv_sem, local_sem
):
    me = Place()
    me.greet()
    send = Copies(send_sem, recv_sem)
    c, other = me.c, 1 - me.c
    step = 1 - 2 * c
    slot, slot_other = me.yl * 2 + c, me.yl * 2 + other
    toward, away = me.ring(step), me.ring(-step)
    t_toward, t_relay, t_sib = me.rank(step, c), me.rank(step, other), me.rank(0, other)
    pairs = ((wqkv, qkv, tmp_qkv), (wgu, gu, tmp_gu))
    kept = []

    def keep(src, dst):
        copy = pltpu.make_async_copy(src, dst, local_sem.at[len(kept)])
        copy.start()
        kept.append(copy)

    relays = [send(src.at[t_relay], tmp, me.sibling()) for src, _, tmp in pairs]
    for src, dst, _ in pairs:
        send(src.at[t_sib], dst.at[slot], me.sibling())
        send(src.at[t_toward], dst.at[slot], toward)
    send(wo, oh.at[me.yl], toward)
    begun = gather_begin(me, send, tok, tok_all)
    keep(tok, tok_all.at[me.t])
    keep(wo, oh.at[me.yl])
    for src, dst, _ in pairs:
        keep(src.at[me.t], dst.at[slot])
    for relay, (_, dst, tmp) in zip(relays, pairs):
        relay.wait_recv()
        send(tmp, dst.at[slot_other], away)
    gather_rest(me, send, tok_all, begun)
    for copy in kept:
        copy.wait()
    send.finish()


def first_gather(tok, wqkv, wgu, wo):
    def like(shape):
        return jax.ShapeDtypeStruct(shape, BF)

    rows = wo.shape[0]
    return pl.pallas_call(
        first_kernel,
        out_shape=(
            like((NT,) + tok.shape),
            like((4,) + wqkv.shape[1:]),
            like((4,) + wgu.shape[1:]),
            like((2,) + wo.shape),
            like(wqkv.shape[1:]),
            like(wgu.shape[1:]),
        ),
        in_specs=[ANY] * 4,
        out_specs=(ANY,) * 6,
        scratch_shapes=[
            pltpu.SemaphoreType.DMA((20,)),
            pltpu.SemaphoreType.DMA((20,)),
            pltpu.SemaphoreType.DMA((4,)),
        ],
        compiler_params=pltpu.CompilerParams(collective_id=0, has_side_effects=True),
        name="first_gather",
    )(tok, wqkv, wgu, wo)[:4]


QROWS = 2 * TOK
CHUNK = NX * TOK


def keys_of(ref, kt):
    return jnp.concatenate([ref[x, kt] for x in range(NX)], axis=0)


def attend_kernel(x_ref, q_ref, k_ref, v_ref, start_ref, o_ref, lse_ref):
    x = x_ref[0]

    def tile(t, kt, q, start, carry, diagonal):
        top, total, acc = carry
        s = mm_nt(q, keys_of(k_ref, kt))
        place = kt * CHUNK + lax.broadcasted_iota(jnp.int32, (QROWS, CHUNK), 1)
        keep = place >= start
        if diagonal:
            row = lax.broadcasted_iota(jnp.int32, (QROWS, CHUNK), 0)
            query = t * CHUNK + x * TOK + lax.rem(row, TOK)
            keep = keep & (place <= query)
        s = jnp.where(keep, s, -jnp.inf)
        new_top = jnp.maximum(top, jnp.max(s, axis=1, keepdims=True))
        p = jnp.exp2(s - new_top)
        factor = jnp.exp2(top - new_top)
        total = total * factor + jnp.sum(p, axis=1, keepdims=True)
        acc = acc * factor + mm(p.astype(BF), keys_of(v_ref, kt))
        return new_top, total, acc

    def one(t, _):
        q = jnp.concatenate([q_ref[0, t], q_ref[1, t]], axis=0)
        start = jnp.concatenate([start_ref[t]] * 2, axis=0)
        carry = (
            jnp.full((QROWS, 1), -1e30, F32),
            jnp.zeros((QROWS, 1), F32),
            jnp.zeros((QROWS, HD), F32),
        )
        carry = lax.fori_loop(0, t, lambda kt, c: tile(t, kt, q, start, c, False), carry)
        top, total, acc = tile(t, t, q, start, carry, True)
        o = acc / total
        lse = top + jnp.log2(total)
        o_ref[0, t], o_ref[1, t] = o[:TOK], o[TOK:]
        lse_ref[0, t], lse_ref[1, t] = lse[:TOK], lse[TOK:]
        return 0

    lax.fori_loop(0, NT, one, 0)


SM = pl.BlockSpec(memory_space=pltpu.SMEM)


def attend(x_index, q, k, v, start):
    return pl.pallas_call(
        attend_kernel,
        out_shape=(
            jax.ShapeDtypeStruct((2, NT, TOK, HD), F32),
            jax.ShapeDtypeStruct((2, NT, TOK, 1), F32),
        ),
        in_specs=[SM, VM, VM, VM, VM],
        out_specs=(VM, VM),
        compiler_params=pltpu.CompilerParams(vmem_limit_bytes=40 * 2**20),
        name="attend",
    )(x_index, q, k, v, start)


def attend_back_kernel(
    x_ref, q_ref, k_ref, v_ref, go_ref, start_ref, lse_ref, delta_ref, gq_ref, gk_ref, gv_ref
):
    x = x_ref[0]
    gk_ref[...] = jnp.zeros_like(gk_ref)
    gv_ref[...] = jnp.zeros_like(gv_ref)

    def tile(t, kt, given, gq, diagonal):
        q, go, start, lse, delta = given
        k, v = keys_of(k_ref, kt), keys_of(v_ref, kt)
        s = mm_nt(k, q)
        place = kt * CHUNK + lax.broadcasted_iota(jnp.int32, (CHUNK, QROWS), 0)
        keep = place >= start
        if diagonal:
            column = lax.broadcasted_iota(jnp.int32, (CHUNK, QROWS), 1)
            query = t * CHUNK + x * TOK + lax.rem(column, TOK)
            keep = keep & (place <= query)
        p = jnp.where(keep, jnp.exp2(s - lse), 0.0)
        gp = mm_nt(v, go)
        gs = (p * (gp - delta)).astype(BF)
        gv = mm(p.astype(BF), go)
        gk = mm(gs, q)
        for n in range(NX):
            rows = slice(n * TOK, (n + 1) * TOK)
            gv_ref[n, kt] += gv[rows]
            gk_ref[n, kt] += gk[rows]
        return gq + mm_tn(gs, k)

    def one(t, _):
        q = jnp.concatenate([q_ref[0, t], q_ref[1, t]], axis=0)
        go = jnp.concatenate([go_ref[0, t], go_ref[1, t]], axis=0)
        start = jnp.concatenate([start_ref[t]] * 2, axis=1)
        lse = jnp.concatenate([lse_ref[0, t], lse_ref[1, t]], axis=1)
        delta = jnp.concatenate([delta_ref[0, t], delta_ref[1, t]], axis=1)
        given = (q, go, start, lse, delta)
        gq = jnp.zeros((QROWS, HD), F32)
        gq = lax.fori_loop(0, t, lambda kt, g: tile(t, kt, given, g, False), gq)
        gq = tile(t, t, given, gq, True) * SCALE
        gq_ref[0, t], gq_ref[1, t] = gq[:TOK], gq[TOK:]
        return 0

    lax.fori_loop(0, NT, one, 0)


def attend_back(x_index, q, k, v, go, start, lse, delta):
    return pl.pallas_call(
        attend_back_kernel,
        out_shape=(
            jax.ShapeDtypeStruct((2, NT, TOK, HD), F32),
            jax.ShapeDtypeStruct((NX, NT, TOK, HD), F32),
            jax.ShapeDtypeStruct((NX, NT, TOK, HD), F32),
        ),
        in_specs=[SM] + [VM] * 7,
        out_specs=(VM, VM, VM),
        compiler_params=pltpu.CompilerParams(vmem_limit_bytes=48 * 2**20),
        name="attend_back",
    )(x_index, q, k, v, go, start, lse, delta)


def turn(v, cosine, sine):
    half = HD // 2
    v1, v2 = v[..., :half], v[..., half:]
    return jnp.concatenate([v1 * cosine - v2 * sine, v2 * cosine + v1 * sine], axis=-1)


def body(
    tokens,
    doc_lengths,
    w_query,
    w_key,
    w_value,
    w_output,
    w_gate,
    w_up,
    w_down,
    gain_attn,
    gain_mlp,
    cotangent,
):
    width = tokens.shape[2]
    rows = w_query.shape[0]
    hidden_width = w_gate.shape[1]
    part = hidden_width // NT
    everyone = ("z", "yl", "c")
    x_index = lax.axis_index("x")
    yl, c, yh = lax.axis_index("yl"), lax.axis_index("c"), lax.axis_index("yh")
    ylc = yl * 2 + c
    x_scalar = x_index.reshape(1)

    wqkv = jnp.concatenate(
        [
            w_query.reshape(rows, NT, 2 * HD),
            w_key.reshape(rows, NT, HD),
            w_value.reshape(rows, NT, HD),
        ],
        axis=2,
    ).transpose(1, 0, 2)

    def hidden_slices(w):
        w = w.reshape(rows, 4, 4, 2, TOK).transpose(2, 3, 0, 1, 4)
        return w.reshape(NT, rows, part)

    wgu = jnp.concatenate([hidden_slices(w_gate), hidden_slices(w_up)], axis=2)
    down_own = lax.dynamic_slice_in_dim(w_down, yh * TOK, TOK, 0)
    gains = lax.all_gather(jnp.stack([gain_attn, gain_mlp], axis=1), everyone, axis=0, tiled=True)
    gains = gains.astype(F32)
    g1, g2 = gains[:, 0][None, :], gains[:, 1][None, :]
    tok_all, qkv_part, gu_part, o_half = first_gather(tokens[0], wqkv, wgu, w_output)
    qkv_w = lax.all_gather(qkv_part, "z", axis=0, tiled=True).reshape(width, 4 * HD)
    gu_w = lax.all_gather(gu_part, "z", axis=0, tiled=True).reshape(width, 2 * part)
    down_w = lax.all_gather(down_own, "z", axis=0, tiled=True)
    o_w = lax.all_gather(o_half, ("z", "c"), axis=0)
    o_w = o_w.reshape((4, 2) + o_half.shape).transpose(0, 2, 1, 3, 4).reshape(width, width)
    cot_all = lax.all_gather(cotangent[0], GROUP, axis=0, tiled=True)

    lengths = doc_lengths[0]
    places = (
        jnp.arange(NT, dtype=jnp.int32)[:, None] * CHUNK
        + x_index * TOK
        + jnp.arange(TOK, dtype=jnp.int32)[None, :]
    ).reshape(-1)
    segment, start = doc_layout(lengths, places)
    valid = (segment < lengths.shape[0]).astype(F32)[:, None]
    angles = (places - start).astype(F32)[:, None] * jnp.asarray(frequency_table(HD))[None, :]
    cosine, sine = jnp.cos(angles), jnp.sin(angles)
    start = start.reshape(NT, TOK)

    x_all = tok_all.reshape(NT * TOK, width).astype(F32)
    h1 = x_all * lax.rsqrt(jnp.mean(x_all * x_all, axis=1, keepdims=True) + NORM_EPS)
    h1 = (h1 * g1).astype(BF)
    qkv = mm(h1, qkv_w)
    q = turn(qkv[:, : 2 * HD].reshape(-1, 2, HD), cosine[:, None], sine[:, None])
    q = (q * (SCALE * LOG2E)).astype(BF).transpose(1, 0, 2).reshape(2, NT, TOK, HD)
    k = turn(qkv[:, 2 * HD : 3 * HD], cosine, sine).astype(BF).reshape(NT, TOK, HD)
    v = qkv[:, 3 * HD :].astype(BF).reshape(NT, TOK, HD)
    kv = lax.all_gather(jnp.stack([k, v]), "x", axis=0)
    k_all, v_all = kv[:, 0], kv[:, 1]
    attended, lse = attend(x_scalar, q, k_all, v_all, start[..., None])
    flat = attended.transpose(1, 2, 0, 3).reshape(NT * TOK, 2 * HD)
    ob = (flat * valid).astype(BF)
    ob_all = gather_group(ob, "gather_ob", 1)
    ob_all = ob_all.transpose(1, 0, 2).reshape(NT * TOK, width)

    x2 = x_all + mm(ob_all, o_w)
    r2 = lax.rsqrt(jnp.mean(x2 * x2, axis=1, keepdims=True) + NORM_EPS)
    h2 = (x2 * r2 * g2).astype(BF)
    gu = mm(h2, gu_w)
    gate, up = gu[:, :part], gu[:, part:]
    sigmoid = jax.nn.sigmoid(gate)
    silu = gate * sigmoid
    hidden = (silu * up).astype(BF)
    y_part = mm(hidden, down_w).astype(BF).reshape(NT, TOK, width)
    gh = mm_nt(cot_all, down_w)
    ggate = (gh * up * sigmoid * (1.0 + gate * (1.0 - sigmoid))).astype(BF)
    gup = (gh * silu).astype(BF)
    ggu = jnp.concatenate([ggate, gup], axis=1)
    gh2_part = mm_nt(ggu, gu_w).astype(BF).reshape(NT, TOK, width)
    gh2 = scatter_group(gh2_part, "scatter_gh2", 2)
    t = ylc * 2 + yh
    own = lax.dynamic_slice_in_dim(x2, t * TOK, TOK, 0)
    own_r2 = lax.dynamic_slice_in_dim(r2, t * TOK, TOK, 0)
    n2 = own * own_r2
    gm = gh2 * g2
    gain_mlp_grad = jnp.sum(gh2 * n2, axis=0)
    gx2 = own_r2 * (gm - n2 * jnp.mean(gm * n2, axis=1, keepdims=True)) + cotangent[0].astype(F32)
    ga = gather_group(gx2.astype(BF), "gather_ga", 3).reshape(NT * TOK, width)
    layer_out = own + scatter_group(y_part, "scatter_y", 4)

    o_rows = lax.dynamic_slice_in_dim(o_w, t * 2 * HD, 2 * HD, 0)
    go = (mm_nt(ga, o_rows) * valid).astype(BF)
    delta = jnp.sum((go.astype(F32) * flat).reshape(NT, TOK, 2, HD), axis=3)
    delta = delta.transpose(2, 0, 1)[:, :, None, :]
    go4 = go.reshape(NT, TOK, 2, HD).transpose(2, 0, 1, 3)
    gq, gk, gv = attend_back(
        x_scalar, q, k_all, v_all, go4, start[:, None, :], lse.transpose(0, 1, 3, 2), delta
    )
    gkv = jnp.stack([gk * LN2, gv], axis=1).astype(BF)
    gkv = lax.psum_scatter(gkv, "x", scatter_dimension=0).astype(F32)
    gq = turn(gq.transpose(1, 2, 0, 3).reshape(-1, 2, HD), cosine[:, None], -sine[:, None])
    gk = turn(gkv[0].reshape(-1, HD), cosine, -sine)
    gqkv = jnp.concatenate([gq.reshape(-1, 2 * HD), gk, gkv[1].reshape(-1, HD)], axis=1).astype(BF)
    gh1_part = mm_nt(gqkv, qkv_w).astype(BF).reshape(NT, TOK, width)
    gh1 = scatter_group(gh1_part, "scatter_gh1", 5)
    x_own = tokens[0].astype(F32)
    r1 = lax.rsqrt(jnp.mean(x_own * x_own, axis=1, keepdims=True) + NORM_EPS)
    n1 = x_own * r1
    gn = gh1 * g1
    gain_attn_grad = jnp.sum(gh1 * n1, axis=0)
    tokens_grad = gx2 + r1 * (gn - n1 * jnp.mean(gn * n1, axis=1, keepdims=True))

    ob_heads = ob_all.reshape(NT * TOK, 4, 4, HD)
    ob_mine = lax.dynamic_index_in_dim(ob_heads, ylc, 2, keepdims=False).reshape(NT * TOK, 4 * HD)
    ga_mine = lax.dynamic_slice_in_dim(ga, yh * (width // 2), width // 2, 1)
    grad_o = mm_tn(ob_mine, ga_mine).astype(BF)
    grad_gu = mm_tn(h2, ggu).astype(BF)
    grad_down = mm_tn(hidden, cot_all).astype(BF)
    grad_qkv = mm_tn(h1, gqkv).astype(BF)
    gain_grads = jnp.stack([gain_attn_grad, gain_mlp_grad], axis=1).astype(BF)
    gain_grads = jnp.pad(gain_grads, ((0, 0), (0, TOK - 2)))

    def over_z(a):
        return lax.psum_scatter(a, "z", scatter_dimension=0, tiled=True)

    sum_gu, sum_down, sum_o = over_z(grad_gu), over_z(grad_down), over_z(grad_o)
    sum_qkv = over_z(jnp.concatenate([grad_qkv, gain_grads], axis=1))
    columns = jnp.concatenate([sum_gu, sum_qkv], axis=1)
    columns = lax.all_to_all(columns, ("yl", "c"), split_axis=0, concat_axis=0, tiled=True)
    columns, sum_down, sum_o = lax.psum((columns, sum_down, sum_o), "x")
    columns = lax.all_gather(columns, "yh", axis=0)
    sum_down = lax.all_gather(sum_down, "yh", axis=0, tiled=True).astype(F32)
    sum_o = lax.all_gather(sum_o, "yh", axis=1, tiled=True).astype(F32)
    columns = columns.reshape(2, 4, rows, 2 * part + 4 * TOK).astype(F32)
    columns = columns.transpose(2, 1, 0, 3)

    def hidden_columns(a):
        return a.reshape(rows, 4, 2, 4, TOK).transpose(0, 3, 1, 2, 4).reshape(rows, hidden_width)

    grad_gate = hidden_columns(columns[..., :part])
    grad_up = hidden_columns(columns[..., part : 2 * part])
    base = 2 * part
    grad_query = columns[..., base : base + 2 * HD].reshape(rows, width)
    grad_key = columns[..., base + 2 * HD : base + 3 * HD].reshape(rows, KV * HD)
    grad_value = columns[..., base + 3 * HD : base + 4 * HD].reshape(rows, KV * HD)
    grad_gains = jnp.sum(columns[..., base + 4 * HD : base + 4 * HD + 2], axis=(1, 2))
    return (
        layer_out.astype(BF)[None],
        tokens_grad.astype(BF)[None],
        grad_query,
        grad_key,
        grad_value,
        sum_o,
        grad_gate,
        grad_up,
        sum_down,
        grad_gains[:, 0],
        grad_gains[:, 1],
    )


def solution(mesh):
    fine = Mesh(mesh.devices.reshape(4, 2, 2, 2, 4), AXES)
    by_token = P("z", ("yl", "c", "yh", "x"), None)
    by_row = P(("z", "yl", "c"), None)
    by_feature = P(("z", "yl", "c"))
    return jax.shard_map(
        body,
        mesh=fine,
        in_specs=(by_token, P("z", None))
        + (by_row,) * 7
        + (by_feature, by_feature, by_token),
        out_specs=(by_token, by_token) + (by_row,) * 7 + (by_feature, by_feature),
        check_vma=False,
    )
```

```python
from functools import partial

import jax
import jax.numpy as jnp
import numpy as np
from jax import lax
from jax.experimental import pallas as pl
from jax.experimental.pallas import tpu as pltpu
from jax.sharding import Mesh
from jax.sharding import PartitionSpec as P

HEADS = 16
KV = 8
HD = 96
NORM_EPS = 1e-05
LOG2E = 1.4426950408889634
LN2 = 0.6931471805599453
SCALE = HD ** (-0.5)
BF = jnp.bfloat16
F32 = jnp.float32
AXES = ("z", "yl", "c", "yh", "x")
GROUP = ("yl", "c", "yh")
MESH = pl.DeviceIdType.MESH
TOK = 128
NT = 8
NX = 4


def frequency_table(head_width):
    halfway = head_width // 2
    base_freq = 500000.0 ** (-np.arange(halfway) * 2.0 / head_width)
    wavelength = 2.0 * np.pi / base_freq
    smooth = (8192.0 / wavelength - 1.0) / 3.0
    middle = (1.0 - smooth) * base_freq / 32.0 + smooth * base_freq
    freq_table = np.where(
        wavelength > 8192.0, base_freq / 32.0, np.where(wavelength < 2048.0, base_freq, middle)
    )
    return freq_table.astype(np.float32)


def doc_layout(lengths, places):
    doc_count = lengths.shape[0]
    doc_ends = jnp.cumsum(lengths)
    starts = doc_ends - lengths
    segment = jnp.sum((places[:, None] >= doc_ends[None, :]).astype(jnp.int32), axis=1)
    chosen = segment[:, None] == jnp.arange(doc_count, dtype=jnp.int32)[None, :]
    offset = jnp.sum(jnp.where(chosen, starts[None, :], 0), axis=1) + jnp.where(
        segment == doc_count, doc_ends[doc_count - 1], 0
    )
    return (segment, offset)


def mm(a, b):
    return jnp.dot(a, b, preferred_element_type=F32)


def mm_nt(a, b):
    return lax.dot_general(a, b, (((1,), (1,)), ((), ())), preferred_element_type=F32)


def mm_tn(a, b):
    return lax.dot_general(a, b, (((0,), (0,)), ((), ())), preferred_element_type=F32)


class Place:
    def __init__(self):
        self.z, self.x = lax.axis_index("z"), lax.axis_index("x")
        self.yl, self.c, self.yh = (lax.axis_index(name) for name in GROUP)
        self.y = self.yh * 2 + self.yl
        self.t = self.rank(0, self.c)

    def rank(self, k, c):
        y = lax.rem(self.y + (k + 4), 4)
        return lax.rem(y, 2) * 4 + c * 2 + y // 2

    def along_y(self, k):
        y = lax.rem(self.y + (k + 4), 4)
        return {"yh": y // 2, "yl": lax.rem(y, 2)}

    def x_at(self, k):
        return lax.rem(self.x + (k + 4), 4)

    def z_at(self, k):
        return lax.rem(self.z + (k + 4), 4)

    def along_x(self, k):
        return {"x": self.x_at(k)}

    def along_z(self, k):
        return {"z": self.z_at(k)}

    def sibling(self):
        return {"c": 1 - self.c}

    def greet(self, others=()):
        barrier = pltpu.get_barrier_semaphore()
        everyone = (self.along_y(1), self.along_y(-1), self.sibling()) + tuple(others)
        for who in everyone:
            pl.semaphore_signal(barrier, inc=1, device_id=who, device_id_type=MESH)
        pl.semaphore_wait(barrier, len(everyone))


class Sent:
    def __init__(self, copy):
        self.copy, self.arrived = copy, False

    def wait_recv(self):
        if not self.arrived:
            self.copy.wait_recv()
        self.arrived = True

    def wait_send(self):
        self.copy.wait_send()


class Copies:
    def __init__(self, send_sem, recv_sem, local_sem=None):
        self.send_sem, self.recv_sem, self.local_sem = send_sem, recv_sem, local_sem
        self.all, self.locals = [], []

    def __call__(self, src, dst, who):
        i = len(self.all)
        copy = pltpu.make_async_remote_copy(
            src_ref=src,
            dst_ref=dst,
            send_sem=self.send_sem.at[i],
            recv_sem=self.recv_sem.at[i],
            device_id=who,
            device_id_type=MESH,
        )
        copy.start()
        sent = Sent(copy)
        self.all.append(sent)
        return sent

    def local(self, src, dst):
        copy = pltpu.make_async_copy(src, dst, self.local_sem.at[len(self.locals)])
        copy.start()
        self.locals.append(copy)
        return copy

    def finish(self):
        for sent in self.all:
            sent.wait_recv()
        for sent in self.all:
            sent.wait_send()


class Gather:
    def __init__(self, send, along, slot, cut, src=None):
        self.send, self.along, self.slot, self.cut = send, along, slot, cut
        src = slot(0) if src is None else src
        self.up = send(src, slot(0), along(1))
        self.down = send(src, slot(0), along(-1))

    def forward(self):
        self.up.wait_recv()
        part = self.cut(self.slot(-1), 0)
        self.far_up = self.send(part, part, self.along(1))
        self.down.wait_recv()
        part = self.cut(self.slot(1), 1)
        self.far_down = self.send(part, part, self.along(-1))

    def end(self):
        self.far_up.wait_recv()
        self.far_down.wait_recv()


def halves(ref, i):
    half = ref.shape[0] // 2
    return ref.at[pl.ds(i * half, half)]


ANY = pl.BlockSpec(memory_space=pl.ANY)
VM = pl.BlockSpec(memory_space=pltpu.VMEM)
SM = pl.BlockSpec(memory_space=pltpu.SMEM)
GROUP_ROWS = NT * TOK
QROWS = 2 * TOK
CHUNK = NX * TOK
PACKED = GROUP_ROWS + GROUP_ROWS // 2


def starts_of(lengths_ref, place):
    end, start = 0, jnp.zeros_like(place)
    for i in range(lengths_ref.shape[1]):
        end = end + lengths_ref[0, i]
        start = jnp.maximum(start, jnp.where(place >= end, end, 0))
    return start, end


def places_of(me, tile, shape, axis):
    row = lax.broadcasted_iota(jnp.int32, shape, axis)
    return (tile + row // TOK) * CHUNK + me.x * TOK + lax.rem(row, TOK)


def turn(v, cosine, sine):
    half = HD // 2
    return v * cosine + jnp.concatenate([-v[:, half:], v[:, :half]], axis=1) * sine


def unpack(packed, n):
    low, high = packed[n:, : TOK // 2], packed[n:, TOK // 2 :]
    tail = jnp.concatenate([low, high], axis=0)
    return jnp.concatenate([packed[:n], tail, jnp.zeros_like(tail)], axis=1)


def front_kernel(
    lengths, freq, tok, cot, wq, wk, wv, wg, wu, wo, wd, gain1, gain2,
    tok_all, cot_all, h1_out, gu_w, o_w, down_w, kv_out, q_out, o_out, lse_out, ob_out, gains_out, qkv_w,
    tokv, h1, slices_q, slices_u, tmp_q, tmp_u, gq, kv, keyv, starts, top, total, acc,
    send_sem, recv_sem, local_sem,
):
    me = Place()
    me.greet((me.along_x(1), me.along_x(-1), me.along_z(1), me.along_z(-1)))
    send = Copies(send_sem, recv_sem, local_sem)
    c, other = me.c, 1 - me.c
    step = 1 - 2 * c
    slot, slot_other = me.yl * 2 + c, me.yl * 2 + other
    toward, away = me.along_y(step), me.along_y(-step)
    t_toward, t_relay, t_sib = me.rank(step, c), me.rank(step, other), me.rank(0, other)
    rows, width = wq.shape

    slices_q[:, rows:, :] = jnp.zeros_like(slices_q[:, rows:, :])
    for t in range(NT):
        slices_q[t, :rows] = jnp.concatenate(
            [
                wq[:, 2 * HD * t : 2 * HD * (t + 1)],
                wk[:, HD * t : HD * (t + 1)],
                wv[:, HD * t : HD * (t + 1)],
            ],
            axis=1,
        )
        slices_q[t, rows : rows + 1, :rows] = gain1[...]
        slices_q[t, rows + 1 : rows + 2, :rows] = gain2[...]
    relay_q = send(slices_q.at[t_relay], tmp_q, me.sibling())
    arrived_q = [
        send(slices_q.at[t_sib], gq.at[me.z, slot], me.sibling()),
        send(slices_q.at[t_toward], gq.at[me.z, slot], toward),
    ]
    own_q = send.local(slices_q.at[me.t], gq.at[me.z, slot])
    own_tok = send.local(tok, tokv.at[me.t])
    tokens = Gather(send, me.along_y, lambda k: tokv.at[me.rank(k, c)], halves, tok)
    tok_sib = [send(tok, tokv.at[me.t], me.sibling())]
    quarter = 32
    rows_of = lambda i: pl.ds(pl.multiple_of(i * quarter, quarter), quarter)
    down_src = wd.at[pl.ds(pl.multiple_of(me.yh * TOK + me.x * quarter, quarter), quarter)]
    own_down = send.local(down_src, down_w.at[me.z, rows_of(me.x)])
    down_z = Gather(
        send, me.along_z, lambda k: down_w.at[me.z_at(k), rows_of(me.x)], halves, down_src
    )
    relay_q.wait_recv()
    arrived_q.append(send(tmp_q, gq.at[me.z, slot_other], away))

    part = wg.shape[1] // NT
    for t in range(NT):
        for n in range(4):
            at = n * 2 * CHUNK + t * TOK
            slices_u[t, :, n * TOK : (n + 1) * TOK] = wg[:, at : at + TOK]
            slices_u[t, :, part + n * TOK : part + (n + 1) * TOK] = wu[:, at : at + TOK]

    for t in range(NT):
        place = places_of(me, t, (TOK, TOK), 0)
        starts[t], _ = starts_of(lengths, place)

    own_q.wait()
    for copy in arrived_q:
        copy.wait_recv()
    qkv_z = Gather(send, me.along_z, lambda k: gq.at[me.z_at(k)], halves)
    tokens.forward()
    tok_sib += [
        send(tokv.at[me.rank(k, c)], tokv.at[me.rank(k, c)], me.sibling()) for k in (-1, 1)
    ]
    relay_u = send(slices_u.at[t_relay], tmp_u, me.sibling())
    arrived_u = [
        send(slices_u.at[t_sib], gu_w.at[me.z, slot], me.sibling()),
        send(slices_u.at[t_toward], gu_w.at[me.z, slot], toward),
    ]
    own_u = send.local(slices_u.at[me.t], gu_w.at[me.z, slot])
    third = pl.ds(pl.multiple_of(me.x * CHUNK * 3 // 4, TOK), CHUNK * 3 // 4)
    arrived_o = send(wo, o_w.at[me.z, me.yl, c], toward)
    own_o = send.local(wo, o_w.at[me.z, me.yl, c])
    relay_u.wait_recv()
    arrived_u.append(send(tmp_u, gu_w.at[me.z, slot_other], away))
    own_down.wait()
    down_z.forward()
    qkv_z.forward()
    tokens.end()
    far = tokv.at[me.rank(2, c)]
    tok_sib.append(send(far, far, me.sibling()))
    cots = Gather(send, me.along_y, lambda k: cot_all.at[me.rank(k, c)], halves, cot)
    own_cot = send.local(cot, cot_all.at[me.t])
    cot_sib = [send(cot, cot_all.at[me.t], me.sibling())]
    down_z.end()
    down_x = Gather(
        send, me.along_x, lambda k: down_w.at[:, rows_of(me.x_at(k))], halves
    )
    own_u.wait()
    for copy in arrived_u:
        copy.wait_recv()
    qkv_z.end()
    gu_z = Gather(send, me.along_z, lambda k: gu_w.at[me.z_at(k)], halves)
    own_o.wait()
    arrived_o.wait_recv()
    o_z = Gather(send, me.along_z, lambda k: o_w.at[me.z_at(k), :, c, :, third], halves)
    own_tok.wait()
    for copy in tok_sib:
        copy.wait_recv()
    tok_out = send.local(tokv, tok_all)

    gains = [
        jnp.concatenate(
            [gq[z, n, rows + g : rows + g + 1, :rows] for z in range(4) for n in range(4)], axis=1
        ).astype(F32)
        for g in range(2)
    ]
    gains_out[...] = jnp.concatenate(gains, axis=0)
    for z in range(4):
        for n in range(4):
            at = (z * 4 + n) * rows
            qkv_w[at : at + rows] = gq[z, n, :rows]
    tails = []
    for i in range(4):
        place = places_of(me, 2 * i, (QROWS, HD), 0)
        start, _ = starts_of(lengths, place)
        angle = (place - start).astype(F32) * freq[...]
        cosine, sine = jnp.cos(angle), jnp.sin(angle)
        x = jnp.concatenate([tokv[2 * i], tokv[2 * i + 1]], axis=0).astype(F32)
        h = x * lax.rsqrt(jnp.mean(x * x, axis=1, keepdims=True) + NORM_EPS)
        h = (h * gains[0]).astype(BF)
        h1[2 * i], h1[2 * i + 1] = h[:TOK], h[TOK:]
        qkv = mm(h, qkv_w[...])
        blank = jnp.zeros((QROWS, TOK - HD), BF)
        for n in range(2):
            q = turn(qkv[:, n * HD : (n + 1) * HD], cosine, sine) * (SCALE * LOG2E)
            q = jnp.concatenate([q.astype(BF), blank], axis=1)
            q_out[2 * i, n * TOK : (n + 1) * TOK] = q[:TOK]
            q_out[2 * i + 1, n * TOK : (n + 1) * TOK] = q[TOK:]
        k = turn(qkv[:, 2 * HD : 3 * HD], cosine, sine)
        kv[me.x, i * QROWS : (i + 1) * QROWS] = jnp.concatenate(
            [k, qkv[:, 3 * HD : 3 * HD + TOK - HD]], axis=1
        ).astype(BF)
        tails.append(qkv[:, 3 * HD + TOK - HD :].astype(BF))
    for i in range(2):
        at = GROUP_ROWS + i * QROWS
        kv[me.x, at : at + QROWS] = jnp.concatenate([tails[i], tails[i + 2]], axis=1)
    kvs = Gather(send, me.along_x, lambda k: kv.at[me.x_at(k)], halves)
    h1_copy = send.local(h1, h1_out)

    top[...] = jnp.full_like(top, -1e30)
    total[...] = jnp.zeros_like(total)
    acc[...] = jnp.zeros_like(acc)

    def source(s):
        x = lax.rem(me.x + s + s // 2 - 2 * (s // 3), 4)
        keyv[...] = unpack(kv[x], GROUP_ROWS)
        lane = lax.broadcasted_iota(jnp.int32, (QROWS, TOK), 1)
        for t in range(NT):
            n = (t + 1) * TOK
            q = q_out[t]
            score = mm_nt(q, keyv[:n, :TOK])
            start = jnp.concatenate([starts[t]] * 2, axis=0)
            kept = []
            for b in range(t + 1):
                key = lane + (b * CHUNK + x * TOK)
                keep = key >= start
                if b == t:
                    row = lax.broadcasted_iota(jnp.int32, (QROWS, TOK), 0)
                    keep = keep & (key <= lax.rem(row, TOK) + (t * CHUNK + me.x * TOK))
                kept.append(jnp.where(keep, score[:, b * TOK : (b + 1) * TOK], -jnp.inf))
            score = jnp.concatenate(kept, axis=1) if t else kept[0]
            old = top[t]
            new = jnp.maximum(old, jnp.max(score, axis=1, keepdims=True))
            p = jnp.exp2(score - new)
            factor = jnp.exp2(old - new)
            top[t] = new
            total[t] = total[t] * factor + jnp.sum(p, axis=1, keepdims=True)
            acc[t] = acc[t] * factor + mm(p.astype(BF), keyv[:n])

    def after_own():
        kvs.forward()
        down_x.forward()

    def before_last():
        gu_z.forward()
        o_z.forward()
        cots.forward()
        cot_sib.extend(
            send(cot_all.at[me.rank(k, c)], cot_all.at[me.rank(k, c)], me.sibling())
            for k in (-1, 1)
        )
        kvs.end()

    source(0)
    after_own()
    pl.loop(1, 3)(source)
    before_last()
    source(3)

    o_z.end()
    o_x = Gather(
        send,
        me.along_x,
        lambda k: o_w.at[
            :, :, c, :, pl.ds(pl.multiple_of(me.x_at(k) * (CHUNK * 3 // 4), TOK), CHUNK * 3 // 4)
        ],
        halves,
    )
    kv_copy = send.local(kv, kv_out)
    bits = []
    for t in range(NT):
        o = acc[t][:, HD : 2 * HD] / total[t]
        lse = top[t] + jnp.log2(total[t])
        o_out[t] = o
        lse_out[t] = jnp.transpose(jnp.broadcast_to(lse, (QROWS, TOK)))[:1]
        place = places_of(me, t, (TOK, 2 * HD), 0)
        _, end = starts_of(lengths, place)
        ob = jnp.concatenate([o[:TOK], o[TOK:]], axis=1)
        ob = jnp.where(place < end, ob, 0.0).astype(BF)
        ob_out[t * TOK : (t + 1) * TOK] = ob[:, :TOK]
        bits.append(ob[:, TOK:])
    for t in range(4):
        at = GROUP_ROWS + t * TOK
        ob_out[at : at + TOK] = jnp.concatenate([bits[t], bits[t + 4]], axis=1)
    down_x.end()
    gu_z.end()
    cots.end()
    far = cot_all.at[me.rank(2, c)]
    cot_sib.append(send(far, far, me.sibling()))
    o_x.forward()
    o_x.end()
    send(o_w.at[:, :, c], o_w.at[:, :, c], me.sibling())
    for copy in (own_cot, tok_out, h1_copy, kv_copy):
        copy.wait()
    send.finish()


def front(lengths, tok, cot, wq, wk, wv, wg, wu, wo, wd, gain1, gain2):
    def like(*shape, dtype=BF):
        return jax.ShapeDtypeStruct(shape, dtype)

    rows, width = wq.shape
    part = wg.shape[1] // NT
    freq = jnp.asarray(np.tile(frequency_table(HD), 2)[None])
    outs = (
        (like(NT, TOK, width), ANY),
        (like(NT, TOK, width), ANY),
        (like(NT, TOK, width), ANY),
        (like(4, 4, rows, 2 * part), ANY),
        (like(4, 2, 2, rows, width), ANY),
        (like(4, TOK, width), ANY),
        (like(NX, PACKED, TOK), ANY),
        (like(NT, QROWS, TOK), VM),
        (like(NT, QROWS, HD, dtype=F32), VM),
        (like(NT, 1, QROWS, dtype=F32), VM),
        (like(PACKED, TOK), VM),
        (like(2, width, dtype=F32), VM),
        (like(width, 4 * HD), VM),
    )
    padded = rows + 16
    return pl.pallas_call(
        front_kernel,
        out_shape=tuple(o[0] for o in outs),
        in_specs=[SM, VM, ANY, ANY, VM, VM, VM, VM, VM, ANY, ANY, VM, VM],
        out_specs=tuple(o[1] for o in outs),
        scratch_shapes=[
            pltpu.VMEM((NT, TOK, width), BF),
            pltpu.VMEM((NT, TOK, width), BF),
            pltpu.VMEM((NT, padded, 4 * HD), BF),
            pltpu.VMEM((NT, rows, 2 * part), BF),
            pltpu.VMEM((padded, 4 * HD), BF),
            pltpu.VMEM((rows, 2 * part), BF),
            pltpu.VMEM((4, 4, padded, 4 * HD), BF),
            pltpu.VMEM((NX, PACKED, TOK), BF),
            pltpu.VMEM((GROUP_ROWS, 2 * TOK), BF),
            pltpu.VMEM((NT, TOK, TOK), jnp.int32),
            pltpu.VMEM((NT, QROWS, 1), F32),
            pltpu.VMEM((NT, QROWS, 1), F32),
            pltpu.VMEM((NT, QROWS, 2 * TOK), F32),
            pltpu.SemaphoreType.DMA((64,)),
            pltpu.SemaphoreType.DMA((64,)),
            pltpu.SemaphoreType.DMA((16,)),
        ],
        compiler_params=pltpu.CompilerParams(
            collective_id=0, has_side_effects=True, vmem_limit_bytes=56 * 2**20
        ),
        name="front",
    )(lengths, freq, tok, cot, wq, wk, wv, wg, wu, wo, wd, gain1, gain2)


def gather_begin(me, send, own, out):
    return [
        send(own, out.at[me.t], me.along_y(1)),
        send(own, out.at[me.t], me.along_y(-1)),
        send(own, out.at[me.t], me.sibling()),
    ]


def gather_rest(me, send, out, begun):
    down, up, mine = begun
    half = out.shape[1] // 2
    below, above, far = me.rank(-1, me.c), me.rank(1, me.c), me.rank(2, me.c)
    down.wait_recv()
    part = out.at[below, pl.ds(0, half)]
    on_down = send(part, part, me.along_y(1))
    sib_below = send(out.at[below], out.at[below], me.sibling())
    up.wait_recv()
    part = out.at[above, pl.ds(half, half)]
    on_up = send(part, part, me.along_y(-1))
    sib_above = send(out.at[above], out.at[above], me.sibling())
    on_down.wait_recv()
    on_up.wait_recv()
    sib_far = send(out.at[far], out.at[far], me.sibling())
    for copy in (mine, sib_below, sib_above, sib_far):
        copy.wait_recv()


def gather_kernel(own, out, send_sem, recv_sem, local_sem):
    me = Place()
    me.greet()
    send = Copies(send_sem, recv_sem)
    begun = gather_begin(me, send, own, out)
    local = pltpu.make_async_copy(own, out.at[me.t], local_sem)
    local.start()
    gather_rest(me, send, out, begun)
    local.wait()
    send.finish()


def gather_group(own, name, number):
    rows, width = own.shape
    return pl.pallas_call(
        gather_kernel,
        out_shape=jax.ShapeDtypeStruct((NT, rows, width), own.dtype),
        in_specs=[ANY],
        out_specs=ANY,
        scratch_shapes=[
            pltpu.SemaphoreType.DMA((8,)),
            pltpu.SemaphoreType.DMA((8,)),
            pltpu.SemaphoreType.DMA,
        ],
        compiler_params=pltpu.CompilerParams(collective_id=number, has_side_effects=True),
        name=name,
    )(own)


def scatter_kernel(part, out, sib, far_a, far_b, near_a, near_b, mid, send_sem, recv_sem):
    me = Place()
    me.greet()
    send = Copies(send_sem, recv_sem)
    half = TOK // 2
    lo, hi = pl.ds(0, half), pl.ds(half, half)
    other = 1 - me.c
    from_sib = {}
    for k in (2, 1, 3, 0):
        from_sib[k] = send(part.at[me.rank(k, other)], sib.at[k], me.sibling())

    def both(k, rows):
        return part[me.rank(k, me.c), rows].astype(F32) + sib[k, rows].astype(F32)

    from_sib[2].wait_recv()
    mid[2] = both(2, slice(None)).astype(BF)
    far_up = send(mid.at[2, lo], far_a, me.along_y(1))
    far_down = send(mid.at[2, hi], far_b, me.along_y(-1))
    from_sib[1].wait_recv()
    mid[1, half:] = both(1, slice(half, TOK)).astype(BF)
    up_hi = send(mid.at[1, hi], near_a.at[hi], me.along_y(1))
    from_sib[3].wait_recv()
    mid[3, :half] = both(3, slice(0, half)).astype(BF)
    down_lo = send(mid.at[3, lo], near_b.at[lo], me.along_y(-1))
    far_up.wait_recv()
    mid[1, :half] = (both(1, slice(0, half)) + far_a[...].astype(F32)).astype(BF)
    up_lo = send(mid.at[1, lo], near_a.at[lo], me.along_y(1))
    far_down.wait_recv()
    mid[3, half:] = (both(3, slice(half, TOK)) + far_b[...].astype(F32)).astype(BF)
    down_hi = send(mid.at[3, hi], near_b.at[hi], me.along_y(-1))
    from_sib[0].wait_recv()
    total = both(0, slice(None))
    for copy in (up_hi, up_lo, down_lo, down_hi):
        copy.wait_recv()
    out[...] = total + near_a[...].astype(F32) + near_b[...].astype(F32)
    send.finish()


def scatter_group(part, name, number):
    _, rows, width = part.shape
    half = rows // 2
    return pl.pallas_call(
        scatter_kernel,
        out_shape=jax.ShapeDtypeStruct((rows, width), F32),
        in_specs=[VM],
        out_specs=VM,
        scratch_shapes=[
            pltpu.VMEM((4, rows, width), BF),
            pltpu.VMEM((half, width), BF),
            pltpu.VMEM((half, width), BF),
            pltpu.VMEM((rows, width), BF),
            pltpu.VMEM((rows, width), BF),
            pltpu.VMEM((4, rows, width), BF),
            pltpu.SemaphoreType.DMA((10,)),
            pltpu.SemaphoreType.DMA((10,)),
        ],
        compiler_params=pltpu.CompilerParams(
            collective_id=number, has_side_effects=True, vmem_limit_bytes=40 * 2**20
        ),
        name=name,
    )(part)


def keys_of(ref, kt):
    return jnp.concatenate([ref[x, kt] for x in range(NX)], axis=0)


def attend_back_kernel(
    x_ref, q_ref, k_ref, v_ref, go_ref, start_ref, lse_ref, delta_ref, gq_ref, gk_ref, gv_ref
):
    x = x_ref[0]
    gk_ref[...] = jnp.zeros_like(gk_ref)
    gv_ref[...] = jnp.zeros_like(gv_ref)

    def tile(t, kt, given, gq, diagonal):
        q, go, start, lse, delta = given
        k, v = keys_of(k_ref, kt), keys_of(v_ref, kt)
        s = mm_nt(k, q)
        place = kt * CHUNK + lax.broadcasted_iota(jnp.int32, (CHUNK, QROWS), 0)
        keep = place >= start
        if diagonal:
            column = lax.broadcasted_iota(jnp.int32, (CHUNK, QROWS), 1)
            query = t * CHUNK + x * TOK + lax.rem(column, TOK)
            keep = keep & (place <= query)
        p = jnp.where(keep, jnp.exp2(s - lse), 0.0)
        gp = mm_nt(v, go)
        gs = (p * (gp - delta)).astype(BF)
        gv = mm(p.astype(BF), go)
        gk = mm(gs, q)
        for n in range(NX):
            rows = slice(n * TOK, (n + 1) * TOK)
            gv_ref[n, kt] += gv[rows]
            gk_ref[n, kt] += gk[rows]
        return gq + mm_tn(gs, k)

    def one(t, _):
        q = jnp.concatenate([q_ref[0, t], q_ref[1, t]], axis=0)
        go = jnp.concatenate([go_ref[0, t], go_ref[1, t]], axis=0)
        start = jnp.concatenate([start_ref[t]] * 2, axis=1)
        lse = jnp.concatenate([lse_ref[0, t], lse_ref[1, t]], axis=1)
        delta = jnp.concatenate([delta_ref[0, t], delta_ref[1, t]], axis=1)
        given = (q, go, start, lse, delta)
        gq = jnp.zeros((QROWS, HD), F32)
        gq = lax.fori_loop(0, t, lambda kt, g: tile(t, kt, given, g, False), gq)
        gq = tile(t, t, given, gq, True) * SCALE
        gq_ref[0, t], gq_ref[1, t] = gq[:TOK], gq[TOK:]
        return 0

    lax.fori_loop(0, NT, one, 0)


def attend_back(x_index, q, k, v, go, start, lse, delta):
    return pl.pallas_call(
        attend_back_kernel,
        out_shape=(
            jax.ShapeDtypeStruct((2, NT, TOK, HD), F32),
            jax.ShapeDtypeStruct((NX, NT, TOK, HD), F32),
            jax.ShapeDtypeStruct((NX, NT, TOK, HD), F32),
        ),
        in_specs=[SM] + [VM] * 7,
        out_specs=(VM, VM, VM),
        compiler_params=pltpu.CompilerParams(vmem_limit_bytes=48 * 2**20),
        name="attend_back",
    )(x_index, q, k, v, go, start, lse, delta)


def turn3(v, cosine, sine):
    half = HD // 2
    v1, v2 = v[..., :half], v[..., half:]
    return jnp.concatenate([v1 * cosine - v2 * sine, v2 * cosine + v1 * sine], axis=-1)


def body(
    tokens,
    doc_lengths,
    w_query,
    w_key,
    w_value,
    w_output,
    w_gate,
    w_up,
    w_down,
    gain_attn,
    gain_mlp,
    cotangent,
):
    width = tokens.shape[2]
    rows = w_query.shape[0]
    hidden_width = w_gate.shape[1]
    part = hidden_width // NT
    everyone = ("z", "yl", "c")
    x_index = lax.axis_index("x")
    yl, c, yh = lax.axis_index("yl"), lax.axis_index("c"), lax.axis_index("yh")
    ylc = yl * 2 + c
    x_scalar = x_index.reshape(1)

    tok_all, cot_all, h1, gu_w, o_w, down_w, kv_packed, qp, o, lse, ob, gains, qkv_w = front(
        doc_lengths,
        tokens[0],
        cotangent[0],
        w_query,
        w_key,
        w_value,
        w_gate,
        w_up,
        w_output,
        w_down,
        gain_attn.reshape(1, -1),
        gain_mlp.reshape(1, -1),
    )
    gu_w = gu_w.reshape(width, 2 * part)
    o_w = o_w.reshape(width, width)
    down_w = down_w.reshape(part, width)
    cot_all = cot_all.reshape(NT * TOK, width)
    h1 = h1.reshape(NT * TOK, width)
    g1, g2 = gains[:1], gains[1:]

    lengths = doc_lengths[0]
    places = (
        jnp.arange(NT, dtype=jnp.int32)[:, None] * CHUNK
        + x_index * TOK
        + jnp.arange(TOK, dtype=jnp.int32)[None, :]
    ).reshape(-1)
    segment, start = doc_layout(lengths, places)
    valid = (segment < lengths.shape[0]).astype(F32)[:, None]
    angles = (places - start).astype(F32)[:, None] * jnp.asarray(frequency_table(HD))[None, :]
    cosine, sine = jnp.cos(angles), jnp.sin(angles)
    start = start.reshape(NT, TOK)

    x_all = tok_all.reshape(NT * TOK, width).astype(F32)
    q = qp[:, :, :HD].reshape(NT, 2, TOK, HD).transpose(1, 0, 2, 3)
    kv_all = jax.vmap(lambda a: unpack(a, NT * TOK))(kv_packed)
    k_all = kv_all[:, :, :HD].reshape(NX, NT, TOK, HD)
    v_all = kv_all[:, :, HD : 2 * HD].reshape(NX, NT, TOK, HD)
    flat = o.reshape(NT, 2, TOK, HD).transpose(0, 2, 1, 3).reshape(NT * TOK, 2 * HD)
    lse = lse.reshape(NT, 2, TOK).transpose(1, 0, 2)[:, :, None, :]
    ob_all = gather_group(ob, "gather_ob", 1)
    ob_all = jax.vmap(lambda a: unpack(a, NT * TOK))(ob_all)[:, :, : 2 * HD]
    ob_all = ob_all.transpose(1, 0, 2).reshape(NT * TOK, width)

    x2 = x_all + mm(ob_all, o_w)
    r2 = lax.rsqrt(jnp.mean(x2 * x2, axis=1, keepdims=True) + NORM_EPS)
    h2 = (x2 * r2 * g2).astype(BF)
    gu = mm(h2, gu_w)
    gate, up = gu[:, :part], gu[:, part:]
    sigmoid = jax.nn.sigmoid(gate)
    silu = gate * sigmoid
    hidden = (silu * up).astype(BF)
    y_part = mm(hidden, down_w).astype(BF).reshape(NT, TOK, width)
    gh = mm_nt(cot_all, down_w)
    ggate = (gh * up * sigmoid * (1.0 + gate * (1.0 - sigmoid))).astype(BF)
    gup = (gh * silu).astype(BF)
    ggu = jnp.concatenate([ggate, gup], axis=1)
    gh2_part = mm_nt(ggu, gu_w).astype(BF).reshape(NT, TOK, width)
    gh2 = scatter_group(gh2_part, "scatter_gh2", 2)
    t = ylc * 2 + yh
    own = lax.dynamic_slice_in_dim(x2, t * TOK, TOK, 0)
    own_r2 = lax.dynamic_slice_in_dim(r2, t * TOK, TOK, 0)
    n2 = own * own_r2
    gm = gh2 * g2
    gain_mlp_grad = jnp.sum(gh2 * n2, axis=0)
    gx2 = own_r2 * (gm - n2 * jnp.mean(gm * n2, axis=1, keepdims=True)) + cotangent[0].astype(F32)
    ga = gather_group(gx2.astype(BF), "gather_ga", 3).reshape(NT * TOK, width)
    layer_out = own + scatter_group(y_part, "scatter_y", 4)

    o_rows = lax.dynamic_slice_in_dim(o_w, t * 2 * HD, 2 * HD, 0)
    go = (mm_nt(ga, o_rows) * valid).astype(BF)
    delta = jnp.sum((go.astype(F32) * flat).reshape(NT, TOK, 2, HD), axis=3)
    delta = delta.transpose(2, 0, 1)[:, :, None, :]
    go4 = go.reshape(NT, TOK, 2, HD).transpose(2, 0, 1, 3)
    gq, gk, gv = attend_back(
        x_scalar, q, k_all, v_all, go4, start[:, None, :], lse, delta
    )
    gkv = jnp.stack([gk * LN2, gv], axis=1).astype(BF)
    gkv = lax.psum_scatter(gkv, "x", scatter_dimension=0).astype(F32)
    gq = turn3(gq.transpose(1, 2, 0, 3).reshape(-1, 2, HD), cosine[:, None], -sine[:, None])
    gk = turn3(gkv[0].reshape(-1, HD), cosine, -sine)
    gqkv = jnp.concatenate([gq.reshape(-1, 2 * HD), gk, gkv[1].reshape(-1, HD)], axis=1).astype(BF)
    gh1_part = mm_nt(gqkv, qkv_w).astype(BF).reshape(NT, TOK, width)
    gh1 = scatter_group(gh1_part, "scatter_gh1", 5)
    x_own = tokens[0].astype(F32)
    r1 = lax.rsqrt(jnp.mean(x_own * x_own, axis=1, keepdims=True) + NORM_EPS)
    n1 = x_own * r1
    gn = gh1 * g1
    gain_attn_grad = jnp.sum(gh1 * n1, axis=0)
    tokens_grad = gx2 + r1 * (gn - n1 * jnp.mean(gn * n1, axis=1, keepdims=True))

    ob_heads = ob_all.reshape(NT * TOK, 4, 4, HD)
    ob_mine = lax.dynamic_index_in_dim(ob_heads, ylc, 2, keepdims=False).reshape(NT * TOK, 4 * HD)
    ga_mine = lax.dynamic_slice_in_dim(ga, yh * (width // 2), width // 2, 1)
    grad_o = mm_tn(ob_mine, ga_mine).astype(BF)
    grad_gu = mm_tn(h2, ggu).astype(BF)
    grad_down = mm_tn(hidden, cot_all).astype(BF)
    grad_qkv = mm_tn(h1, gqkv).astype(BF)
    gain_grads = jnp.stack([gain_attn_grad, gain_mlp_grad], axis=1).astype(BF)
    gain_grads = jnp.pad(gain_grads, ((0, 0), (0, TOK - 2)))

    def over_z(a):
        return lax.psum_scatter(a, "z", scatter_dimension=0, tiled=True)

    sum_gu, sum_down, sum_o = over_z(grad_gu), over_z(grad_down), over_z(grad_o)
    sum_qkv = over_z(jnp.concatenate([grad_qkv, gain_grads], axis=1))
    columns = jnp.concatenate([sum_gu, sum_qkv], axis=1)
    columns = lax.all_to_all(columns, ("yl", "c"), split_axis=0, concat_axis=0, tiled=True)
    columns, sum_down, sum_o = lax.psum((columns, sum_down, sum_o), "x")
    columns = lax.all_gather(columns, "yh", axis=0)
    sum_down = lax.all_gather(sum_down, "yh", axis=0, tiled=True).astype(F32)
    sum_o = lax.all_gather(sum_o, "yh", axis=1, tiled=True).astype(F32)
    columns = columns.reshape(2, 4, rows, 2 * part + 4 * TOK).astype(F32)
    columns = columns.transpose(2, 1, 0, 3)

    def hidden_columns(a):
        return a.reshape(rows, 4, 2, 4, TOK).transpose(0, 3, 1, 2, 4).reshape(rows, hidden_width)

    grad_gate = hidden_columns(columns[..., :part])
    grad_up = hidden_columns(columns[..., part : 2 * part])
    base = 2 * part
    grad_query = columns[..., base : base + 2 * HD].reshape(rows, width)
    grad_key = columns[..., base + 2 * HD : base + 3 * HD].reshape(rows, KV * HD)
    grad_value = columns[..., base + 3 * HD : base + 4 * HD].reshape(rows, KV * HD)
    grad_gains = jnp.sum(columns[..., base + 4 * HD : base + 4 * HD + 2], axis=(1, 2))
    return (
        layer_out.astype(BF)[None],
        tokens_grad.astype(BF)[None],
        grad_query,
        grad_key,
        grad_value,
        sum_o,
        grad_gate,
        grad_up,
        sum_down,
        grad_gains[:, 0],
        grad_gains[:, 1],
    )


def solution(mesh):
    fine = Mesh(mesh.devices.reshape(4, 2, 2, 2, 4), AXES)
    by_token = P("z", ("yl", "c", "yh", "x"), None)
    by_row = P(("z", "yl", "c"), None)
    by_feature = P(("z", "yl", "c"))
    return jax.shard_map(
        body,
        mesh=fine,
        in_specs=(by_token, P("z", None))
        + (by_row,) * 7
        + (by_feature, by_feature, by_token),
        out_specs=(by_token, by_token) + (by_row,) * 7 + (by_feature, by_feature),
        check_vma=False,
    )
```

```python
import jax
import jax.numpy as jnp
import numpy as np
from jax import lax
from jax.experimental import pallas as pl
from jax.experimental.pallas import tpu as pltpu
from jax.sharding import Mesh
from jax.sharding import PartitionSpec as P

HEADS = 16
KV = 8
HD = 96
NORM_EPS = 1e-05
LOG2E = 1.4426950408889634
LN2 = 0.6931471805599453
SCALE = HD ** (-0.5)
BF = jnp.bfloat16
F32 = jnp.float32
AXES = ("z", "yl", "c", "yh", "x")
GROUP = ("yl", "c", "yh")
MESH = pl.DeviceIdType.MESH
TOK = 128
NT = 8
NX = 4


def frequency_table(head_width):
    halfway = head_width // 2
    base_freq = 500000.0 ** (-np.arange(halfway) * 2.0 / head_width)
    wavelength = 2.0 * np.pi / base_freq
    smooth = (8192.0 / wavelength - 1.0) / 3.0
    middle = (1.0 - smooth) * base_freq / 32.0 + smooth * base_freq
    freq_table = np.where(
        wavelength > 8192.0, base_freq / 32.0, np.where(wavelength < 2048.0, base_freq, middle)
    )
    return freq_table.astype(np.float32)


def mm(a, b):
    return jnp.dot(a, b, preferred_element_type=F32)


def mm_nt(a, b):
    return lax.dot_general(a, b, (((1,), (1,)), ((), ())), preferred_element_type=F32)


def mm_tn(a, b):
    return lax.dot_general(a, b, (((0,), (0,)), ((), ())), preferred_element_type=F32)


class Place:
    def __init__(self):
        self.z, self.x = lax.axis_index("z"), lax.axis_index("x")
        self.yl, self.c, self.yh = (lax.axis_index(name) for name in GROUP)
        self.y = self.yh * 2 + self.yl
        self.t = self.rank(0, self.c)

    def rank(self, k, c):
        y = lax.rem(self.y + (k + 4), 4)
        return lax.rem(y, 2) * 4 + c * 2 + y // 2

    def along_y(self, k):
        y = lax.rem(self.y + (k + 4), 4)
        return {"yh": y // 2, "yl": lax.rem(y, 2)}

    def x_at(self, k):
        return lax.rem(self.x + (k + 4), 4)

    def z_at(self, k):
        return lax.rem(self.z + (k + 4), 4)

    def along_x(self, k):
        return {"x": self.x_at(k)}

    def along_z(self, k):
        return {"z": self.z_at(k)}

    def sibling(self):
        return {"c": 1 - self.c}

    def greet(self, others=()):
        barrier = pltpu.get_barrier_semaphore()
        everyone = (self.along_y(1), self.along_y(-1), self.sibling()) + tuple(others)
        for who in everyone:
            pl.semaphore_signal(barrier, inc=1, device_id=who, device_id_type=MESH)
        pl.semaphore_wait(barrier, len(everyone))


class Sent:
    def __init__(self, copy):
        self.copy, self.arrived = copy, False

    def wait_recv(self):
        if not self.arrived:
            self.copy.wait_recv()
        self.arrived = True

    def wait_send(self):
        self.copy.wait_send()


class Copies:
    def __init__(self, send_sem, recv_sem, local_sem=None):
        self.send_sem, self.recv_sem, self.local_sem = send_sem, recv_sem, local_sem
        self.all, self.locals = [], []

    def __call__(self, src, dst, who):
        i = len(self.all)
        assert i < self.send_sem.shape[0]
        copy = pltpu.make_async_remote_copy(
            src_ref=src,
            dst_ref=dst,
            send_sem=self.send_sem.at[i],
            recv_sem=self.recv_sem.at[i],
            device_id=who,
            device_id_type=MESH,
        )
        copy.start()
        sent = Sent(copy)
        self.all.append(sent)
        return sent

    def local(self, src, dst):
        assert len(self.locals) < self.local_sem.shape[0]
        copy = pltpu.make_async_copy(src, dst, self.local_sem.at[len(self.locals)])
        copy.start()
        self.locals.append(copy)
        return copy

    def finish(self):
        for sent in self.all:
            sent.wait_recv()
        for sent in self.all:
            sent.wait_send()


class Gather:
    def __init__(self, send, along, slot, cut, src=None):
        self.send, self.along, self.slot, self.cut = send, along, slot, cut
        src = slot(0) if src is None else src
        self.up = send(src, slot(0), along(1))
        self.down = send(src, slot(0), along(-1))

    def forward(self):
        self.up.wait_recv()
        part = self.cut(self.slot(-1), 0)
        self.far_up = self.send(part, part, self.along(1))
        self.down.wait_recv()
        part = self.cut(self.slot(1), 1)
        self.far_down = self.send(part, part, self.along(-1))

    def end(self):
        self.far_up.wait_recv()
        self.far_down.wait_recv()


def halves(ref, i):
    half = ref.shape[0] // 2
    return ref.at[pl.ds(i * half, half)]


ANY = pl.BlockSpec(memory_space=pl.ANY)
VM = pl.BlockSpec(memory_space=pltpu.VMEM)
SM = pl.BlockSpec(memory_space=pltpu.SMEM)
GROUP_ROWS = NT * TOK
QROWS = 2 * TOK
CHUNK = NX * TOK
PACKED = GROUP_ROWS + GROUP_ROWS // 2


def starts_of(lengths_ref, place):
    end, start = 0, jnp.zeros_like(place)
    for i in range(lengths_ref.shape[1]):
        end = end + lengths_ref[0, i]
        start = jnp.maximum(start, jnp.where(place >= end, end, 0))
    return start, end


def places_of(me, tile, shape, axis):
    row = lax.broadcasted_iota(jnp.int32, shape, axis)
    return (tile + row // TOK) * CHUNK + me.x * TOK + lax.rem(row, TOK)


def turn(v, cosine, sine):
    half = HD // 2
    return v * cosine + jnp.concatenate([-v[:, half:], v[:, :half]], axis=1) * sine


def unpack(packed, n):
    low, high = packed[n:, : TOK // 2], packed[n:, TOK // 2 :]
    tail = jnp.concatenate([low, high], axis=0)
    return jnp.concatenate([packed[:n], tail, jnp.zeros_like(tail)], axis=1)


def front_kernel(
    lengths, freq, tok, cot, wq, wk, wv, wg, wu, wo, wd, gain1, gain2,
    tok_all, cot_all, h1_out, gu_w, o_w, down_w, kv_out, q_out, o_out, lse_out, ob_out, gains_out, qkv_w,
    tokv, h1, slices_q, slices_u, tmp_q, tmp_u, gq, kv, keyv, starts, top, total, acc,
    send_sem, recv_sem, local_sem,
):
    me = Place()
    me.greet((me.along_x(1), me.along_x(-1), me.along_z(1), me.along_z(-1)))
    send = Copies(send_sem, recv_sem, local_sem)
    c, other = me.c, 1 - me.c
    step = 1 - 2 * c
    slot, slot_other = me.yl * 2 + c, me.yl * 2 + other
    toward, away = me.along_y(step), me.along_y(-step)
    t_toward, t_relay, t_sib = me.rank(step, c), me.rank(step, other), me.rank(0, other)
    rows, width = wq.shape

    slices_q[:, rows:, :] = jnp.zeros_like(slices_q[:, rows:, :])
    for t in range(NT):
        slices_q[t, :rows] = jnp.concatenate(
            [
                wq[:, 2 * HD * t : 2 * HD * (t + 1)],
                wk[:, HD * t : HD * (t + 1)],
                wv[:, HD * t : HD * (t + 1)],
            ],
            axis=1,
        )
        slices_q[t, rows : rows + 1, :rows] = gain1[...]
        slices_q[t, rows + 1 : rows + 2, :rows] = gain2[...]
    relay_q = send(slices_q.at[t_relay], tmp_q, me.sibling())
    arrived_q = [
        send(slices_q.at[t_sib], gq.at[me.z, slot], me.sibling()),
        send(slices_q.at[t_toward], gq.at[me.z, slot], toward),
    ]
    own_q = send.local(slices_q.at[me.t], gq.at[me.z, slot])
    own_tok = send.local(tok, tokv.at[me.t])
    tokens = Gather(send, me.along_y, lambda k: tokv.at[me.rank(k, c)], halves, tok)
    tok_sib = [send(tok, tokv.at[me.t], me.sibling())]
    quarter = 32
    rows_of = lambda i: pl.ds(pl.multiple_of(i * quarter, quarter), quarter)
    down_src = wd.at[pl.ds(pl.multiple_of(me.yh * TOK + me.x * quarter, quarter), quarter)]
    own_down = send.local(down_src, down_w.at[me.z, rows_of(me.x)])
    down_z = Gather(
        send, me.along_z, lambda k: down_w.at[me.z_at(k), rows_of(me.x)], halves, down_src
    )
    relay_q.wait_recv()
    arrived_q.append(send(tmp_q, gq.at[me.z, slot_other], away))

    part = wg.shape[1] // NT
    for t in range(NT):
        for n in range(4):
            at = n * 2 * CHUNK + t * TOK
            slices_u[t, :, n * TOK : (n + 1) * TOK] = wg[:, at : at + TOK]
            slices_u[t, :, part + n * TOK : part + (n + 1) * TOK] = wu[:, at : at + TOK]

    for t in range(NT):
        place = places_of(me, t, (TOK, TOK), 0)
        starts[t], _ = starts_of(lengths, place)

    own_q.wait()
    for copy in arrived_q:
        copy.wait_recv()
    qkv_z = Gather(send, me.along_z, lambda k: gq.at[me.z_at(k)], halves)
    tokens.forward()
    tok_sib += [
        send(tokv.at[me.rank(k, c)], tokv.at[me.rank(k, c)], me.sibling()) for k in (-1, 1)
    ]
    relay_u = send(slices_u.at[t_relay], tmp_u, me.sibling())
    arrived_u = [
        send(slices_u.at[t_sib], gu_w.at[me.z, slot], me.sibling()),
        send(slices_u.at[t_toward], gu_w.at[me.z, slot], toward),
    ]
    own_u = send.local(slices_u.at[me.t], gu_w.at[me.z, slot])
    third = pl.ds(pl.multiple_of(me.x * CHUNK * 3 // 4, TOK), CHUNK * 3 // 4)
    arrived_o = send(wo, o_w.at[me.z, me.yl, c], toward)
    own_o = send.local(wo, o_w.at[me.z, me.yl, c])
    relay_u.wait_recv()
    arrived_u.append(send(tmp_u, gu_w.at[me.z, slot_other], away))
    own_down.wait()
    down_z.forward()
    qkv_z.forward()
    tokens.end()
    far = tokv.at[me.rank(2, c)]
    tok_sib.append(send(far, far, me.sibling()))
    cots = Gather(send, me.along_y, lambda k: cot_all.at[me.rank(k, c)], halves, cot)
    own_cot = send.local(cot, cot_all.at[me.t])
    cot_sib = [send(cot, cot_all.at[me.t], me.sibling())]
    down_z.end()
    down_x = Gather(
        send, me.along_x, lambda k: down_w.at[:, rows_of(me.x_at(k))], halves
    )
    own_u.wait()
    for copy in arrived_u:
        copy.wait_recv()
    qkv_z.end()
    gu_z = Gather(send, me.along_z, lambda k: gu_w.at[me.z_at(k)], halves)
    own_o.wait()
    arrived_o.wait_recv()
    o_z = Gather(send, me.along_z, lambda k: o_w.at[me.z_at(k), :, c, :, third], halves)
    own_tok.wait()
    for copy in tok_sib:
        copy.wait_recv()
    tok_out = send.local(tokv, tok_all)

    gains = [
        jnp.concatenate(
            [gq[z, n, rows + g : rows + g + 1, :rows] for z in range(4) for n in range(4)], axis=1
        ).astype(F32)
        for g in range(2)
    ]
    gains_out[...] = jnp.concatenate(gains, axis=0)
    for z in range(4):
        for n in range(4):
            at = (z * 4 + n) * rows
            qkv_w[at : at + rows] = gq[z, n, :rows]
    tails = []
    for i in range(4):
        place = places_of(me, 2 * i, (QROWS, HD), 0)
        start, _ = starts_of(lengths, place)
        angle = (place - start).astype(F32) * freq[...]
        cosine, sine = jnp.cos(angle), jnp.sin(angle)
        x = jnp.concatenate([tokv[2 * i], tokv[2 * i + 1]], axis=0).astype(F32)
        h = x * lax.rsqrt(jnp.mean(x * x, axis=1, keepdims=True) + NORM_EPS)
        h = (h * gains[0]).astype(BF)
        h1[2 * i], h1[2 * i + 1] = h[:TOK], h[TOK:]
        qkv = mm(h, qkv_w[...])
        blank = jnp.zeros((QROWS, TOK - HD), BF)
        for n in range(2):
            q = turn(qkv[:, n * HD : (n + 1) * HD], cosine, sine) * (SCALE * LOG2E)
            q = jnp.concatenate([q.astype(BF), blank], axis=1)
            q_out[2 * i, n * TOK : (n + 1) * TOK] = q[:TOK]
            q_out[2 * i + 1, n * TOK : (n + 1) * TOK] = q[TOK:]
        k = turn(qkv[:, 2 * HD : 3 * HD], cosine, sine)
        kv[me.x, i * QROWS : (i + 1) * QROWS] = jnp.concatenate(
            [k, qkv[:, 3 * HD : 3 * HD + TOK - HD]], axis=1
        ).astype(BF)
        tails.append(qkv[:, 3 * HD + TOK - HD :].astype(BF))
    for i in range(2):
        at = GROUP_ROWS + i * QROWS
        kv[me.x, at : at + QROWS] = jnp.concatenate([tails[i], tails[i + 2]], axis=1)
    kvs = Gather(send, me.along_x, lambda k: kv.at[me.x_at(k)], halves)
    h1_copy = send.local(h1, h1_out)

    top[...] = jnp.full_like(top, -1e30)
    total[...] = jnp.zeros_like(total)
    acc[...] = jnp.zeros_like(acc)

    def source(s):
        x = lax.rem(me.x + s + s // 2 - 2 * (s // 3), 4)
        keyv[...] = unpack(kv[x], GROUP_ROWS)
        lane = lax.broadcasted_iota(jnp.int32, (QROWS, TOK), 1)
        for t in range(NT):
            n = (t + 1) * TOK
            q = q_out[t]
            score = mm_nt(q, keyv[:n, :TOK])
            start = jnp.concatenate([starts[t]] * 2, axis=0)
            kept = []
            for b in range(t + 1):
                key = lane + (b * CHUNK + x * TOK)
                keep = key >= start
                if b == t:
                    row = lax.broadcasted_iota(jnp.int32, (QROWS, TOK), 0)
                    keep = keep & (key <= lax.rem(row, TOK) + (t * CHUNK + me.x * TOK))
                kept.append(jnp.where(keep, score[:, b * TOK : (b + 1) * TOK], -jnp.inf))
            score = jnp.concatenate(kept, axis=1) if t else kept[0]
            old = top[t]
            new = jnp.maximum(old, jnp.max(score, axis=1, keepdims=True))
            p = jnp.exp2(score - new)
            factor = jnp.exp2(old - new)
            top[t] = new
            total[t] = total[t] * factor + jnp.sum(p, axis=1, keepdims=True)
            acc[t] = acc[t] * factor + mm(p.astype(BF), keyv[:n])

    def after_own():
        kvs.forward()
        down_x.forward()

    def before_last():
        gu_z.forward()
        o_z.forward()
        cots.forward()
        cot_sib.extend(
            send(cot_all.at[me.rank(k, c)], cot_all.at[me.rank(k, c)], me.sibling())
            for k in (-1, 1)
        )
        kvs.end()

    source(0)
    after_own()
    pl.loop(1, 3)(source)
    before_last()
    source(3)

    o_z.end()
    o_x = Gather(
        send,
        me.along_x,
        lambda k: o_w.at[
            :, :, c, :, pl.ds(pl.multiple_of(me.x_at(k) * (CHUNK * 3 // 4), TOK), CHUNK * 3 // 4)
        ],
        halves,
    )
    kv_copy = send.local(kv, kv_out)
    bits = []
    for t in range(NT):
        o = acc[t][:, HD : 2 * HD] / total[t]
        lse = top[t] + jnp.log2(total[t])
        o_out[t] = o
        lse_out[t] = jnp.transpose(jnp.broadcast_to(lse, (QROWS, TOK)))[:1]
        place = places_of(me, t, (TOK, 2 * HD), 0)
        _, end = starts_of(lengths, place)
        ob = jnp.concatenate([o[:TOK], o[TOK:]], axis=1)
        ob = jnp.where(place < end, ob, 0.0).astype(BF)
        ob_out[t * TOK : (t + 1) * TOK] = ob[:, :TOK]
        bits.append(ob[:, TOK:])
    for t in range(4):
        at = GROUP_ROWS + t * TOK
        ob_out[at : at + TOK] = jnp.concatenate([bits[t], bits[t + 4]], axis=1)
    down_x.end()
    gu_z.end()
    cots.end()
    far = cot_all.at[me.rank(2, c)]
    cot_sib.append(send(far, far, me.sibling()))
    o_x.forward()
    o_x.end()
    send(o_w.at[:, :, c], o_w.at[:, :, c], me.sibling())
    for copy in (own_cot, tok_out, h1_copy, kv_copy):
        copy.wait()
    send.finish()


def front(lengths, tok, cot, wq, wk, wv, wg, wu, wo, wd, gain1, gain2):
    def like(*shape, dtype=BF):
        return jax.ShapeDtypeStruct(shape, dtype)

    rows, width = wq.shape
    part = wg.shape[1] // NT
    freq = jnp.asarray(np.tile(frequency_table(HD), 2)[None])
    outs = (
        (like(NT, TOK, width), ANY),
        (like(NT, TOK, width), ANY),
        (like(NT, TOK, width), ANY),
        (like(4, 4, rows, 2 * part), ANY),
        (like(4, 2, 2, rows, width), ANY),
        (like(4, TOK, width), ANY),
        (like(NX, PACKED, TOK), ANY),
        (like(NT, QROWS, TOK), VM),
        (like(NT, QROWS, HD, dtype=F32), VM),
        (like(NT, 1, QROWS, dtype=F32), VM),
        (like(PACKED, TOK), VM),
        (like(2, width, dtype=F32), VM),
        (like(width, 4 * HD), VM),
    )
    padded = rows + 16
    return pl.pallas_call(
        front_kernel,
        out_shape=tuple(o[0] for o in outs),
        in_specs=[SM, VM, ANY, ANY, VM, VM, VM, VM, VM, ANY, ANY, VM, VM],
        out_specs=tuple(o[1] for o in outs),
        scratch_shapes=[
            pltpu.VMEM((NT, TOK, width), BF),
            pltpu.VMEM((NT, TOK, width), BF),
            pltpu.VMEM((NT, padded, 4 * HD), BF),
            pltpu.VMEM((NT, rows, 2 * part), BF),
            pltpu.VMEM((padded, 4 * HD), BF),
            pltpu.VMEM((rows, 2 * part), BF),
            pltpu.VMEM((4, 4, padded, 4 * HD), BF),
            pltpu.VMEM((NX, PACKED, TOK), BF),
            pltpu.VMEM((GROUP_ROWS, 2 * TOK), BF),
            pltpu.VMEM((NT, TOK, TOK), jnp.int32),
            pltpu.VMEM((NT, QROWS, 1), F32),
            pltpu.VMEM((NT, QROWS, 1), F32),
            pltpu.VMEM((NT, QROWS, 2 * TOK), F32),
            pltpu.SemaphoreType.DMA((64,)),
            pltpu.SemaphoreType.DMA((64,)),
            pltpu.SemaphoreType.DMA((16,)),
        ],
        compiler_params=pltpu.CompilerParams(
            collective_id=0, has_side_effects=True, vmem_limit_bytes=56 * 2**20
        ),
        name="front",
    )(lengths, freq, tok, cot, wq, wk, wv, wg, wu, wo, wd, gain1, gain2)


class Scatter:
    def __init__(self, me, send, mine, sib, mid, far, near):
        self.me, self.send, self.mine, self.sib, self.mid = me, send, mine, sib, mid
        self.far, self.near, self.from_sib = far, near, {}
        self.half = sib.shape[1] // 2

    def hand(self, k, src):
        self.from_sib[k] = self.send(src, self.sib.at[k], self.me.sibling())

    def pair(self, k, i):
        rows = slice(i * self.half, (i + 1) * self.half)
        return self.mine(k, rows).astype(F32) + self.sib[k, rows].astype(F32)

    def put(self, k, i, value):
        self.mid[k, i * self.half : (i + 1) * self.half] = value.astype(BF)
        return self.mid.at[k, pl.ds(i * self.half, self.half)]

    def step2(self):
        self.from_sib[2].wait_recv()
        up, down = self.me.along_y(1), self.me.along_y(-1)
        self.far_up = self.send(self.put(2, 0, self.pair(2, 0)), self.far.at[0], up)
        self.far_down = self.send(self.put(2, 1, self.pair(2, 1)), self.far.at[1], down)

    def step1(self):
        self.from_sib[1].wait_recv()
        src = self.put(1, 1, self.pair(1, 1))
        self.last = [self.send(src, halves(self.near.at[0], 1), self.me.along_y(1))]

    def step3(self):
        self.from_sib[3].wait_recv()
        src = self.put(3, 0, self.pair(3, 0))
        self.last.append(self.send(src, halves(self.near.at[1], 0), self.me.along_y(-1)))

    def step0(self):
        self.far_up.wait_recv()
        src = self.put(1, 0, self.pair(1, 0) + self.far[0].astype(F32))
        self.last.append(self.send(src, halves(self.near.at[0], 0), self.me.along_y(1)))
        self.far_down.wait_recv()
        src = self.put(3, 1, self.pair(3, 1) + self.far[1].astype(F32))
        self.last.append(self.send(src, halves(self.near.at[1], 1), self.me.along_y(-1)))

    def end(self):
        self.from_sib[0].wait_recv()
        for copy in self.last:
            copy.wait_recv()
        total = self.mine(0, slice(None)).astype(F32) + self.sib[0].astype(F32)
        return total + self.near[0].astype(F32) + self.near[1].astype(F32)


def middle_kernel(
    lengths, ob, tok_all, cot_all, o_w, gu_w, down_w, gains, o_in,
    go_out, delta_out, gx2_out, x2_out, y_out, grad_gu, grad_down, grad_o, gain_out,
    obv, obx, ow, guw, dw, cotv, tokv, x2, h2, hid, ggu, mine, tosib, sib, mid, far, near,
    send_sem, recv_sem, local_sem,
):
    me = Place()
    me.greet()
    send = Copies(send_sem, recv_sem, local_sem)
    c, other = me.c, 1 - me.c
    width = gains.shape[1]
    part = hid.shape[2]
    pair = 2 * HD
    blocks = Gather(send, me.along_y, lambda k: obv.at[me.rank(k, c)], halves, ob)
    ob_sib = [send(ob, obv.at[me.t], me.sibling())]
    own = send.local(ob, obv.at[me.t])
    loads = [
        send.local(tok_all, tokv),
        send.local(o_w, ow.at[pl.ds(0, width)]),
        send.local(gu_w, guw),
        send.local(cot_all, cotv),
        send.local(down_w, dw),
    ]
    ow[width:] = jnp.zeros_like(ow[width:])

    def project(ranks, first):
        for t in ranks:
            obx[t] = unpack(obv[t], GROUP_ROWS)

        @pl.loop(0, 4)
        def _(i):
            rows = pl.ds(pl.multiple_of(i * QROWS, QROWS), QROWS)
            for n in range(3):
                cols = slice(n * CHUNK, (n + 1) * CHUNK)
                if first:
                    value = jnp.concatenate(
                        [tokv[2 * i, :, cols], tokv[2 * i + 1, :, cols]], axis=0
                    ).astype(F32)
                else:
                    value = x2[rows, cols]
                for t in ranks:
                    w = ow[pl.ds(pl.multiple_of(t * pair, pair // 3), 2 * TOK), cols]
                    value += mm(obx[t, rows], w)
                x2[rows, cols] = value

    own.wait()
    ob_sib[0].wait_recv()
    loads[0].wait()
    loads[1].wait()
    project([me.t, me.rank(0, other)], True)
    blocks.forward()
    ob_sib = [
        send(obv.at[me.rank(k, c)], obv.at[me.rank(k, c)], me.sibling()) for k in (-1, 1)
    ]
    project([me.rank(-1, c), me.rank(1, c)], False)
    for copy in ob_sib:
        copy.wait_recv()
    project([me.rank(-1, other), me.rank(1, other)], False)
    blocks.end()
    last = send(obv.at[me.rank(2, c)], obv.at[me.rank(2, c)], me.sibling())
    loads[2].wait()
    loads[3].wait()
    loads[4].wait()
    last.wait_recv()
    project([me.rank(2, c), me.rank(2, other)], False)

    g2 = gains[1:2]
    sums = Scatter(me, send, lambda k, at: mine[k, at], sib, mid, far, near)

    def at(t):
        return pl.ds(pl.multiple_of(t * TOK, TOK), TOK)

    def feed(k):
        ranks = (me.rank(k, c), me.rank(k, other))
        x = jnp.concatenate([x2[at(t)] for t in ranks], axis=0)
        h = x * lax.rsqrt(jnp.mean(x * x, axis=1, keepdims=True) + NORM_EPS)
        h = (h * g2).astype(BF)
        gu = mm(h, guw[...])
        gate, up = gu[:, :part], gu[:, part:]
        sigmoid = 1.0 / (1.0 + jnp.exp(-gate))
        silu = gate * sigmoid
        hidden = (silu * up).astype(BF)
        cot = jnp.concatenate([cotv[t] for t in ranks], axis=0)
        gh = mm_nt(cot, dw[...])
        ggate = (gh * up * sigmoid * (1.0 + gate * (1.0 - sigmoid))).astype(BF)
        gup = (gh * silu).astype(BF)
        both = jnp.concatenate([ggate, gup], axis=1)
        gh2 = mm_nt(both, guw[...]).astype(BF)
        mine[k], tosib[k] = gh2[:TOK], gh2[TOK:]
        sums.hand(k, tosib.at[k])
        y = mm(hidden, dw[...]).astype(BF)
        for n, t in enumerate(ranks):
            rows = slice(n * TOK, (n + 1) * TOK)
            h2[t], hid[t], ggu[t], y_out[t] = h[rows], hidden[rows], both[rows], y[rows]

    feed(2)
    feed(1)
    sums.step2()
    feed(3)
    sums.step1()
    feed(0)
    sums.step3()
    sums.step0()

    @pl.loop(0, 3)
    def _(n):
        cols = pl.ds(pl.multiple_of(n * CHUNK, CHUNK), CHUNK)
        cot = cotv[:, :, cols].reshape(GROUP_ROWS, CHUNK)
        value = mm_tn(hid[...].reshape(GROUP_ROWS, part), cot).astype(BF)
        grad_down[:, :, cols] = value.reshape(4, TOK, CHUNK)

    gh2 = sums.end()
    x = x2[at(me.t)]
    x2_out[...] = x
    r2 = lax.rsqrt(jnp.mean(x * x, axis=1, keepdims=True) + NORM_EPS)
    n2 = x * r2
    gm = gh2 * g2
    gain_out[...] = jnp.sum(gh2 * n2, axis=0, keepdims=True)
    gx2 = r2 * (gm - n2 * jnp.mean(gm * n2, axis=1, keepdims=True)) + cotv[me.t].astype(F32)
    gx2_out[...] = gx2
    gav = tokv
    gav[me.t] = gx2.astype(BF)
    back = Gather(send, me.along_y, lambda k: gav.at[me.rank(k, c)], halves)
    back_sib = [send(gav.at[me.t], gav.at[me.t], me.sibling())]

    def grad_columns(z):
        cols = pl.ds(pl.multiple_of(z * 4 * HD, TOK), 4 * HD)
        h = h2[:, :, cols].reshape(GROUP_ROWS, 4 * HD)
        value = mm_tn(h, ggu[...].reshape(GROUP_ROWS, 2 * part)).astype(BF)
        for n in range(4):
            for j in range(8):
                grad_gu[z, n, j * HD : (j + 1) * HD] = value[
                    n * HD : (n + 1) * HD, j * TOK : (j + 1) * TOK
                ]

    pl.loop(0, 3)(grad_columns)
    back.forward()
    back_sib += [
        send(gav.at[me.rank(k, c)], gav.at[me.rank(k, c)], me.sibling()) for k in (-1, 1)
    ]
    grad_columns(3)
    back.end()
    back_sib.append(send(gav.at[me.rank(2, c)], gav.at[me.rank(2, c)], me.sibling()))
    for copy in back_sib:
        copy.wait_recv()

    w_own = ow[pl.ds(pl.multiple_of(me.t * pair, pair // 3), pair)]
    for i in range(4):
        ga = jnp.concatenate([gav[2 * i], gav[2 * i + 1]], axis=0)
        go = mm_nt(ga, w_own)
        place = places_of(me, 2 * i, (QROWS, pair), 0)
        _, end = starts_of(lengths, place)
        go = jnp.where(place < end, go, 0.0).astype(BF)
        for n in range(2):
            t = 2 * i + n
            both = [go[n * TOK : (n + 1) * TOK, h * HD : (h + 1) * HD] for h in range(2)]
            both = jnp.concatenate(both, axis=0)
            delta = jnp.sum(both.astype(F32) * o_in[t], axis=1, keepdims=True)
            delta_out[t] = jnp.transpose(jnp.broadcast_to(delta, (QROWS, TOK)))[:1]
            before, after = jnp.zeros((QROWS, HD), BF), jnp.zeros((QROWS, 2 * TOK - pair), BF)
            go_out[t] = jnp.concatenate([before, both, after], axis=1)
    half = width // 2
    cols = pl.ds(pl.multiple_of(me.yh * half, half), half)
    ga_half = gav[:, :, cols].reshape(GROUP_ROWS, half)
    for z in range(4):
        value = mm_tn(obx[2 * z + me.yl], ga_half)
        value = jnp.where(c == 0, value[:HD], value[HD:pair]).astype(BF)
        for j in range(6):
            grad_o[z, j * HD : (j + 1) * HD] = value[:, j * TOK : (j + 1) * TOK]
        grad_o[z, 6 * HD :] = jnp.zeros_like(grad_o[z, 6 * HD :])
    send.finish()


def middle(lengths, ob, tok_all, cot_all, o_w, gu_w, down_w, gains, o):
    def like(*shape, dtype=BF):
        return jax.ShapeDtypeStruct(shape, dtype)

    def vmem(*shape, dtype=BF):
        return pltpu.VMEM(shape, dtype)

    width = o_w.shape[1]
    part = down_w.shape[0]
    outs = (
        like(NT, QROWS, 2 * TOK),
        like(NT, 1, QROWS, dtype=F32),
        like(TOK, width, dtype=F32),
        like(TOK, width, dtype=F32),
        like(NT, TOK, width),
        like(4, 4, 8 * HD, TOK),
        like(4, TOK, width),
        like(4, 6 * HD + 64, TOK),
        like(1, width, dtype=F32),
    )
    return pl.pallas_call(
        middle_kernel,
        out_shape=outs,
        in_specs=[SM, ANY, ANY, ANY, ANY, ANY, ANY, VM, VM],
        out_specs=(VM,) * len(outs),
        scratch_shapes=[
            vmem(NT, PACKED, TOK),
            vmem(NT, GROUP_ROWS, 2 * TOK),
            vmem(width + 2 * TOK - 2 * HD, width),
            vmem(width, 2 * part),
            vmem(part, width),
            vmem(NT, TOK, width),
            vmem(NT, TOK, width),
            vmem(GROUP_ROWS, width, dtype=F32),
            vmem(NT, TOK, width),
            vmem(NT, TOK, part),
            vmem(NT, TOK, 2 * part),
            vmem(4, TOK, width),
            vmem(4, TOK, width),
            vmem(4, TOK, width),
            vmem(4, TOK, width),
            vmem(2, TOK // 2, width),
            vmem(2, TOK, width),
            pltpu.SemaphoreType.DMA((40,)),
            pltpu.SemaphoreType.DMA((40,)),
            pltpu.SemaphoreType.DMA((8,)),
        ],
        compiler_params=pltpu.CompilerParams(
            collective_id=1, has_side_effects=True, vmem_limit_bytes=63 * 2**20
        ),
        name="middle",
    )(lengths, ob, tok_all, cot_all, o_w, gu_w, down_w, gains, o)


class RingSum:
    def __init__(self, send, along, block, buffers):
        self.send, self.along, self.block = send, along, block
        self.far, self.near, self.mid = buffers

    def begin(self):
        send, up, down = self.send, self.along(1), self.along(-1)
        self.far_up = send(halves(self.block(2), 0), self.far.at[0], up)
        self.far_down = send(halves(self.block(2), 1), self.far.at[1], down)
        self.last = [
            send(halves(self.block(1), 1), halves(self.near.at[0], 1), up),
            send(halves(self.block(3), 0), halves(self.near.at[1], 0), down),
        ]

    def middle(self):
        for i, (copy, k) in enumerate(((self.far_up, 1), (self.far_down, 3))):
            copy.wait_recv()
            value = halves(self.block(k), i)[...].astype(F32) + self.far[i].astype(F32)
            self.mid[i] = value.astype(BF)
            self.last.append(
                self.send(self.mid.at[i], halves(self.near.at[i], i), self.along(2 * i + 1))
            )

    def end(self):
        for copy in self.last:
            copy.wait_recv()
        total = self.block(0)[...].astype(F32) + self.near[0].astype(F32)
        return (total + self.near[1].astype(F32)).astype(BF)


class Exchange:
    def __init__(self, me, send, block, from_sib, slots):
        self.me, self.send, self.block, self.from_sib, self.slots = me, send, block, from_sib, slots
        self.first = send(block.at[:, 1 - me.c], from_sib, me.sibling())

    def second(self):
        me = self.me
        self.first.wait_recv()
        mine, theirs = me.t, me.rank(0, 1 - me.c)
        self.copies = []
        for k, yl in ((1, 1 - me.yl), (-1, 1 - me.yl), (2, me.yl)):
            for src, t in ((self.block.at[yl, me.c], mine), (self.from_sib.at[yl], theirs)):
                self.copies.append(self.send(src, self.slots.at[t], me.along_y(k)))
        self.slots[mine] = self.block[me.yl, me.c]
        self.slots[theirs] = self.from_sib[me.yl]

    def end(self):
        for copy in self.copies:
            copy.wait_recv()


def back_kernel(
    lengths, freq, kv, q_in, go_in, lse, delta, y_part, grad_gu, grad_down, grad_o, h1, tokv, qkv_w,
    gx2, x2_own, gains, gain2,
    layer_out, tokens_grad, all_gu, all_q, all_down, all_o,
    keyv, gkv, gq, staged, arrived, gqkv, starts,
    y_sib, y_mid, y_far, y_near, mine, tosib, sib, mid, far, near, grad_q,
    u_far, u_near, u_mid, d_far, d_near, d_mid, o_far, o_near, o_mid, q_far, q_near, q_mid,
    u_sum, d_sum, o_sum, q_sum,
    ux_far, ux_near, ux_mid, dx_far, dx_near, dx_mid, ox_far, ox_near, ox_mid, qx_far, qx_near, qx_mid,
    u_mine, q_mine, u_from, q_from,
    send_sem, recv_sem, local_sem,
):
    me = Place()
    me.greet(
        tuple(me.along_x(k) for k in (1, -1, 2))
        + (me.along_z(1), me.along_z(-1), me.along_y(2))
    )
    send = Copies(send_sem, recv_sem, local_sem)
    c, other = me.c, 1 - me.c
    rows = HD

    def over_z(ref, buffers):
        return RingSum(send, me.along_z, lambda k: ref.at[me.z_at(k)], buffers)

    down_z = over_z(grad_down, (d_far, d_near, d_mid))
    gu_z = over_z(grad_gu, (u_far, u_near, u_mid))
    out_z = over_z(grad_o, (o_far, o_near, o_mid))
    down_z.begin()
    gu_z.begin()
    out_z.begin()
    y_mine = lambda k, at: y_part[me.rank(k, c), at]
    ys = Scatter(me, send, y_mine, y_sib, y_mid, y_far, y_near)
    for k in (2, 1, 3, 0):
        ys.hand(k, y_part.at[me.rank(k, other)])

    for t in range(NT):
        starts[t], _ = starts_of(lengths, places_of(me, t, (1, TOK), 1))
    gq[...] = jnp.zeros_like(gq)
    lane = lax.broadcasted_iota(jnp.int32, (1, 2 * TOK), 1)
    lane_scale = jnp.where(lane < HD, LN2, 1.0)

    def source(k):
        x = me.x_at(k)
        keyv[...] = unpack(kv[x], GROUP_ROWS)
        gkv[...] = jnp.zeros_like(gkv)
        row = lax.broadcasted_iota(jnp.int32, (TOK, QROWS), 0)
        for t in range(NT):
            n = (t + 1) * TOK
            q, go = q_in[t], go_in[t]
            start = jnp.concatenate([starts[t]] * 2, axis=1)
            p = jnp.exp2(mm_nt(keyv[:n, :TOK], q) - lse[t])
            kept = []
            for b in range(t + 1):
                key = row + (b * CHUNK + x * TOK)
                keep = key >= start
                if b == t:
                    column = lax.broadcasted_iota(jnp.int32, (TOK, QROWS), 1)
                    keep = keep & (key <= lax.rem(column, TOK) + (t * CHUNK + me.x * TOK))
                kept.append(jnp.where(keep, p[b * TOK : (b + 1) * TOK], 0.0))
            p = jnp.concatenate(kept, axis=0) if t else kept[0]
            gp = mm_nt(keyv[:n], go)
            gs = (p * (gp - delta[t])).astype(BF)
            gkv[:n] += mm(p.astype(BF), go)
            gkv[:n, :TOK] += mm(gs, q)
            gq[t] += mm_tn(gs, keyv[:n, :TOK])

    def stage(n):
        value = (gkv[...] * lane_scale).astype(BF)
        staged[n, :GROUP_ROWS] = value[:, :TOK]
        tail = value[:, TOK : TOK + TOK // 2]
        staged[n, GROUP_ROWS:] = jnp.concatenate(
            [tail[: GROUP_ROWS // 2], tail[GROUP_ROWS // 2 :]], axis=1
        )

    source(2)
    stage(0)
    sums = [send(staged.at[0], arrived.at[0], me.along_x(2))]
    down_z.middle()
    ys.step2()
    ys.step1()

    @pl.loop(0, 2)
    def _(n):
        source(2 * n + 1)
        stage(n + 1)

    sums += [send(staged.at[n + 1], arrived.at[n + 1], me.along_x(2 * n + 1)) for n in range(2)]
    gu_z.middle()
    out_z.middle()
    ys.step3()
    ys.step0()
    d_sum[...] = down_z.end()
    quarter = d_sum.shape[0] // 4

    def quarters(ref, size, leading):
        def block(k):
            at = pl.ds(pl.multiple_of(me.x_at(k) * size, 16), size)
            return ref.at[:, at] if leading else ref.at[at]

        return block

    down_x = RingSum(send, me.along_x, quarters(d_sum, quarter, False), (dx_far, dx_near, dx_mid))
    down_x.begin()
    source(0)
    layer_out[...] = (x2_own[...] + ys.end()).astype(BF)
    total = gkv[...] * lane_scale
    for n in range(3):
        sums[n].wait_recv()
        total += unpack(arrived[n], GROUP_ROWS).astype(F32)
    gkv[...] = total

    for i in range(4):
        place = places_of(me, 2 * i, (QROWS, HD), 0)
        start, _ = starts_of(lengths, place)
        angle = (place - start).astype(F32) * freq[...]
        cosine, sine = jnp.cos(angle), -jnp.sin(angle)
        at = slice(i * QROWS, (i + 1) * QROWS)
        parts = []
        for h in range(2):
            of = slice(h * TOK, (h + 1) * TOK)
            g = jnp.concatenate([gq[2 * i, of, :HD], gq[2 * i + 1, of, :HD]], axis=0)
            parts.append(turn(g * SCALE, cosine, sine))
        parts.append(turn(gkv[at, :HD], cosine, sine))
        parts.append(gkv[at, HD : 2 * HD])
        gqkv[at] = jnp.concatenate(parts, axis=1).astype(BF)

    h_sums = Scatter(me, send, lambda k, at: mine[k, at], sib, mid, far, near)
    g1 = gains[0:1]
    gain1 = jnp.zeros_like(g1)

    def normed(x):
        x = x.astype(F32)
        r = lax.rsqrt(jnp.mean(x * x, axis=1, keepdims=True) + NORM_EPS)
        return x * r, r

    def feed(k):
        ranks = (me.rank(k, c), me.rank(k, other))
        g = [gqkv[pl.ds(pl.multiple_of(t * TOK, TOK), TOK)] for t in ranks]
        gh = mm_nt(jnp.concatenate(g, axis=0), qkv_w[...])
        low = gh.astype(BF)
        mine[k], tosib[k] = low[:TOK], low[TOK:]
        h_sums.hand(k, tosib.at[k])
        n1, _ = normed(jnp.concatenate([tokv[t] for t in ranks], axis=0))
        return jnp.sum(gh * n1, axis=0, keepdims=True)

    gain1 += feed(2)
    gain1 += feed(1)
    h_sums.step2()
    gain1 += feed(3)
    h_sums.step1()
    gain1 += feed(0)
    h_sums.step3()
    both = jnp.concatenate([gain1, gain2[...]], axis=0)
    both = jnp.concatenate([both, jnp.zeros((14, both.shape[1]), F32)], axis=0).astype(BF)

    span = 4 * rows
    for z in range(4):
        h = h1[:, :, z * span : (z + 1) * span].reshape(GROUP_ROWS, span)
        g = mm_tn(h, gqkv[...]).astype(BF)
        for n in range(4):
            for j in range(3):
                grad_q[z, n, j * rows : (j + 1) * rows] = g[
                    n * rows : (n + 1) * rows, j * TOK : (j + 1) * TOK
                ]
            at = z * span + n * rows
            extra = jnp.concatenate([both[:, at : at + rows], jnp.zeros((16, TOK - rows), BF)], axis=1)
            grad_q[z, n, 3 * rows :] = jnp.concatenate([extra, jnp.zeros_like(extra)], axis=0)
    q_z = over_z(grad_q, (q_far, q_near, q_mid))
    q_z.begin()
    h_sums.step0()

    u_sum[...] = gu_z.end()
    gu_x = RingSum(
        send, me.along_x, quarters(u_sum, u_sum.shape[1] // 4, True), (ux_far, ux_near, ux_mid)
    )
    gu_x.begin()
    o_sum[...] = out_z.end()
    out_x = RingSum(
        send, me.along_x, quarters(o_sum, o_sum.shape[0] // 4, False), (ox_far, ox_near, ox_mid)
    )
    out_x.begin()
    down_x.middle()
    out_x.middle()
    gu_x.middle()
    all_down[me.x, me.yh] = down_x.end()
    down_y = send(all_down.at[me.x, me.yh], all_down.at[me.x, me.yh], me.along_y(2))
    all_o[me.x, me.yh] = out_x.end()
    out_y = send(all_o.at[me.x, me.yh], all_o.at[me.x, me.yh], me.along_y(2))
    u_mine[...] = gu_x.end().reshape(u_mine.shape)
    u_rows = Exchange(me, send, u_mine, u_from, all_gu.at[me.x])
    q_z.middle()
    gh1 = h_sums.end()
    n1, r1 = normed(tokv[me.t])
    gn = gh1 * g1
    gx = gx2[...] + r1 * (gn - n1 * jnp.mean(gn * n1, axis=1, keepdims=True))
    tokens_grad[...] = gx.astype(BF)
    u_rows.second()

    def over_x(ref):
        return Gather(send, me.along_x, lambda k: ref.at[me.x_at(k)], halves)

    down_y.wait_recv()
    down_all = over_x(all_down)
    out_y.wait_recv()
    out_all = over_x(all_o)
    q_sum[...] = q_z.end()
    q_x = RingSum(
        send, me.along_x, quarters(q_sum, q_sum.shape[1] // 4, True), (qx_far, qx_near, qx_mid)
    )
    q_x.begin()
    u_rows.end()
    gu_all = over_x(all_gu)
    q_x.middle()
    q_mine[...] = q_x.end().reshape(q_mine.shape)
    q_rows = Exchange(me, send, q_mine, q_from, all_q.at[me.x])
    down_all.forward()
    out_all.forward()
    q_rows.second()
    gu_all.forward()
    q_rows.end()
    q_all = over_x(all_q)
    q_all.forward()
    send.finish()


def back(*args):
    lengths = args[0]
    grad_gu, grad_down, grad_o, qkv_w = args[7], args[8], args[9], args[12]
    freq = jnp.asarray(np.tile(frequency_table(HD), 2)[None])
    width = qkv_w.shape[0]
    u_rows, o_rows = grad_gu.shape[2], grad_o.shape[1]
    q_rows = 3 * HD + 32

    def like(*shape, dtype=BF):
        return jax.ShapeDtypeStruct(shape, dtype)

    def vmem(*shape, dtype=BF):
        return pltpu.VMEM(shape, dtype)

    def ring(*shape):
        half = (shape[0] // 2,) + shape[1:]
        return [vmem(2, *half), vmem(2, *shape), vmem(2, *half)]

    def group(mine):
        head = [vmem(4, TOK, width)] * (4 if mine else 2)
        return head + [vmem(2, TOK // 2, width), vmem(2, TOK, width)]

    outs = (
        like(TOK, width),
        like(TOK, width),
        like(4, NT, u_rows // 4, TOK),
        like(4, NT, q_rows // 4, TOK),
        like(4, 2, TOK // 4, width),
        like(4, 2, o_rows // 4, TOK),
    )
    return pl.pallas_call(
        back_kernel,
        out_shape=outs,
        in_specs=[SM] + [VM] * (len(args)),
        out_specs=(VM,) * len(outs),
        scratch_shapes=[
            vmem(GROUP_ROWS, 2 * TOK),
            vmem(GROUP_ROWS, 2 * TOK, dtype=F32),
            vmem(NT, QROWS, TOK, dtype=F32),
            vmem(3, PACKED, TOK),
            vmem(3, PACKED, TOK),
            vmem(GROUP_ROWS, 4 * HD),
            vmem(NT, 1, TOK, dtype=jnp.int32),
            *group(False),
            *group(True),
            vmem(4, 4, q_rows, TOK),
            *ring(4, u_rows, TOK),
            *ring(TOK, width),
            *ring(o_rows, TOK),
            *ring(4, q_rows, TOK),
            vmem(4, u_rows, TOK),
            vmem(TOK, width),
            vmem(o_rows, TOK),
            vmem(4, q_rows, TOK),
            *ring(4, u_rows // 4, TOK),
            *ring(TOK // 4, width),
            *ring(o_rows // 4, TOK),
            *ring(4, q_rows // 4, TOK),
            vmem(2, 2, u_rows // 4, TOK),
            vmem(2, 2, q_rows // 4, TOK),
            vmem(2, u_rows // 4, TOK),
            vmem(2, q_rows // 4, TOK),
            pltpu.SemaphoreType.DMA((112,)),
            pltpu.SemaphoreType.DMA((112,)),
            pltpu.SemaphoreType.DMA((4,)),
        ],
        compiler_params=pltpu.CompilerParams(
            collective_id=2, has_side_effects=True, vmem_limit_bytes=63 * 2**20
        ),
        name="back",
    )(lengths, freq, *args[1:])


def finish_kernel(
    layer_out, tokens_grad, all_gu, all_q, all_down, all_o,
    layer_to, tokens_to, to_q, to_k, to_v, to_o, to_gate, to_up, to_down, to_gain,
):
    layer_to[0], tokens_to[0] = layer_out[...], tokens_grad[...]
    for t in range(NT):
        for j in range(8):
            tile = all_gu[j // 2, t, (j % 2) * HD : (j % 2 + 1) * HD].astype(F32)
            at = (j % 4) * 2 * CHUNK + t * TOK
            if j < 4:
                to_gate[:, at : at + TOK] = tile
            else:
                to_up[:, at : at + TOK] = tile
    gains = jnp.zeros((2, TOK), F32)
    heads = []
    for t in range(NT):
        value = jnp.concatenate([all_q[x, t] for x in range(4)], axis=0).astype(F32)
        tiles = [value[j * HD : (j + 1) * HD] for j in range(3)]
        heads.append(jnp.concatenate(tiles, axis=1))
        gains += value[3 * HD : 3 * HD + 2]
    to_gain[...] = gains
    to_q[...] = jnp.concatenate([h[:, : 2 * HD] for h in heads], axis=1)
    to_k[...] = jnp.concatenate([h[:, 2 * HD : 3 * HD] for h in heads], axis=1)
    to_v[...] = jnp.concatenate([h[:, 3 * HD :] for h in heads], axis=1)
    for yh in range(2):
        value = jnp.concatenate([all_o[x, yh] for x in range(4)], axis=0).astype(F32)
        for j in range(6):
            at = (yh * 6 + j) * TOK
            to_o[:, at : at + TOK] = value[j * HD : (j + 1) * HD]
        for x in range(4):
            size = all_down.shape[2]
            at = yh * TOK + x * size
            to_down[at : at + size] = all_down[x, yh].astype(F32)


def finish(layer_out, tokens_grad, all_gu, all_q, all_down, all_o):
    rows, width = layer_out.shape
    part = all_gu.shape[2] * 4 // HD * TOK // 2
    shapes = [
        ((1, rows, width), BF),
        ((1, rows, width), BF),
        ((HD, width), F32),
        ((HD, width // 2), F32),
        ((HD, width // 2), F32),
        ((HD, width), F32),
        ((HD, NT * part), F32),
        ((HD, NT * part), F32),
        ((2 * TOK, width), F32),
        ((2, TOK), F32),
    ]
    return pl.pallas_call(
        finish_kernel,
        out_shape=tuple(jax.ShapeDtypeStruct(*s) for s in shapes),
        in_specs=[VM] * 6,
        out_specs=(VM,) * len(shapes),
        compiler_params=pltpu.CompilerParams(vmem_limit_bytes=40 * 2**20),
        name="finish",
    )(layer_out, tokens_grad, all_gu, all_q, all_down, all_o)


def body(
    tokens,
    doc_lengths,
    w_query,
    w_key,
    w_value,
    w_output,
    w_gate,
    w_up,
    w_down,
    gain_attn,
    gain_mlp,
    cotangent,
):
    width = tokens.shape[2]
    part = w_gate.shape[1] // NT
    tok_all, cot_all, h1, gu_w, o_w, down_w, kv, q, o, lse, ob, gains, qkv_w = front(
        doc_lengths,
        tokens[0],
        cotangent[0],
        w_query,
        w_key,
        w_value,
        w_gate,
        w_up,
        w_output,
        w_down,
        gain_attn.reshape(1, -1),
        gain_mlp.reshape(1, -1),
    )
    go, delta, gx2, own, y_part, grad_gu, grad_down, grad_o, gain2 = middle(
        doc_lengths,
        ob,
        tok_all,
        cot_all,
        o_w.reshape(width, width),
        gu_w.reshape(width, 2 * part),
        down_w.reshape(part, width),
        gains,
        o,
    )
    sums = back(
        doc_lengths, kv, q, go, lse, delta, y_part, grad_gu, grad_down, grad_o, h1, tok_all, qkv_w,
        gx2, own, gains, gain2,
    )
    *most, to_gain = finish(*sums)
    layer_out, tokens_grad, grad_q, grad_k, grad_v, grad_out, grad_gate, grad_up, grad_dn = most
    return (
        layer_out,
        tokens_grad,
        grad_q,
        grad_k,
        grad_v,
        grad_out,
        grad_gate,
        grad_up,
        grad_dn,
        to_gain[0, :HD],
        to_gain[1, :HD],
    )


def solution(mesh):
    fine = Mesh(mesh.devices.reshape(4, 2, 2, 2, 4), AXES)
    by_token = P("z", ("yl", "c", "yh", "x"), None)
    by_row = P(("z", "yl", "c"), None)
    by_feature = P(("z", "yl", "c"))
    return jax.shard_map(
        body,
        mesh=fine,
        in_specs=(by_token, P("z", None))
        + (by_row,) * 7
        + (by_feature, by_feature, by_token),
        out_specs=(by_token, by_token) + (by_row,) * 7 + (by_feature, by_feature),
        check_vma=False,
    )
```

```python
import jax
import jax.numpy as jnp
import numpy as np
from jax import lax
from jax.experimental import pallas as pl
from jax.experimental.pallas import tpu as pltpu
from jax.sharding import Mesh
from jax.sharding import PartitionSpec as P

HEADS = 16
KV = 8
HD = 96
NORM_EPS = 1e-05
LOG2E = 1.4426950408889634
LN2 = 0.6931471805599453
SCALE = HD ** (-0.5)
BF = jnp.bfloat16
F32 = jnp.float32
AXES = ("z", "yl", "c", "yh", "x")
GROUP = ("yl", "c", "yh")
MESH = pl.DeviceIdType.MESH
TOK = 128
NT = 8
NX = 4


def frequency_table(head_width):
    halfway = head_width // 2
    base_freq = 500000.0 ** (-np.arange(halfway) * 2.0 / head_width)
    wavelength = 2.0 * np.pi / base_freq
    smooth = (8192.0 / wavelength - 1.0) / 3.0
    middle = (1.0 - smooth) * base_freq / 32.0 + smooth * base_freq
    freq_table = np.where(
        wavelength > 8192.0, base_freq / 32.0, np.where(wavelength < 2048.0, base_freq, middle)
    )
    return freq_table.astype(np.float32)


def mm(a, b):
    return jnp.dot(a, b, preferred_element_type=F32)


def mm_nt(a, b):
    return lax.dot_general(a, b, (((1,), (1,)), ((), ())), preferred_element_type=F32)


def mm_tn(a, b):
    return lax.dot_general(a, b, (((0,), (0,)), ((), ())), preferred_element_type=F32)


class Place:
    def __init__(self):
        self.z, self.x = lax.axis_index("z"), lax.axis_index("x")
        self.yl, self.c, self.yh = (lax.axis_index(name) for name in GROUP)
        self.y = self.yh * 2 + self.yl
        self.t = self.rank(0, self.c)

    def rank(self, k, c):
        y = lax.rem(self.y + (k + 4), 4)
        return lax.rem(y, 2) * 4 + c * 2 + y // 2

    def y_at(self, k):
        return lax.rem(self.y + (k + 4), 4)

    def along_y(self, k):
        y = self.y_at(k)
        return {"yh": y // 2, "yl": lax.rem(y, 2)}

    def x_at(self, k):
        return lax.rem(self.x + (k + 4), 4)

    def z_at(self, k):
        return lax.rem(self.z + (k + 4), 4)

    def along_x(self, k):
        return {"x": self.x_at(k)}

    def along_z(self, k):
        return {"z": self.z_at(k)}

    def sibling(self):
        return {"c": 1 - self.c}

    def greet(self, others=()):
        barrier = pltpu.get_barrier_semaphore()
        everyone = (self.along_y(1), self.along_y(-1), self.sibling()) + tuple(others)
        for who in everyone:
            pl.semaphore_signal(barrier, inc=1, device_id=who, device_id_type=MESH)
        pl.semaphore_wait(barrier, len(everyone))


class Kept:
    def __init__(self, copy):
        self.copy, self.done = copy, False

    def wait(self):
        if not self.done:
            self.copy.wait()
        self.done = True


class Sent:
    def __init__(self, copy):
        self.copy, self.arrived = copy, False

    def wait_recv(self):
        if not self.arrived:
            self.copy.wait_recv()
        self.arrived = True

    def wait_send(self):
        self.copy.wait_send()


class Copies:
    def __init__(self, send_sem, recv_sem, local_sem=None):
        self.send_sem, self.recv_sem, self.local_sem = send_sem, recv_sem, local_sem
        self.all, self.locals = [], []

    def __call__(self, src, dst, who):
        i = len(self.all)
        assert i < self.send_sem.shape[0]
        copy = pltpu.make_async_remote_copy(
            src_ref=src,
            dst_ref=dst,
            send_sem=self.send_sem.at[i],
            recv_sem=self.recv_sem.at[i],
            device_id=who,
            device_id_type=MESH,
        )
        copy.start()
        sent = Sent(copy)
        self.all.append(sent)
        return sent

    def local(self, src, dst):
        assert len(self.locals) < self.local_sem.shape[0]
        copy = pltpu.make_async_copy(src, dst, self.local_sem.at[len(self.locals)])
        copy.start()
        kept = Kept(copy)
        self.locals.append(kept)
        return kept

    def finish(self):
        for kept in self.locals:
            kept.wait()
        for sent in self.all:
            sent.wait_recv()
        for sent in self.all:
            sent.wait_send()


class Gather:
    def __init__(self, send, along, slot, cut, src=None):
        self.send, self.along, self.slot, self.cut = send, along, slot, cut
        src = slot(0) if src is None else src
        to = slot(0)
        self.first = [send(cut(src, i), cut(to, i), along(1 - 2 * i)) for i in range(2)]
        self.second = [send(cut(src, 1 - i), cut(to, 1 - i), along(1 - 2 * i)) for i in range(2)]

    def forward(self):
        self.far = []
        for i in range(2):
            self.first[i].wait_recv()
            part = self.cut(self.slot(2 * i - 1), i)
            self.far.append(self.send(part, part, self.along(1 - 2 * i)))
        for copy in self.second:
            copy.wait_recv()

    def end(self):
        for copy in self.far:
            copy.wait_recv()


class Neighbours:
    def __init__(self, send, along, src, slot):
        self.up = send(src, slot(0), along(1))
        self.down = send(src, slot(0), along(-1))


class Relay:
    def __init__(self, send, along, take, slot, cut):
        self.up = send(cut(take(-1), 0), cut(slot(-1), 0), along(1))
        self.down = send(cut(take(1), 1), cut(slot(1), 1), along(-1))

    def end(self):
        self.up.wait_recv()
        self.down.wait_recv()


def halves(ref, i):
    half = ref.shape[0] // 2
    return ref.at[pl.ds(i * half, half)]


ANY = pl.BlockSpec(memory_space=pl.ANY)
VM = pl.BlockSpec(memory_space=pltpu.VMEM)
SM = pl.BlockSpec(memory_space=pltpu.SMEM)
GROUP_ROWS = NT * TOK
QROWS = 2 * TOK
CHUNK = NX * TOK
PACKED = GROUP_ROWS + GROUP_ROWS // 2


def starts_of(lengths_ref, place):
    end, start = 0, jnp.zeros_like(place)
    for i in range(lengths_ref.shape[1]):
        end = end + lengths_ref[0, i]
        start = jnp.maximum(start, jnp.where(place >= end, end, 0))
    return start, end


def places_of(me, tile, shape, axis):
    row = lax.broadcasted_iota(jnp.int32, shape, axis)
    return (tile + row // TOK) * CHUNK + me.x * TOK + lax.rem(row, TOK)


def turn(v, cosine, sine):
    half = HD // 2
    return v * cosine + jnp.concatenate([-v[:, half:], v[:, :half]], axis=1) * sine


def unpack(packed, n):
    low, high = packed[n:, : TOK // 2], packed[n:, TOK // 2 :]
    tail = jnp.concatenate([low, high], axis=0)
    return jnp.concatenate([packed[:n], tail, jnp.zeros_like(tail)], axis=1)


def front_kernel(
    lengths, freq, tok, cot, wq, wk, wv, wg, wu, wo, wd, gain1, gain2,
    tok_all, cot_all, h1_out, gu_w, o_w, down_w, kv_out, q_out, o_out, lse_out, ob_out, gains_out, qkv_w,
    tokv, h1, slices_q, slices_u, tmp_q, tmp_u, gq, kv, keyv, starts, top, total, acc, w_kv, w_q, down_v,
    send_sem, recv_sem, local_sem,
):
    me = Place()
    me.greet((me.along_x(1), me.along_x(-1), me.along_z(1), me.along_z(-1)))
    send = Copies(send_sem, recv_sem, local_sem)
    c, other = me.c, 1 - me.c
    step = 1 - 2 * c
    slot, slot_other = me.yl * 2 + c, me.yl * 2 + other
    toward, away = me.along_y(step), me.along_y(-step)
    t_toward, t_relay, t_sib = me.rank(step, c), me.rank(step, other), me.rank(0, other)
    rows, width = wq.shape

    quarter = TOK // 4
    down_rows = lambda k: pl.ds(pl.multiple_of(me.x_at(k) * quarter, quarter), quarter)
    down_src = wd.at[pl.ds(pl.multiple_of(me.yh * TOK + me.x * quarter, quarter), quarter)]
    own_down = send.local(down_src, down_v)
    down_z = Gather(send, me.along_z, lambda k: down_w.at[me.z_at(k), down_rows(0)], halves, down_src)

    slices_q[:, rows:, :] = jnp.zeros_like(slices_q[:, rows:, :])
    for t in range(NT):
        slices_q[t, :rows] = jnp.concatenate(
            [
                wq[:, 2 * HD * t : 2 * HD * (t + 1)],
                wk[:, HD * t : HD * (t + 1)],
                wv[:, HD * t : HD * (t + 1)],
            ],
            axis=1,
        )
        slices_q[t, rows : rows + 1, :rows] = gain1[...]
        slices_q[t, rows + 1 : rows + 2, :rows] = gain2[...]
    relay_q = send(slices_q.at[t_relay], tmp_q, me.sibling())
    arrived_q = [
        send(slices_q.at[t_sib], gq.at[me.z, slot], me.sibling()),
        send(slices_q.at[t_toward], gq.at[me.z, slot], toward),
    ]
    own_q = send.local(slices_q.at[me.t], gq.at[me.z, slot])
    relay_q.wait_recv()
    arrived_q.append(send(tmp_q, gq.at[me.z, slot_other], away))
    own_tok = send.local(tok, tokv.at[me.t])
    down_z.forward()
    own_down.wait()
    own_down = send.local(down_v, down_w.at[me.z, down_rows(0)])

    part = wg.shape[1] // NT
    for t in range(NT):
        for n in range(4):
            at = n * 2 * CHUNK + t * TOK
            slices_u[t, :, n * TOK : (n + 1) * TOK] = wg[:, at : at + TOK]
            slices_u[t, :, part + n * TOK : part + (n + 1) * TOK] = wu[:, at : at + TOK]

    for t in range(NT):
        place = places_of(me, t, (TOK, TOK), 0)
        starts[t], _ = starts_of(lengths, place)

    own_q.wait()
    for copy in arrived_q:
        copy.wait_recv()
    qkv_z = Gather(send, me.along_z, lambda k: gq.at[me.z_at(k)], halves)
    tokens = Gather(send, me.along_y, lambda k: tokv.at[me.rank(k, c)], halves, tok)
    tok_sib = [send(tok, tokv.at[me.t], me.sibling())]
    own_down.wait()
    down_z.end()
    down_spread = lambda k: down_w.at[:, down_rows(k)]
    down_x = Gather(send, me.along_x, down_spread, halves)
    arrived_o = send(wo, o_w.at[me.z, me.yl, c], toward)
    own_o = send.local(wo, o_w.at[me.z, me.yl, c])
    qkv_z.forward()
    tokens.forward()
    tok_sib += [
        send(tokv.at[me.rank(k, c)], tokv.at[me.rank(k, c)], me.sibling()) for k in (-1, 1)
    ]
    relay_u = send(slices_u.at[t_relay], tmp_u, me.sibling())
    arrived_u = [
        send(slices_u.at[t_sib], gu_w.at[me.z, slot], me.sibling()),
        send(slices_u.at[t_toward], gu_w.at[me.z, slot], toward),
    ]
    own_u = send.local(slices_u.at[me.t], gu_w.at[me.z, slot])
    relay_u.wait_recv()
    arrived_u.append(send(tmp_u, gu_w.at[me.z, slot_other], away))
    third = CHUNK * 3 // 4
    columns = lambda k: pl.ds(pl.multiple_of(me.x_at(k) * third, TOK), third)
    own_o.wait()
    arrived_o.wait_recv()
    o_z = Gather(send, me.along_z, lambda k: o_w.at[me.z_at(k), :, c, :, columns(0)], halves)
    tokens.end()
    far = tokv.at[me.rank(2, c)]
    tok_sib.append(send(far, far, me.sibling()))
    qkv_z.end()
    own_tok.wait()
    for copy in tok_sib:
        copy.wait_recv()
    send.local(tokv, tok_all)
    o_z.forward()

    down_x.forward()

    gains = [
        jnp.concatenate(
            [gq[z, n, rows + g : rows + g + 1, :rows] for z in range(4) for n in range(4)], axis=1
        ).astype(F32)
        for g in range(2)
    ]
    gains_out[...] = jnp.concatenate(gains, axis=0)
    for z in range(4):
        for n in range(4):
            at = (z * 4 + n) * rows
            w = gq[z, n, :rows]
            qkv_w[at : at + rows] = w
            w_q[at : at + rows] = w[:, : 2 * HD]
            w_kv[at : at + rows] = w[:, 2 * HD :]
    tails, turns = [], []
    for i in range(4):
        place = places_of(me, 2 * i, (QROWS, HD), 0)
        start, _ = starts_of(lengths, place)
        angle = (place - start).astype(F32) * freq[...]
        cosine, sine = jnp.cos(angle), jnp.sin(angle)
        x = jnp.concatenate([tokv[2 * i], tokv[2 * i + 1]], axis=0).astype(F32)
        h = x * lax.rsqrt(jnp.mean(x * x, axis=1, keepdims=True) + NORM_EPS)
        h = (h * gains[0]).astype(BF)
        h1[2 * i], h1[2 * i + 1] = h[:TOK], h[TOK:]
        pair = mm(h, w_kv[...])
        k = turn(pair[:, :HD], cosine, sine)
        kv[me.x, i * QROWS : (i + 1) * QROWS] = jnp.concatenate(
            [k, pair[:, HD:TOK]], axis=1
        ).astype(BF)
        tails.append(pair[:, TOK:].astype(BF))
        turns.append((cosine, sine))
    for i in range(2):
        at = GROUP_ROWS + i * QROWS
        kv[me.x, at : at + QROWS] = jnp.concatenate([tails[i], tails[i + 2]], axis=1)
    kvs = Gather(send, me.along_x, lambda k: kv.at[me.x_at(k)], halves)
    send.local(h1, h1_out)
    own_u.wait()
    for copy in arrived_u:
        copy.wait_recv()
    Neighbours(send, me.along_z, gu_w.at[me.z], lambda k: gu_w.at[me.z_at(k)])
    cots = Gather(send, me.along_y, lambda k: cot_all.at[me.rank(k, c)], halves, cot)
    send(cot, cot_all.at[me.t], me.sibling())
    blank = jnp.zeros((QROWS, TOK - HD), BF)
    for i in range(4):
        h = jnp.concatenate([h1[2 * i], h1[2 * i + 1]], axis=0)
        both = mm(h, w_q[...])
        for n in range(2):
            q = turn(both[:, n * HD : (n + 1) * HD], *turns[i]) * (SCALE * LOG2E)
            q = jnp.concatenate([q.astype(BF), blank], axis=1)
            q_out[2 * i, n * TOK : (n + 1) * TOK] = q[:TOK]
            q_out[2 * i + 1, n * TOK : (n + 1) * TOK] = q[TOK:]

    top[...] = jnp.full_like(top, -1e30)
    total[...] = jnp.zeros_like(total)
    acc[...] = jnp.zeros_like(acc)

    def source(s):
        x = lax.rem(me.x + s + s // 2 - 2 * (s // 3), 4)
        keyv[...] = unpack(kv[x], GROUP_ROWS)
        lane = lax.broadcasted_iota(jnp.int32, (QROWS, TOK), 1)
        for t in range(NT):
            n = (t + 1) * TOK
            q = q_out[t]
            score = mm_nt(q, keyv[:n, :TOK])
            start = jnp.concatenate([starts[t]] * 2, axis=0)
            kept = []
            for b in range(t + 1):
                key = lane + (b * CHUNK + x * TOK)
                keep = key >= start
                if b == t:
                    row = lax.broadcasted_iota(jnp.int32, (QROWS, TOK), 0)
                    keep = keep & (key <= lax.rem(row, TOK) + (t * CHUNK + me.x * TOK))
                kept.append(jnp.where(keep, score[:, b * TOK : (b + 1) * TOK], -jnp.inf))
            score = jnp.concatenate(kept, axis=1) if t else kept[0]
            old = top[t]
            new = jnp.maximum(old, jnp.max(score, axis=1, keepdims=True))
            p = jnp.exp2(score - new)
            factor = jnp.exp2(old - new)
            top[t] = new
            total[t] = total[t] * factor + jnp.sum(p, axis=1, keepdims=True)
            acc[t] = acc[t] * factor + mm(p.astype(BF), keyv[:n])

    source(0)
    kvs.forward()
    o_z.end()
    spread = lambda k: o_w.at[:, :, c, :, columns(k)]
    Neighbours(send, me.along_x, spread(0), spread)
    pl.loop(1, 3)(source)
    cots.forward()
    for k in (-1, 1):
        send(cot_all.at[me.rank(k, c)], cot_all.at[me.rank(k, c)], me.sibling())
    kvs.end()
    source(3)
    send.local(kv, kv_out)
    for t in range(NT):
        o = acc[t][:, HD : 2 * HD] / total[t]
        lse = top[t] + jnp.log2(total[t])
        o_out[t] = o
        lse_out[t] = jnp.transpose(jnp.broadcast_to(lse, (QROWS, TOK)))[:1]
        place = places_of(me, t, (TOK, 2 * HD), 0)
        _, end = starts_of(lengths, place)
        ob = jnp.concatenate([o[:TOK], o[TOK:]], axis=1)
        ob = jnp.where(place < end, ob, 0.0).astype(BF)
        tail = ob[:, TOK:]
        ob_out[t, :TOK] = ob[:, :TOK]
        ob_out[t, TOK:] = jnp.concatenate([tail[: TOK // 2], tail[TOK // 2 :]], axis=1)
    cots.end()
    far = cot_all.at[me.rank(2, c)]
    send(far, far, me.sibling())
    send.finish()


def front(lengths, tok, cot, wq, wk, wv, wg, wu, wo, wd, gain1, gain2):
    def like(*shape, dtype=BF):
        return jax.ShapeDtypeStruct(shape, dtype)

    rows, width = wq.shape
    part = wg.shape[1] // NT
    freq = jnp.asarray(np.tile(frequency_table(HD), 2)[None])
    outs = (
        (like(NT, TOK, width), ANY),
        (like(NT, TOK, width), ANY),
        (like(NT, TOK, width), ANY),
        (like(4, 4, rows, 2 * part), ANY),
        (like(4, 2, 2, rows, width), ANY),
        (like(4, TOK, width), ANY),
        (like(NX, PACKED, TOK), ANY),
        (like(NT, QROWS, TOK), VM),
        (like(NT, QROWS, HD, dtype=F32), VM),
        (like(NT, 1, QROWS, dtype=F32), VM),
        (like(NT, TOK * 3 // 2, TOK), VM),
        (like(2, width, dtype=F32), VM),
        (like(width, 4 * HD), VM),
    )
    padded = rows + 16
    return pl.pallas_call(
        front_kernel,
        out_shape=tuple(o[0] for o in outs),
        in_specs=[SM, VM, ANY, ANY, VM, VM, VM, VM, VM, VM, ANY, VM, VM],
        out_specs=tuple(o[1] for o in outs),
        scratch_shapes=[
            pltpu.VMEM((NT, TOK, width), BF),
            pltpu.VMEM((NT, TOK, width), BF),
            pltpu.VMEM((NT, padded, 4 * HD), BF),
            pltpu.VMEM((NT, rows, 2 * part), BF),
            pltpu.VMEM((padded, 4 * HD), BF),
            pltpu.VMEM((rows, 2 * part), BF),
            pltpu.VMEM((4, 4, padded, 4 * HD), BF),
            pltpu.VMEM((NX, PACKED, TOK), BF),
            pltpu.VMEM((GROUP_ROWS, 2 * TOK), BF),
            pltpu.VMEM((NT, TOK, TOK), jnp.int32),
            pltpu.VMEM((NT, QROWS, 1), F32),
            pltpu.VMEM((NT, QROWS, 1), F32),
            pltpu.VMEM((NT, QROWS, 2 * TOK), F32),
            pltpu.VMEM((width, 2 * HD), BF),
            pltpu.VMEM((width, 2 * HD), BF),
            pltpu.VMEM((TOK // 4, width), BF),
            pltpu.SemaphoreType.DMA((80,)),
            pltpu.SemaphoreType.DMA((80,)),
            pltpu.SemaphoreType.DMA((16,)),
        ],
        compiler_params=pltpu.CompilerParams(
            collective_id=0, has_side_effects=True, vmem_limit_bytes=56 * 2**20
        ),
        name="front",
    )(lengths, freq, tok, cot, wq, wk, wv, wg, wu, wo, wd, gain1, gain2)


class Scatter:
    def __init__(self, me, send, mine, sib, mid, far, near):
        self.me, self.send, self.mine, self.sib, self.mid = me, send, mine, sib, mid
        self.far, self.near, self.from_sib = far, near, {}
        self.half = sib.shape[1] // 2

    def hand(self, k, src):
        self.from_sib[k] = self.send(src, self.sib.at[k], self.me.sibling())

    def pair(self, k, i):
        rows = slice(i * self.half, (i + 1) * self.half)
        return self.mine(k, rows).astype(F32) + self.sib[k, rows].astype(F32)

    def put(self, k, i, value):
        self.mid[k, i * self.half : (i + 1) * self.half] = value.astype(BF)
        return self.mid.at[k, pl.ds(i * self.half, self.half)]

    def step2(self):
        self.from_sib[2].wait_recv()
        up, down = self.me.along_y(1), self.me.along_y(-1)
        self.far_up = self.send(self.put(2, 0, self.pair(2, 0)), self.far.at[0], up)
        self.far_down = self.send(self.put(2, 1, self.pair(2, 1)), self.far.at[1], down)

    def step1(self):
        self.from_sib[1].wait_recv()
        src = self.put(1, 1, self.pair(1, 1))
        self.last = [self.send(src, halves(self.near.at[0], 1), self.me.along_y(1))]

    def step3(self):
        self.from_sib[3].wait_recv()
        src = self.put(3, 0, self.pair(3, 0))
        self.last.append(self.send(src, halves(self.near.at[1], 0), self.me.along_y(-1)))

    def step0(self):
        self.far_up.wait_recv()
        src = self.put(1, 0, self.pair(1, 0) + self.far[0].astype(F32))
        self.last.append(self.send(src, halves(self.near.at[0], 0), self.me.along_y(1)))
        self.far_down.wait_recv()
        src = self.put(3, 1, self.pair(3, 1) + self.far[1].astype(F32))
        self.last.append(self.send(src, halves(self.near.at[1], 1), self.me.along_y(-1)))

    def end(self):
        self.from_sib[0].wait_recv()
        for copy in self.last:
            copy.wait_recv()
        total = self.mine(0, slice(None)).astype(F32) + self.sib[0].astype(F32)
        return total + self.near[0].astype(F32) + self.near[1].astype(F32)


class RingSum:
    def __init__(self, send, along, block, buffers):
        self.send, self.along, self.block = send, along, block
        self.far, self.direct, self.summed, self.mid = buffers

    def begin(self):
        self.begin_far()
        self.begin_near()

    def begin_far(self):
        send, up, down = self.send, self.along(1), self.along(-1)
        self.first = [
            send(halves(self.block(2), 0), self.far.at[0], up),
            send(halves(self.block(2), 1), self.far.at[1], down),
        ]

    def begin_near(self):
        send, up, down = self.send, self.along(1), self.along(-1)
        self.near = [
            send(halves(self.block(1), 1), self.direct.at[0], up),
            send(halves(self.block(3), 0), self.direct.at[1], down),
        ]

    def middle(self):
        self.last = []
        for i, k in enumerate((1, 3)):
            self.first[i].wait_recv()
            value = halves(self.block(k), i)[...].astype(F32) + self.far[i].astype(F32)
            self.mid[i] = value.astype(BF)
            self.last.append(
                self.send(self.mid.at[i], self.summed.at[i], self.along(2 * i + 1))
            )

    def end(self, to):
        for i in range(2):
            self.near[1 - i].wait_recv()
            self.last[i].wait_recv()
            value = halves(self.block(0), i)[...].astype(F32) + self.direct[1 - i].astype(F32)
            halves(to, i)[...] = (value + self.summed[i].astype(F32)).astype(BF)


def middle_kernel(
    lengths, ob, tok_all, cot_all, cot, o_w, gu_w, down_w, gains, o_in,
    go_out, delta_out, gx2_out, x2_out, y_out, u_out, d_sum, grad_o, gain_out,
    obv, obx, ow, guw, dw, cotv, tokv, h2, hid, ggu, ghs, mine, tosib, sib, mid, far, near, y_buf,
    grad_gu, grad_down, d_far, d_direct, d_summed, d_mid, o_buf,
    send_sem, recv_sem, local_sem,
):
    me = Place()
    me.greet(
        tuple(me.along_x(k) for k in (1, -1))
        + (me.along_z(1), me.along_z(-1), me.along_y(2))
    )
    send = Copies(send_sem, recv_sem, local_sem)
    c, other = me.c, 1 - me.c
    width = gains.shape[1]
    part = hid.shape[2]
    third = width // 4
    half = width // 2

    order = (2, 1, -1, 0)
    arrivals = []

    def tokens_of(ref, k):
        y = me.y_at(k)
        return ref.at[lax.rem(y, 2), :, y // 2]

    def send_tokens(i):
        arrivals.append(
            [
                send(
                    tokens_of(ob, d + order[i]), tokens_of(obv.at[me.t], d + order[i]), me.along_y(d)
                )
                for d in (1, -1, 2)
            ]
        )

    send_tokens(0)
    own_sib = send(ob, obv.at[me.t], me.sibling())
    own_ob = send.local(ob, obv.at[me.t])
    columns = lambda k: pl.ds(pl.multiple_of(me.x_at(k) * third, TOK), third)
    spread = lambda ref, k: ref.at[:, :, c, :, columns(k)]
    o_far = Relay(send, me.along_x, lambda k: spread(o_w, k), lambda k: spread(ow, k), halves)
    o_sib = [send(spread(o_w, k), spread(ow, k), me.sibling()) for k in (0, 1, -1)]
    loads = [send.local(tok_all, tokv)]
    loads += [send.local(spread(o_w, k), spread(ow, k)) for k in (0, 1, -1)]
    gu_far = Relay(
        send, me.along_z, lambda k: gu_w.at[me.z_at(k)], lambda k: guw.at[me.z_at(k)], halves
    )
    quarter = TOK // 4

    def down_spread(ref, k):
        return ref.at[:, pl.ds(pl.multiple_of(me.x_at(k) * quarter, quarter), quarter)]

    send_tokens(1)
    loads += [send.local(gu_w.at[me.z_at(k)], guw.at[me.z_at(k)]) for k in (0, 1, -1)]
    late = [send.local(down_w, dw)]
    late.append(send.local(cot, cotv.at[me.t]))
    for k in range(4):
        for core in (c, other):
            if k or core is other:
                t = me.rank(k, core)
                late.append(send.local(cot_all.at[t], cotv.at[t]))
    from_sib = []

    def hand_over(i):
        for copy in arrivals[i]:
            copy.wait_recv()
        now = []
        for d in (1, -1, 2):
            block = tokens_of(obv.at[me.rank(d, c)], order[i])
            now.append(send(block, block, me.sibling()))
        from_sib.append(now)

    hand_over(0)
    send_tokens(2)
    for copy in late:
        copy.wait()

    @pl.loop(0, 4)
    def _(i):
        cot = jnp.concatenate([cotv[2 * i], cotv[2 * i + 1]], axis=0)
        gh = mm_nt(cot, dw[...].reshape(part, width))
        ghs[2 * i], ghs[2 * i + 1] = gh[:TOK], gh[TOK:]

    o_far.end()
    o_sib.append(send(spread(ow, 2), spread(ow, 2), me.sibling()))
    hand_over(1)
    send_tokens(3)
    own_ob.wait()
    own_sib.wait_recv()
    for copy in loads[:4]:
        copy.wait()
    for copy in o_sib:
        copy.wait_recv()

    g2 = gains[1:2]
    sums = Scatter(me, send, lambda k, at: mine[k, at], sib, mid, far, near)
    w_gu = lambda: guw[...].reshape(width, 2 * part)
    w_down = lambda: dw[...].reshape(part, width)
    w_out = lambda: ow[...].reshape(width, width)

    def feed(i):
        k = order[i] % 4
        for copy in from_sib[i]:
            copy.wait_recv()
        ranks = (me.rank(k, c), me.rank(k, other))
        heads = []
        for s in range(NT):
            blocks = [obv[s, t // 4, lax.rem(t // 2, 2), lax.rem(t, 2)] for t in ranks]
            heads.append(
                jnp.concatenate([unpack(block, TOK)[:, : 2 * HD] for block in blocks], axis=0)
            )
        heads = jnp.concatenate(heads, axis=1)
        x = jnp.concatenate([tokv[t] for t in ranks], axis=0).astype(F32) + mm(heads, w_out())
        if k == 0:
            x2_out[...] = x[:TOK]
        h = x * lax.rsqrt(jnp.mean(x * x, axis=1, keepdims=True) + NORM_EPS)
        h = (h * g2).astype(BF)
        if i == 0:
            gu_far.end()
            for copy in loads[4:]:
                copy.wait()
        gu = mm(h, w_gu())
        gate, up = gu[:, :part], gu[:, part:]
        sigmoid = 1.0 / (1.0 + jnp.exp(-gate))
        silu = gate * sigmoid
        hidden = (silu * up).astype(BF)
        gh = jnp.concatenate([ghs[t] for t in ranks], axis=0)
        ggate = (gh * up * sigmoid * (1.0 + gate * (1.0 - sigmoid))).astype(BF)
        gup = (gh * silu).astype(BF)
        both = jnp.concatenate([ggate, gup], axis=1)
        gh2 = mm_nt(both, w_gu()).astype(BF)
        mine[k], tosib[k] = gh2[:TOK], gh2[TOK:]
        sums.hand(k, tosib.at[k])
        y = mm(hidden, w_down()).astype(BF)
        for n, t in enumerate(ranks):
            rows = slice(n * TOK, (n + 1) * TOK)
            obx[t], h2[t], hid[t], ggu[t], y_buf[t] = (
                heads[rows], h[rows], hidden[rows], both[rows], y[rows],
            )

    feed(0)
    hand_over(2)
    feed(1)
    hand_over(3)
    sums.step2()
    feed(2)
    sums.step1()
    feed(3)
    sums.step3()
    sums.step0()
    send.local(y_buf, y_out)

    @pl.loop(0, 3)
    def _(n):
        cols = pl.ds(pl.multiple_of(n * CHUNK, CHUNK), CHUNK)
        cot = cotv[:, :, cols].reshape(GROUP_ROWS, CHUNK)
        value = mm_tn(hid[...].reshape(GROUP_ROWS, part), cot).astype(BF)
        grad_down[:, :, cols] = value.reshape(4, TOK, CHUNK)

    down_sum = RingSum(
        send, me.along_x, lambda k: down_spread(grad_down, k), (d_far, d_direct, d_summed, d_mid)
    )
    down_sum.begin()

    gh2 = sums.end()
    x = x2_out[...]
    r2 = lax.rsqrt(jnp.mean(x * x, axis=1, keepdims=True) + NORM_EPS)
    n2 = x * r2
    gm = gh2 * g2
    gain_out[...] = jnp.sum(gh2 * n2, axis=0, keepdims=True)
    gx2 = r2 * (gm - n2 * jnp.mean(gm * n2, axis=1, keepdims=True)) + cotv[me.t].astype(F32)
    gx2_out[...] = gx2
    gav = tokv
    gav[me.t] = gx2.astype(BF)
    back = Gather(send, me.along_y, lambda k: gav.at[me.rank(k, c)], halves)
    back_sib = [send(gav.at[me.t], gav.at[me.t], me.sibling())]

    def grad_columns(k):
        z = me.z_at(k)
        cols = pl.ds(pl.multiple_of(z * 4 * HD, TOK), 4 * HD)
        h = h2[:, :, cols].reshape(GROUP_ROWS, 4 * HD)
        value = mm_tn(h, ggu[...].reshape(GROUP_ROWS, 2 * part)).astype(BF)
        for n in range(4):
            for j in range(8):
                grad_gu[z, n, j * HD : (j + 1) * HD] = value[
                    n * HD : (n + 1) * HD, j * TOK : (j + 1) * TOK
                ]

    pl.loop(0, 2)(grad_columns)
    down_sum.middle()
    pl.loop(2, 3)(grad_columns)
    back.forward()
    back_sib += [
        send(gav.at[me.rank(k, c)], gav.at[me.rank(k, c)], me.sibling()) for k in (-1, 1)
    ]
    pl.loop(3, 4)(grad_columns)
    send.local(grad_gu, u_out)
    back.end()
    back_sib.append(send(gav.at[me.rank(2, c)], gav.at[me.rank(2, c)], me.sibling()))
    down_sum.end(d_sum)
    for copy in back_sib:
        copy.wait_recv()

    w_own = ow[me.t // 2, lax.rem(me.t, 2)].reshape(2 * HD, width)
    for i in range(4):
        ga = jnp.concatenate([gav[2 * i], gav[2 * i + 1]], axis=0)
        go = mm_nt(ga, w_own)
        place = places_of(me, 2 * i, (QROWS, 2 * HD), 0)
        _, end = starts_of(lengths, place)
        go = jnp.where(place < end, go, 0.0).astype(BF)
        for n in range(2):
            t = 2 * i + n
            both = [go[n * TOK : (n + 1) * TOK, h * HD : (h + 1) * HD] for h in range(2)]
            both = jnp.concatenate(both, axis=0)
            delta = jnp.sum(both.astype(F32) * o_in[t], axis=1, keepdims=True)
            delta_out[t] = jnp.transpose(jnp.broadcast_to(delta, (QROWS, TOK)))[:1]
            before, after = jnp.zeros((QROWS, HD), BF), jnp.zeros((QROWS, 2 * TOK - 2 * HD), BF)
            go_out[t] = jnp.concatenate([before, both, after], axis=1)
    ga_half = gav[:, :, pl.ds(pl.multiple_of(me.yh * half, half), half)].reshape(GROUP_ROWS, half)
    for z in range(4):
        block = obx[:, :, z * 4 * HD : (z + 1) * 4 * HD].reshape(GROUP_ROWS, 4 * HD)
        o_buf[...] = mm_tn(block, ga_half)
        at = pl.multiple_of((me.yl * 2 + c) * HD, 8)
        value = o_buf[pl.ds(at, HD)].astype(BF)
        for j in range(6):
            grad_o[z, j * HD : (j + 1) * HD] = value[:, j * TOK : (j + 1) * TOK]
        grad_o[z, 6 * HD :] = jnp.zeros_like(grad_o[z, 6 * HD :])
    send.finish()


def middle(lengths, ob, tok_all, cot_all, cot, o_w, gu_w, down_w, gains, o):
    def like(*shape, dtype=BF):
        return jax.ShapeDtypeStruct(shape, dtype)

    def vmem(*shape, dtype=BF):
        return pltpu.VMEM(shape, dtype)

    width = o_w.shape[-1]
    part = gu_w.shape[-1] // 2
    grad_u = (4, 4, 2 * part * HD // TOK, TOK)
    outs = (
        (like(NT, QROWS, 2 * TOK), VM),
        (like(NT, 1, QROWS, dtype=F32), VM),
        (like(TOK, width, dtype=F32), VM),
        (like(TOK, width, dtype=F32), VM),
        (like(NT, TOK, width), ANY),
        (like(*grad_u), ANY),
        (like(4, TOK // 4, width), VM),
        (like(4, 6 * HD + 64, TOK), VM),
        (like(1, width, dtype=F32), VM),
    )
    return pl.pallas_call(
        middle_kernel,
        out_shape=tuple(o[0] for o in outs),
        in_specs=[SM] + [ANY] * 7 + [VM, VM],
        out_specs=tuple(o[1] for o in outs),
        scratch_shapes=[
            vmem(NT, 2, 2, 2, TOK * 3 // 2, TOK),
            vmem(NT, TOK, width),
            vmem(*o_w.shape),
            vmem(*gu_w.shape),
            vmem(4, TOK, width),
            vmem(NT, TOK, width),
            vmem(NT, TOK, width),
            vmem(NT, TOK, width),
            vmem(NT, TOK, part),
            vmem(NT, TOK, 2 * part),
            vmem(NT, TOK, part, dtype=F32),
            vmem(4, TOK, width),
            vmem(4, TOK, width),
            vmem(4, TOK, width),
            vmem(4, TOK, width),
            vmem(2, TOK // 2, width),
            vmem(2, TOK, width),
            vmem(NT, TOK, width),
            vmem(*grad_u),
            vmem(4, TOK, width),
            *[vmem(2, 2, TOK // 4, width)] * 4,
            vmem(4 * HD, width // 2, dtype=F32),
            pltpu.SemaphoreType.DMA((80,)),
            pltpu.SemaphoreType.DMA((80,)),
            pltpu.SemaphoreType.DMA((24,)),
        ],
        compiler_params=pltpu.CompilerParams(
            collective_id=1, has_side_effects=True, vmem_limit_bytes=63 * 2**20
        ),
        name="middle",
    )(lengths, ob, tok_all, cot_all, cot, o_w, gu_w, down_w, gains, o)


class Exchange:
    def __init__(self, me, send, block, from_sib, slots):
        self.me, self.send, self.block, self.from_sib, self.slots = me, send, block, from_sib, slots
        other = 1 - me.c
        self.first = [
            send(block.at[yl * 2 + other], from_sib.at[yl], me.sibling()) for yl in range(2)
        ]

    def second(self):
        me = self.me
        for copy in self.first:
            copy.wait_recv()
        mine, theirs = me.t, me.rank(0, 1 - me.c)
        self.copies = []
        for k, yl in ((1, 1 - me.yl), (-1, 1 - me.yl), (2, me.yl)):
            for src, t in ((self.block.at[yl * 2 + me.c], mine), (self.from_sib.at[yl], theirs)):
                self.copies.append(self.send(src, self.slots.at[t], me.along_y(k)))
        self.slots[mine] = self.block[me.yl * 2 + me.c]
        self.slots[theirs] = self.from_sib[me.yl]

    def end(self):
        for copy in self.copies:
            copy.wait_recv()


def back_kernel(
    lengths, freq, kv, q_in, go_in, lse, delta, y_hbm, gu_hbm, d_sum, grad_o,
    h1_hbm, tok_hbm, qkv_hbm, gx2, x2_own, gains, gain2,
    layer_out, tokens_grad, all_gu, all_q, all_down, all_o,
    y_mine, grad_gu, u_far, u_direct, h1, tokv, qkv_w,
    keyv, gkv, gq, staged, kv_far, kv_direct, kv_summed, kv_mid, gqkv, starts,
    y_sib, y_mid, y_far, y_near, mine, tosib, sib, mid, far, near, grad_q,
    u_summed, u_mid, o_far, o_direct, o_summed, o_mid, q_far, q_direct, q_summed, q_mid,
    u_sum, o_sum, q_sum,
    ux_far, ux_direct, ux_summed, ux_mid, d_far, d_direct, d_summed, d_mid,
    ox_far, ox_direct, ox_summed, ox_mid, qx_far, qx_direct, qx_summed, qx_mid,
    u_mine, q_mine, u_from, q_from,
    send_sem, recv_sem, local_sem,
):
    me = Place()
    me.greet(
        tuple(me.along_x(k) for k in (1, -1, 2))
        + (me.along_z(1), me.along_z(-1), me.along_y(2))
    )
    send = Copies(send_sem, recv_sem, local_sem)
    c, other = me.c, 1 - me.c
    rows = HD

    def over_z(ref, buffers):
        return RingSum(send, me.along_z, lambda k: ref.at[me.z_at(k)], buffers)

    def quarters(ref, size, leading):
        def block(k):
            at = pl.ds(pl.multiple_of(me.x_at(k) * size, 16), size)
            return ref.at[:, at] if leading else ref.at[at]

        return block

    ys = Scatter(me, send, lambda k, at: y_mine[k, at], y_sib, y_mid, y_far, y_near)
    for k in (2, 1, 3, 0):
        ys.hand(k, y_hbm.at[me.rank(k, other)])
    down_z = over_z(d_sum, (d_far, d_direct, d_summed, d_mid))
    down_z.begin()
    out_z = over_z(grad_o, (o_far, o_direct, o_summed, o_mid))
    out_z.begin()
    loads = [send.local(y_hbm.at[me.rank(k, c)], y_mine.at[k]) for k in range(4)]
    loads += [send.local(gu_hbm.at[me.z_at(k)], grad_gu.at[me.z_at(k)]) for k in (1, 3, 0)]
    late = [send.local(qkv_hbm, qkv_w), send.local(h1_hbm, h1), send.local(tok_hbm, tokv)]

    def over_x(ref):
        return Gather(send, me.along_x, lambda k: ref.at[me.x_at(k)], halves)

    for t in range(NT):
        starts[t], _ = starts_of(lengths, places_of(me, t, (1, TOK), 1))
    gq[...] = jnp.zeros_like(gq)
    lane = lax.broadcasted_iota(jnp.int32, (1, 2 * TOK), 1)
    lane_scale = jnp.where(lane < HD, LN2, 1.0)

    def source(k):
        x = me.x_at(k)
        keyv[...] = unpack(kv[x], GROUP_ROWS)
        gkv[...] = jnp.zeros_like(gkv)
        row = lax.broadcasted_iota(jnp.int32, (TOK, QROWS), 0)
        for t in range(NT):
            n = (t + 1) * TOK
            q, go = q_in[t], go_in[t]
            start = jnp.concatenate([starts[t]] * 2, axis=1)
            p = jnp.exp2(mm_nt(keyv[:n, :TOK], q) - lse[t])
            kept = []
            for b in range(t + 1):
                key = row + (b * CHUNK + x * TOK)
                keep = key >= start
                if b == t:
                    column = lax.broadcasted_iota(jnp.int32, (TOK, QROWS), 1)
                    keep = keep & (key <= lax.rem(column, TOK) + (t * CHUNK + me.x * TOK))
                kept.append(jnp.where(keep, p[b * TOK : (b + 1) * TOK], 0.0))
            p = jnp.concatenate(kept, axis=0) if t else kept[0]
            gp = mm_nt(keyv[:n], go)
            gs = (p * (gp - delta[t])).astype(BF)
            gkv[:n] += mm(p.astype(BF), go)
            gkv[:n, :TOK] += mm(gs, q)
            gq[t] += mm_tn(gs, keyv[:n, :TOK])

    def stage(n):
        value = (gkv[...] * lane_scale).astype(BF)
        staged[n, :GROUP_ROWS] = value[:, :TOK]
        tail = value[:, TOK : TOK + TOK // 2]
        staged[n, GROUP_ROWS:] = jnp.concatenate(
            [tail[: GROUP_ROWS // 2], tail[GROUP_ROWS // 2 :]], axis=1
        )

    kv_sum = RingSum(
        send,
        me.along_x,
        lambda k: staged.at[(None, 1, 0, 2)[k]],
        (kv_far, kv_direct, kv_summed, kv_mid),
    )
    source(2)
    stage(0)
    kv_sum.begin_far()
    down_z.middle()
    out_z.middle()
    over_z(gu_hbm, (u_far, u_direct, u_summed, u_mid)).begin()
    gu_first = send.all[-4:]
    gu_z = over_z(grad_gu, (u_far, u_direct, u_summed, u_mid))
    gu_z.first, gu_z.near = gu_first[:2], gu_first[2:]
    for copy in loads[:4]:
        copy.wait()
    ys.step2()
    ys.step1()

    @pl.loop(0, 2)
    def _(n):
        source(2 * n + 1)
        stage(n + 1)

    kv_sum.begin_near()
    kv_sum.middle()
    down_z.end(all_down.at[me.x, me.yh])
    down_y = send(all_down.at[me.x, me.yh], all_down.at[me.x, me.yh], me.along_y(2))
    out_z.end(o_sum)
    out_x = RingSum(
        send,
        me.along_x,
        quarters(o_sum, o_sum.shape[0] // 4, False),
        (ox_far, ox_direct, ox_summed, ox_mid),
    )
    out_x.begin()
    ys.step3()
    ys.step0()
    source(0)
    out_x.middle()
    down_y.wait_recv()
    for copy in loads[4:] + late:
        copy.wait()
    for i in range(2):
        kv_sum.near[1 - i].wait_recv()
        kv_sum.last[i].wait_recv()
    others = [kv_direct[1 - i].astype(F32) + kv_summed[i].astype(F32) for i in range(2)]
    gkv[...] = gkv[...] * lane_scale + unpack(jnp.concatenate(others, axis=0), GROUP_ROWS)
    gu_z.middle()
    down_all = over_x(all_down)
    out_x.end(all_o.at[me.x, me.yh])
    out_y = send(all_o.at[me.x, me.yh], all_o.at[me.x, me.yh], me.along_y(2))

    for i in range(4):
        place = places_of(me, 2 * i, (QROWS, HD), 0)
        start, _ = starts_of(lengths, place)
        angle = (place - start).astype(F32) * freq[...]
        cosine, sine = jnp.cos(angle), -jnp.sin(angle)
        at = slice(i * QROWS, (i + 1) * QROWS)
        parts = []
        for h in range(2):
            of = slice(h * TOK, (h + 1) * TOK)
            g = jnp.concatenate([gq[2 * i, of, :HD], gq[2 * i + 1, of, :HD]], axis=0)
            parts.append(turn(g * SCALE, cosine, sine))
        parts.append(turn(gkv[at, :HD], cosine, sine))
        parts.append(gkv[at, HD : 2 * HD])
        gqkv[at] = jnp.concatenate(parts, axis=1).astype(BF)

    g1 = gains[0:1]
    span = 4 * rows
    for z in range(4):
        h = h1[:, :, z * span : (z + 1) * span].reshape(GROUP_ROWS, span)
        g = mm_tn(h, gqkv[...])
        of_gain = jnp.sum(g * qkv_w[z * span : (z + 1) * span].astype(F32), axis=1, keepdims=True)
        g = g.astype(BF)
        for n in range(4):
            part = slice(n * rows, (n + 1) * rows)
            for j in range(3):
                grad_q[z, n, j * rows : (j + 1) * rows] = g[part, j * TOK : (j + 1) * TOK]
            at = slice(z * span + n * rows, z * span + (n + 1) * rows)
            first = jnp.transpose(jnp.broadcast_to(of_gain[part], (rows, TOK)))[:1] / g1[:, at]
            extra = jnp.concatenate([first, gain2[:, at]], axis=0)
            extra = jnp.concatenate([extra, jnp.zeros((30, rows), F32)], axis=0)
            extra = jnp.concatenate([extra, jnp.zeros((32, TOK - rows), F32)], axis=1)
            grad_q[z, n, 3 * rows :] = extra.astype(BF)
    q_z = over_z(grad_q, (q_far, q_direct, q_summed, q_mid))
    q_z.begin()
    down_all.forward()
    out_y.wait_recv()
    out_all = over_x(all_o)

    h_sums = Scatter(me, send, lambda k, at: mine[k, at], sib, mid, far, near)

    def feed(k):
        ranks = (me.rank(k, c), me.rank(k, other))
        g = [gqkv[pl.ds(pl.multiple_of(t * TOK, TOK), TOK)] for t in ranks]
        low = mm_nt(jnp.concatenate(g, axis=0), qkv_w[...]).astype(BF)
        mine[k], tosib[k] = low[:TOK], low[TOK:]
        h_sums.hand(k, tosib.at[k])

    feed(2)
    gu_z.end(u_sum)
    gu_x = RingSum(
        send,
        me.along_x,
        quarters(u_sum, u_sum.shape[1] // 4, True),
        (ux_far, ux_direct, ux_summed, ux_mid),
    )
    gu_x.begin()
    feed(1)
    h_sums.step2()
    feed(3)
    h_sums.step1()
    out_all.forward()
    q_z.middle()
    gu_x.middle()
    feed(0)
    h_sums.step3()
    gu_x.end(u_mine)
    u_rows = Exchange(me, send, u_mine, u_from, all_gu.at[me.x])
    layer_out[...] = (x2_own[...] + ys.end()).astype(BF)
    h_sums.step0()
    u_rows.second()
    q_z.end(q_sum)
    q_x = RingSum(
        send,
        me.along_x,
        quarters(q_sum, q_sum.shape[1] // 4, True),
        (qx_far, qx_direct, qx_summed, qx_mid),
    )
    q_x.begin()
    u_rows.end()
    q_x.middle()
    gu_all = over_x(all_gu)
    q_x.end(q_mine)
    q_rows = Exchange(me, send, q_mine, q_from, all_q.at[me.x])
    gh1 = h_sums.end()
    x = tokv[...].astype(F32)
    r1 = lax.rsqrt(jnp.mean(x * x, axis=1, keepdims=True) + NORM_EPS)
    n1 = x * r1
    gn = gh1 * g1
    gx = gx2[...] + r1 * (gn - n1 * jnp.mean(gn * n1, axis=1, keepdims=True))
    tokens_grad[...] = gx.astype(BF)
    q_rows.second()
    q_rows.end()
    q_all = over_x(all_q)
    gu_all.forward()
    q_all.forward()
    send.finish()


def back(*args):
    lengths = args[0]
    grad_gu, grad_o, qkv_w = args[7], args[9], args[12]
    half_u = (2, 2) + grad_gu.shape[2:]
    freq = jnp.asarray(np.tile(frequency_table(HD), 2)[None])
    width = qkv_w.shape[0]
    u_rows, o_rows = grad_gu.shape[2], grad_o.shape[1]
    q_rows = 3 * HD + 32

    def like(*shape, dtype=BF):
        return jax.ShapeDtypeStruct(shape, dtype)

    def vmem(*shape, dtype=BF):
        return pltpu.VMEM(shape, dtype)

    def ring(*shape):
        half = (shape[0] // 2,) + shape[1:]
        return [vmem(2, *half)] * 4

    def group(mine):
        head = [vmem(4, TOK, width)] * (4 if mine else 2)
        return head + [vmem(2, TOK // 2, width), vmem(2, TOK, width)]

    outs = (
        like(TOK, width),
        like(TOK, width),
        like(4, NT, u_rows // 4, TOK),
        like(4, NT, q_rows // 4, TOK),
        like(4, 2, TOK // 4, width),
        like(4, 2, o_rows // 4, TOK),
    )
    return pl.pallas_call(
        back_kernel,
        out_shape=outs,
        in_specs=[SM] + [VM] * 6 + [ANY] * 2 + [VM] * 2 + [ANY] * 3 + [VM] * 4,
        out_specs=(VM,) * len(outs),
        scratch_shapes=[
            vmem(4, TOK, width),
            vmem(*grad_gu.shape),
            vmem(*half_u),
            vmem(*half_u),
            vmem(NT, TOK, width),
            vmem(TOK, width),
            vmem(*qkv_w.shape),
            vmem(GROUP_ROWS, 2 * TOK),
            vmem(GROUP_ROWS, 2 * TOK, dtype=F32),
            vmem(NT, QROWS, TOK, dtype=F32),
            vmem(3, PACKED, TOK),
            *[vmem(2, PACKED // 2, TOK)] * 4,
            vmem(GROUP_ROWS, 4 * HD),
            vmem(NT, 1, TOK, dtype=jnp.int32),
            *group(False),
            *group(True),
            vmem(4, 4, q_rows, TOK),
            vmem(*half_u),
            vmem(*half_u),
            *ring(o_rows, TOK),
            *ring(4, q_rows, TOK),
            vmem(4, u_rows, TOK),
            vmem(o_rows, TOK),
            vmem(4, q_rows, TOK),
            *ring(4, u_rows // 4, TOK),
            *ring(TOK // 4, width),
            *ring(o_rows // 4, TOK),
            *ring(4, q_rows // 4, TOK),
            vmem(4, u_rows // 4, TOK),
            vmem(4, q_rows // 4, TOK),
            vmem(2, u_rows // 4, TOK),
            vmem(2, q_rows // 4, TOK),
            pltpu.SemaphoreType.DMA((128,)),
            pltpu.SemaphoreType.DMA((128,)),
            pltpu.SemaphoreType.DMA((16,)),
        ],
        compiler_params=pltpu.CompilerParams(
            collective_id=2, has_side_effects=True, vmem_limit_bytes=63 * 2**20
        ),
        name="back",
    )(lengths, freq, *args[1:])


def finish_kernel(
    layer_hbm, tokens_hbm, gu_hbm, q_hbm, down_hbm, o_hbm,
    layer_to, tokens_to, to_q, to_k, to_v, to_o, to_gate, to_up, to_down, to_gain1, to_gain2,
    all_gu, all_q, all_down, all_o, sem,
):
    pairs = (
        (gu_hbm, all_gu), (q_hbm, all_q), (down_hbm, all_down), (o_hbm, all_o),
        (layer_hbm, layer_to.at[0]), (tokens_hbm, tokens_to.at[0]),
    )
    copies = [pltpu.make_async_copy(a, b, sem.at[i]) for i, (a, b) in enumerate(pairs)]
    for copy in copies:
        copy.start()
    for copy in copies:
        copy.wait()
    for t in range(NT):
        for j in range(8):
            tile = all_gu[j // 2, t, (j % 2) * HD : (j % 2 + 1) * HD].astype(F32)
            at = (j % 4) * 2 * CHUNK + t * TOK
            if j < 4:
                to_gate[:, at : at + TOK] = tile
            else:
                to_up[:, at : at + TOK] = tile
    gains = jnp.zeros((2, TOK), F32)
    heads = []
    for t in range(NT):
        value = jnp.concatenate([all_q[x, t] for x in range(4)], axis=0).astype(F32)
        tiles = [value[j * HD : (j + 1) * HD] for j in range(3)]
        heads.append(jnp.concatenate(tiles, axis=1))
        gains += value[3 * HD : 3 * HD + 2]
    to_gain1[...] = gains[0, :HD]
    to_gain2[...] = gains[1, :HD]
    to_q[...] = jnp.concatenate([h[:, : 2 * HD] for h in heads], axis=1)
    to_k[...] = jnp.concatenate([h[:, 2 * HD : 3 * HD] for h in heads], axis=1)
    to_v[...] = jnp.concatenate([h[:, 3 * HD :] for h in heads], axis=1)
    for yh in range(2):
        value = jnp.concatenate([all_o[x, yh] for x in range(4)], axis=0).astype(F32)
        for j in range(6):
            at = (yh * 6 + j) * TOK
            to_o[:, at : at + TOK] = value[j * HD : (j + 1) * HD]
        for x in range(4):
            size = all_down.shape[2]
            at = yh * TOK + x * size
            to_down[at : at + size] = all_down[x, yh].astype(F32)


def finish(layer_out, tokens_grad, all_gu, all_q, all_down, all_o):
    rows, width = layer_out.shape
    part = all_gu.shape[2] * 4 // HD * TOK // 2
    shapes = [
        ((1, rows, width), BF),
        ((1, rows, width), BF),
        ((HD, width), F32),
        ((HD, width // 2), F32),
        ((HD, width // 2), F32),
        ((HD, width), F32),
        ((HD, NT * part), F32),
        ((HD, NT * part), F32),
        ((2 * TOK, width), F32),
        ((HD,), F32),
        ((HD,), F32),
    ]
    return pl.pallas_call(
        finish_kernel,
        out_shape=tuple(jax.ShapeDtypeStruct(*s) for s in shapes),
        in_specs=[ANY] * 6,
        out_specs=(VM,) * len(shapes),
        scratch_shapes=[pltpu.VMEM(a.shape, BF) for a in (all_gu, all_q, all_down, all_o)]
        + [pltpu.SemaphoreType.DMA((6,))],
        compiler_params=pltpu.CompilerParams(vmem_limit_bytes=63 * 2**20),
        name="finish",
    )(layer_out, tokens_grad, all_gu, all_q, all_down, all_o)


def body(
    tokens,
    doc_lengths,
    w_query,
    w_key,
    w_value,
    w_output,
    w_gate,
    w_up,
    w_down,
    gain_attn,
    gain_mlp,
    cotangent,
):
    tok_all, cot_all, h1, gu_w, o_w, down_w, kv, q, o, lse, ob, gains, qkv_w = front(
        doc_lengths,
        tokens[0],
        cotangent[0],
        w_query,
        w_key,
        w_value,
        w_gate,
        w_up,
        w_output,
        w_down,
        gain_attn.reshape(1, -1),
        gain_mlp.reshape(1, -1),
    )
    ob = ob.reshape((2, 2, 2) + ob.shape[1:])
    go, delta, gx2, own, y_part, grad_gu, d_sum, grad_o, gain2 = middle(
        doc_lengths, ob, tok_all, cot_all, cotangent[0], o_w, gu_w, down_w, gains, o
    )
    sums = back(
        doc_lengths, kv, q, go, lse, delta, y_part, grad_gu, d_sum, grad_o, h1, tokens[0], qkv_w,
        gx2, own, gains, gain2,
    )
    return finish(*sums)


def solution(mesh):
    fine = Mesh(mesh.devices.reshape(4, 2, 2, 2, 4), AXES)
    by_token = P("z", ("yl", "c", "yh", "x"), None)
    by_row = P(("z", "yl", "c"), None)
    by_feature = P(("z", "yl", "c"))
    return jax.shard_map(
        body,
        mesh=fine,
        in_specs=(by_token, P("z", None))
        + (by_row,) * 7
        + (by_feature, by_feature, by_token),
        out_specs=(by_token, by_token) + (by_row,) * 7 + (by_feature, by_feature),
        check_vma=False,
    )
```

```python
import jax
import jax.numpy as jnp
import numpy as np
from jax import lax
from jax.experimental import pallas as pl
from jax.experimental.pallas import tpu as pltpu
from jax.sharding import Mesh
from jax.sharding import PartitionSpec as P

HEADS = 16
KV = 8
HD = 96
NORM_EPS = 1e-05
LOG2E = 1.4426950408889634
LN2 = 0.6931471805599453
SCALE = HD ** (-0.5)
BF = jnp.bfloat16
F32 = jnp.float32
AXES = ("z", "yl", "c", "yh", "x")
GROUP = ("yl", "c", "yh")
MESH = pl.DeviceIdType.MESH
TOK = 128
NT = 8
NX = 4


def frequency_table(head_width):
    halfway = head_width // 2
    base_freq = 500000.0 ** (-np.arange(halfway) * 2.0 / head_width)
    wavelength = 2.0 * np.pi / base_freq
    smooth = (8192.0 / wavelength - 1.0) / 3.0
    middle = (1.0 - smooth) * base_freq / 32.0 + smooth * base_freq
    freq_table = np.where(
        wavelength > 8192.0, base_freq / 32.0, np.where(wavelength < 2048.0, base_freq, middle)
    )
    return freq_table.astype(np.float32)


def mm(a, b):
    return jnp.dot(a, b, preferred_element_type=F32)


def mm_nt(a, b):
    return lax.dot_general(a, b, (((1,), (1,)), ((), ())), preferred_element_type=F32)


def mm_tn(a, b):
    return lax.dot_general(a, b, (((0,), (0,)), ((), ())), preferred_element_type=F32)


class Place:
    def __init__(self):
        self.z, self.x = lax.axis_index("z"), lax.axis_index("x")
        self.yl, self.c, self.yh = (lax.axis_index(name) for name in GROUP)
        self.y = self.yh * 2 + self.yl
        self.t = self.rank(0, self.c)

    def rank(self, k, c):
        y = lax.rem(self.y + (k + 4), 4)
        return lax.rem(y, 2) * 4 + c * 2 + y // 2

    def y_at(self, k):
        return lax.rem(self.y + (k + 4), 4)

    def along_y(self, k):
        y = self.y_at(k)
        return {"yh": y // 2, "yl": lax.rem(y, 2)}

    def x_at(self, k):
        return lax.rem(self.x + (k + 4), 4)

    def z_at(self, k):
        return lax.rem(self.z + (k + 4), 4)

    def along_x(self, k):
        return {"x": self.x_at(k)}

    def along_z(self, k):
        return {"z": self.z_at(k)}

    def sibling(self):
        return {"c": 1 - self.c}

    def greet(self, others=()):
        barrier = pltpu.get_barrier_semaphore()
        everyone = (self.along_y(1), self.along_y(-1), self.sibling()) + tuple(others)
        for who in everyone:
            pl.semaphore_signal(barrier, inc=1, device_id=who, device_id_type=MESH)
        pl.semaphore_wait(barrier, len(everyone))


class Kept:
    def __init__(self, copy):
        self.copy, self.done = copy, False

    def wait(self):
        if not self.done:
            self.copy.wait()
        self.done = True


class Sent:
    def __init__(self, copy):
        self.copy, self.arrived = copy, False

    def wait_recv(self):
        if not self.arrived:
            self.copy.wait_recv()
        self.arrived = True

    def wait_send(self):
        self.copy.wait_send()


class Copies:
    def __init__(self, send_sem, recv_sem, local_sem=None):
        self.send_sem, self.recv_sem, self.local_sem = send_sem, recv_sem, local_sem
        self.all, self.locals = [], []

    def __call__(self, src, dst, who):
        i = len(self.all)
        assert i < self.send_sem.shape[0]
        copy = pltpu.make_async_remote_copy(
            src_ref=src,
            dst_ref=dst,
            send_sem=self.send_sem.at[i],
            recv_sem=self.recv_sem.at[i],
            device_id=who,
            device_id_type=MESH,
        )
        copy.start()
        sent = Sent(copy)
        self.all.append(sent)
        return sent

    def local(self, src, dst):
        assert len(self.locals) < self.local_sem.shape[0]
        copy = pltpu.make_async_copy(src, dst, self.local_sem.at[len(self.locals)])
        copy.start()
        kept = Kept(copy)
        self.locals.append(kept)
        return kept

    def finish(self):
        for kept in self.locals:
            kept.wait()
        for sent in self.all:
            sent.wait_recv()
        for sent in self.all:
            sent.wait_send()


class Gather:
    def __init__(self, send, along, slot, cut, src=None):
        self.send, self.along, self.slot, self.cut = send, along, slot, cut
        src = slot(0) if src is None else src
        to = slot(0)
        self.first = [send(cut(src, i), cut(to, i), along(1 - 2 * i)) for i in range(2)]
        self.second = [send(cut(src, 1 - i), cut(to, 1 - i), along(1 - 2 * i)) for i in range(2)]

    def hand_on(self):
        self.far = []
        for i in range(2):
            self.first[i].wait_recv()
            part = self.cut(self.slot(2 * i - 1), i)
            self.far.append(self.send(part, part, self.along(1 - 2 * i)))

    def settle(self):
        for copy in self.second:
            copy.wait_recv()

    def forward(self):
        self.hand_on()
        self.settle()

    def end(self):
        for copy in self.far:
            copy.wait_recv()


class Neighbours:
    def __init__(self, send, along, src, slot):
        self.up = send(src, slot(0), along(1))
        self.down = send(src, slot(0), along(-1))


class Relay:
    def __init__(self, send, along, take, slot, cut):
        self.up = send(cut(take(-1), 0), cut(slot(-1), 0), along(1))
        self.down = send(cut(take(1), 1), cut(slot(1), 1), along(-1))

    def end(self):
        self.up.wait_recv()
        self.down.wait_recv()


def halves(ref, i):
    half = ref.shape[0] // 2
    return ref.at[pl.ds(i * half, half)]


ANY = pl.BlockSpec(memory_space=pl.ANY)
VM = pl.BlockSpec(memory_space=pltpu.VMEM)
SM = pl.BlockSpec(memory_space=pltpu.SMEM)
GROUP_ROWS = NT * TOK
QROWS = 2 * TOK
CHUNK = NX * TOK
PACKED = GROUP_ROWS + GROUP_ROWS // 2


def starts_of(lengths_ref, place):
    end, start = 0, jnp.zeros_like(place)
    for i in range(lengths_ref.shape[1]):
        end = end + lengths_ref[0, i]
        start = jnp.maximum(start, jnp.where(place >= end, end, 0))
    return start, end


def places_of(me, tile, shape, axis):
    row = lax.broadcasted_iota(jnp.int32, shape, axis)
    return (tile + row // TOK) * CHUNK + me.x * TOK + lax.rem(row, TOK)


def turn(v, cosine, sine):
    half = HD // 2
    return v * cosine + jnp.concatenate([-v[:, half:], v[:, :half]], axis=1) * sine


def unpack(packed, n):
    half = TOK // 2
    tail = packed[n:].reshape(n // TOK, half, TOK)
    tail = jnp.concatenate([tail[:, :, :half], tail[:, :, half:]], axis=1).reshape(n, half)
    return jnp.concatenate([packed[:n], tail, jnp.zeros_like(tail)], axis=1)


def pack_tail(tail):
    half = TOK // 2
    return jnp.concatenate([tail[:half], tail[half:]], axis=1)


def front_kernel(
    lengths, freq, tok, cot, wq, wk, wv, wg, wu, wo, wd, gain1, gain2,
    tok_all, cot_all, h1_out, gu_w, o_w, down_w, kv_out, q_out, o_out, lse_out, ob_out, gains_out, qkv_w,
    tokv, h1, slices_q, slices_u, tmp_q, tmp_u, gq, kv, keyv, starts, top, total, acc, w_kv, w_q, down_v, cosines, sines,
    send_sem, recv_sem, local_sem,
):
    me = Place()
    me.greet((me.along_x(1), me.along_x(-1), me.along_z(1), me.along_z(-1)))
    send = Copies(send_sem, recv_sem, local_sem)
    c, other = me.c, 1 - me.c
    step = 1 - 2 * c
    slot, slot_other = me.yl * 2 + c, me.yl * 2 + other
    toward, away = me.along_y(step), me.along_y(-step)
    t_toward, t_relay, t_sib = me.rank(step, c), me.rank(step, other), me.rank(0, other)
    rows, width = wq.shape

    quarter = TOK // 4
    down_rows = lambda k: pl.ds(pl.multiple_of(me.x_at(k) * quarter, quarter), quarter)
    down_src = wd.at[pl.ds(pl.multiple_of(me.yh * TOK + me.x * quarter, quarter), quarter)]
    own_down = send.local(down_src, down_v)
    down_z = Gather(send, me.along_z, lambda k: down_w.at[me.z_at(k), down_rows(0)], halves, down_src)

    slices_q[:, rows:, :] = jnp.zeros_like(slices_q[:, rows:, :])
    for t in range(NT):
        slices_q[t, :rows] = jnp.concatenate(
            [
                wq[:, 2 * HD * t : 2 * HD * (t + 1)],
                wk[:, HD * t : HD * (t + 1)],
                wv[:, HD * t : HD * (t + 1)],
            ],
            axis=1,
        )
        slices_q[t, rows : rows + 1, :rows] = gain1[...]
        slices_q[t, rows + 1 : rows + 2, :rows] = gain2[...]
    relay_q = send(slices_q.at[t_relay], tmp_q, me.sibling())
    arrived_q = [
        send(slices_q.at[t_sib], gq.at[me.z, slot], me.sibling()),
        send(slices_q.at[t_toward], gq.at[me.z, slot], toward),
    ]
    own_q = send.local(slices_q.at[me.t], gq.at[me.z, slot])
    relay_q.wait_recv()
    arrived_q.append(send(tmp_q, gq.at[me.z, slot_other], away))
    own_tok = send.local(tok, tokv.at[me.t])
    down_z.forward()
    own_down.wait()
    own_down = send.local(down_v, down_w.at[me.z, down_rows(0)])

    part = wg.shape[1] // NT
    for t in range(NT):
        for n in range(4):
            at = n * 2 * CHUNK + t * TOK
            slices_u[t, :, n * TOK : (n + 1) * TOK] = wg[:, at : at + TOK]
            slices_u[t, :, part + n * TOK : part + (n + 1) * TOK] = wu[:, at : at + TOK]

    for t in range(NT):
        place = places_of(me, t, (TOK, TOK), 0)
        starts[t], _ = starts_of(lengths, place)

    own_q.wait()
    for copy in arrived_q:
        copy.wait_recv()
    qkv_z = Gather(send, me.along_z, lambda k: gq.at[me.z_at(k)], halves)
    tokens = Gather(send, me.along_y, lambda k: tokv.at[me.rank(k, c)], halves, tok)
    tok_sib = [send(tok, tokv.at[me.t], me.sibling())]
    own_down.wait()
    down_z.end()
    down_spread = lambda k: down_w.at[:, down_rows(k)]
    down_x = Gather(send, me.along_x, down_spread, halves)
    third = CHUNK * 3 // 4
    columns = lambda k: pl.ds(pl.multiple_of(me.x_at(k) * third, TOK), third)
    wo_part = wo.at[:, columns(0)]
    own_o = send.local(wo_part, o_w.at[me.z, me.yl, c, :, columns(0)])
    qkv_z.hand_on()
    tokens.hand_on()
    tokens.settle()
    tok_sib += [
        send(tokv.at[me.rank(k, c)], tokv.at[me.rank(k, c)], me.sibling()) for k in (-1, 1)
    ]
    arrived_o = send(wo_part, o_w.at[me.z, me.yl, c, :, columns(0)], toward)
    relay_u = send(slices_u.at[t_relay], tmp_u, me.sibling())
    arrived_u = [
        send(slices_u.at[t_sib], gu_w.at[me.z, slot], me.sibling()),
        send(slices_u.at[t_toward], gu_w.at[me.z, slot], toward),
    ]
    own_u = send.local(slices_u.at[me.t], gu_w.at[me.z, slot])
    relay_u.wait_recv()
    arrived_u.append(send(tmp_u, gu_w.at[me.z, slot_other], away))
    qkv_z.settle()
    qkv_z.end()
    own_tok.wait()

    gains = [
        jnp.concatenate(
            [gq[z, n, rows + g : rows + g + 1, :rows] for z in range(4) for n in range(4)], axis=1
        ).astype(F32)
        for g in range(2)
    ]
    gains_out[...] = jnp.concatenate(gains, axis=0)
    for z in range(4):
        for n in range(4):
            at = (z * 4 + n) * rows
            w = gq[z, n, :rows]
            qkv_w[at : at + rows] = w
            w_q[at : at + rows] = w[:, : 2 * HD]
            w_kv[at : at + rows] = w[:, 2 * HD :]

    def keys_and_values(k):
        ranks = (me.rank(k, c), me.rank(k, other))
        turns = []
        for t in ranks:
            place = places_of(me, t, (TOK, HD), 0)
            start, _ = starts_of(lengths, place)
            angle = (place - start).astype(F32) * freq[...]
            turns.append((jnp.cos(angle), jnp.sin(angle)))
            cosines[t], sines[t] = turns[-1]
        cosine, sine = (jnp.concatenate(both, axis=0) for both in zip(*turns))
        x = jnp.concatenate([tokv[t] for t in ranks], axis=0).astype(F32)
        h = x * lax.rsqrt(jnp.mean(x * x, axis=1, keepdims=True) + NORM_EPS)
        h = (h * gains[0]).astype(BF)
        pair = mm(h, w_kv[...])
        keys = turn(pair[:, :HD], cosine, sine)
        front_part = jnp.concatenate([keys, pair[:, HD:TOK]], axis=1).astype(BF)
        tail = pair[:, TOK:].astype(BF)
        for n, t in enumerate(ranks):
            of = slice(n * TOK, (n + 1) * TOK)
            h1[t] = h[of]
            kv[me.x, pl.ds(pl.multiple_of(t * TOK, TOK), TOK)] = front_part[of]
            at = pl.multiple_of(GROUP_ROWS + t * (TOK // 2), TOK // 2)
            kv[me.x, pl.ds(at, TOK // 2)] = pack_tail(tail[of])

    tok_sib[0].wait_recv()
    keys_and_values(0)
    for copy in tok_sib[1:]:
        copy.wait_recv()
    keys_and_values(1)
    keys_and_values(-1)
    tokens.end()
    far = tokv.at[me.rank(2, c)]
    tok_sib.append(send(far, far, me.sibling()))
    tok_sib[-1].wait_recv()
    keys_and_values(2)
    kvs = Gather(send, me.along_x, lambda k: kv.at[me.x_at(k)], halves)
    send.local(tokv, tok_all)
    send.local(h1, h1_out)
    own_o.wait()
    arrived_o.wait_recv()
    o_z = Gather(send, me.along_z, lambda k: o_w.at[me.z_at(k), :, c, :, columns(0)], halves)
    o_z.hand_on()
    own_u.wait()
    for copy in arrived_u:
        copy.wait_recv()
    Neighbours(send, me.along_z, gu_w.at[me.z], lambda k: gu_w.at[me.z_at(k)])
    cots = Gather(send, me.along_y, lambda k: cot_all.at[me.rank(k, c)], halves, cot)
    send(cot, cot_all.at[me.t], me.sibling())
    blank = jnp.zeros((QROWS, TOK - HD), BF)
    for i in range(4):
        h = jnp.concatenate([h1[2 * i], h1[2 * i + 1]], axis=0)
        both = mm(h, w_q[...])
        cosine, sine = (jnp.concatenate([a[2 * i], a[2 * i + 1]], axis=0) for a in (cosines, sines))
        for n in range(2):
            q = turn(both[:, n * HD : (n + 1) * HD], cosine, sine) * (SCALE * LOG2E)
            q = jnp.concatenate([q.astype(BF), blank], axis=1)
            q_out[2 * i, n * TOK : (n + 1) * TOK] = q[:TOK]
            q_out[2 * i + 1, n * TOK : (n + 1) * TOK] = q[TOK:]

    top[...] = jnp.full_like(top, -1e30)
    total[...] = jnp.zeros_like(total)
    acc[...] = jnp.zeros_like(acc)

    def source(s):
        x = lax.rem(me.x + s + s // 2 - 2 * (s // 3), 4)
        keyv[...] = unpack(kv[x], GROUP_ROWS)
        lane = lax.broadcasted_iota(jnp.int32, (QROWS, TOK), 1)
        for t in range(NT):
            n = (t + 1) * TOK
            q = q_out[t]
            score = mm_nt(q, keyv[:n, :TOK])
            start = jnp.concatenate([starts[t]] * 2, axis=0)
            kept = []
            for b in range(t + 1):
                key = lane + (b * CHUNK + x * TOK)
                keep = key >= start
                if b == t:
                    row = lax.broadcasted_iota(jnp.int32, (QROWS, TOK), 0)
                    keep = keep & (key <= lax.rem(row, TOK) + (t * CHUNK + me.x * TOK))
                kept.append(jnp.where(keep, score[:, b * TOK : (b + 1) * TOK], -jnp.inf))
            score = jnp.concatenate(kept, axis=1) if t else kept[0]
            old = top[t]
            new = jnp.maximum(old, jnp.max(score, axis=1, keepdims=True))
            p = jnp.exp2(score - new)
            factor = jnp.exp2(old - new)
            top[t] = new
            total[t] = total[t] * factor + jnp.sum(p, axis=1, keepdims=True)
            acc[t] = acc[t] * factor + mm(p.astype(BF), keyv[:n])

    down_x.hand_on()
    source(0)
    kvs.hand_on()
    kvs.settle()
    o_z.settle()
    o_z.end()
    spread = lambda k: o_w.at[:, :, c, :, columns(k)]
    Neighbours(send, me.along_x, spread(0), spread)
    pl.loop(1, 3)(source)
    cots.forward()
    for k in (-1, 1):
        send(cot_all.at[me.rank(k, c)], cot_all.at[me.rank(k, c)], me.sibling())
    kvs.end()
    source(3)
    send.local(kv, kv_out)
    for t in range(NT):
        o = acc[t][:, HD : 2 * HD] / total[t]
        lse = top[t] + jnp.log2(total[t])
        o_out[t] = o
        lse_out[t] = jnp.transpose(jnp.broadcast_to(lse, (QROWS, TOK)))[:1]
        place = places_of(me, t, (TOK, 2 * HD), 0)
        _, end = starts_of(lengths, place)
        ob = jnp.concatenate([o[:TOK], o[TOK:]], axis=1)
        ob = jnp.where(place < end, ob, 0.0).astype(BF)
        ob_out[t, :TOK] = ob[:, :TOK]
        ob_out[t, TOK:] = pack_tail(ob[:, TOK:])
    cots.end()
    far = cot_all.at[me.rank(2, c)]
    send(far, far, me.sibling())
    send.finish()


def front(lengths, tok, cot, wq, wk, wv, wg, wu, wo, wd, gain1, gain2):
    def like(*shape, dtype=BF):
        return jax.ShapeDtypeStruct(shape, dtype)

    rows, width = wq.shape
    part = wg.shape[1] // NT
    freq = jnp.asarray(np.tile(frequency_table(HD), 2)[None])
    outs = (
        (like(NT, TOK, width), ANY),
        (like(NT, TOK, width), ANY),
        (like(NT, TOK, width), ANY),
        (like(4, 4, rows, 2 * part), ANY),
        (like(4, 2, 2, rows, width), ANY),
        (like(4, TOK, width), ANY),
        (like(NX, PACKED, TOK), ANY),
        (like(NT, QROWS, TOK), VM),
        (like(NT, QROWS, HD, dtype=F32), VM),
        (like(NT, 1, QROWS, dtype=F32), VM),
        (like(NT, TOK * 3 // 2, TOK), VM),
        (like(2, width, dtype=F32), VM),
        (like(width, 4 * HD), VM),
    )
    padded = rows + 16
    return pl.pallas_call(
        front_kernel,
        out_shape=tuple(o[0] for o in outs),
        in_specs=[SM, VM, ANY, ANY, VM, VM, VM, VM, VM, VM, ANY, VM, VM],
        out_specs=tuple(o[1] for o in outs),
        scratch_shapes=[
            pltpu.VMEM((NT, TOK, width), BF),
            pltpu.VMEM((NT, TOK, width), BF),
            pltpu.VMEM((NT, padded, 4 * HD), BF),
            pltpu.VMEM((NT, rows, 2 * part), BF),
            pltpu.VMEM((padded, 4 * HD), BF),
            pltpu.VMEM((rows, 2 * part), BF),
            pltpu.VMEM((4, 4, padded, 4 * HD), BF),
            pltpu.VMEM((NX, PACKED, TOK), BF),
            pltpu.VMEM((GROUP_ROWS, 2 * TOK), BF),
            pltpu.VMEM((NT, TOK, TOK), jnp.int32),
            pltpu.VMEM((NT, QROWS, 1), F32),
            pltpu.VMEM((NT, QROWS, 1), F32),
            pltpu.VMEM((NT, QROWS, 2 * TOK), F32),
            pltpu.VMEM((width, 2 * HD), BF),
            pltpu.VMEM((width, 2 * HD), BF),
            pltpu.VMEM((TOK // 4, width), BF),
            pltpu.VMEM((NT, TOK, HD), F32),
            pltpu.VMEM((NT, TOK, HD), F32),
            pltpu.SemaphoreType.DMA((80,)),
            pltpu.SemaphoreType.DMA((80,)),
            pltpu.SemaphoreType.DMA((16,)),
        ],
        compiler_params=pltpu.CompilerParams(
            collective_id=0, has_side_effects=True, vmem_limit_bytes=56 * 2**20
        ),
        name="front",
    )(lengths, freq, tok, cot, wq, wk, wv, wg, wu, wo, wd, gain1, gain2)


class Scatter:
    def __init__(self, me, send, mine, sib, mid, far, near):
        self.me, self.send, self.mine, self.sib, self.mid = me, send, mine, sib, mid
        self.far, self.near, self.from_sib = far, near, {}
        self.half = sib.shape[1] // 2

    def hand(self, k, src):
        self.from_sib[k] = self.send(src, self.sib.at[k], self.me.sibling())

    def pair(self, k, i):
        rows = slice(i * self.half, (i + 1) * self.half)
        return self.mine(k, rows).astype(F32) + self.sib[k, rows].astype(F32)

    def put(self, k, i, value):
        self.mid[k, i * self.half : (i + 1) * self.half] = value.astype(BF)
        return self.mid.at[k, pl.ds(i * self.half, self.half)]

    def step2(self):
        self.from_sib[2].wait_recv()
        up, down = self.me.along_y(1), self.me.along_y(-1)
        self.far_up = self.send(self.put(2, 0, self.pair(2, 0)), self.far.at[0], up)
        self.far_down = self.send(self.put(2, 1, self.pair(2, 1)), self.far.at[1], down)

    def step1(self):
        self.from_sib[1].wait_recv()
        src = self.put(1, 1, self.pair(1, 1))
        self.last = [self.send(src, halves(self.near.at[0], 1), self.me.along_y(1))]

    def step3(self):
        self.from_sib[3].wait_recv()
        src = self.put(3, 0, self.pair(3, 0))
        self.last.append(self.send(src, halves(self.near.at[1], 0), self.me.along_y(-1)))

    def step0(self, i):
        k, copy = ((1, self.far_up), (3, self.far_down))[i]
        copy.wait_recv()
        src = self.put(k, i, self.pair(k, i) + self.far[i].astype(F32))
        self.last.append(
            self.send(src, halves(self.near.at[i], i), self.me.along_y(1 - 2 * i))
        )

    def end(self):
        self.from_sib[0].wait_recv()
        for copy in self.last:
            copy.wait_recv()
        total = self.mine(0, slice(None)).astype(F32) + self.sib[0].astype(F32)
        return total + self.near[0].astype(F32) + self.near[1].astype(F32)


class RingSum:
    def __init__(self, send, along, block, buffers):
        self.send, self.along, self.block = send, along, block
        self.far, self.direct, self.summed, self.mid = buffers

    def begin(self):
        self.begin_far()
        self.begin_near()

    def begin_far(self):
        send, up, down = self.send, self.along(1), self.along(-1)
        self.first = [
            send(halves(self.block(2), 0), self.far.at[0], up),
            send(halves(self.block(2), 1), self.far.at[1], down),
        ]

    def begin_near(self):
        send, up, down = self.send, self.along(1), self.along(-1)
        self.near = [
            send(halves(self.block(1), 1), self.direct.at[0], up),
            send(halves(self.block(3), 0), self.direct.at[1], down),
        ]

    def middle(self):
        self.last = []
        for i, k in enumerate((1, 3)):
            self.first[i].wait_recv()
            value = halves(self.block(k), i)[...].astype(F32) + self.far[i].astype(F32)
            self.mid[i] = value.astype(BF)
            self.last.append(
                self.send(self.mid.at[i], self.summed.at[i], self.along(2 * i + 1))
            )

    def end(self, to):
        for i in range(2):
            self.near[1 - i].wait_recv()
            self.last[i].wait_recv()
            value = halves(self.block(0), i)[...].astype(F32) + self.direct[1 - i].astype(F32)
            halves(to, i)[...] = (value + self.summed[i].astype(F32)).astype(BF)


def middle_kernel(
    lengths, ob, tok_all, cot_all, cot, o_w, gu_w, down_w, gains, o_in,
    go_out, delta_out, gx2_out, x2_out, y_out, u_out, d_sum, grad_o, gain_out,
    obv, obx, ow, guw, dw, cotv, tokv, h2, hid, ggu, ghs, mine, tosib, sib, mid, far, near, y_buf,
    grad_gu, grad_down, d_far, d_direct, d_summed, d_mid, o_buf,
    send_sem, recv_sem, local_sem,
):
    me = Place()
    me.greet(
        tuple(me.along_x(k) for k in (1, -1))
        + (me.along_z(1), me.along_z(-1), me.along_y(2))
    )
    send = Copies(send_sem, recv_sem, local_sem)
    c, other = me.c, 1 - me.c
    width = gains.shape[1]
    part = hid.shape[2]
    third = width // 4
    half = width // 2

    order = (2, 1, -1, 0)
    arrivals = []

    def tokens_of(ref, k):
        y = me.y_at(k)
        return ref.at[lax.rem(y, 2), :, y // 2]

    def send_tokens(i):
        arrivals.append(
            [
                send(
                    tokens_of(ob, d + order[i]), tokens_of(obv.at[me.t], d + order[i]), me.along_y(d)
                )
                for d in (1, -1, 2)
            ]
        )

    send_tokens(0)
    own_sib = send(ob, obv.at[me.t], me.sibling())
    own_ob = send.local(ob, obv.at[me.t])
    columns = lambda k: pl.ds(pl.multiple_of(me.x_at(k) * third, TOK), third)
    spread = lambda ref, k: ref.at[:, :, c, :, columns(k)]
    o_far = Relay(send, me.along_x, lambda k: spread(o_w, k), lambda k: spread(ow, k), halves)
    loads = [send.local(spread(o_w, k), spread(ow, k)) for k in (0, 1, -1)]
    loads.append(send.local(tok_all, tokv))
    gu_far = Relay(
        send, me.along_z, lambda k: gu_w.at[me.z_at(k)], lambda k: guw.at[me.z_at(k)], halves
    )
    quarter = TOK // 4

    send_tokens(1)
    loads += [send.local(gu_w.at[me.z_at(k)], guw.at[me.z_at(k)]) for k in (0, 1, -1)]
    down_spread = lambda ref, k: ref.at[
        :, pl.ds(pl.multiple_of(me.x_at(k) * quarter, quarter), quarter)
    ]
    late = [send.local(down_w, dw)]
    late.append(send.local(cot, cotv.at[me.t]))
    for k in range(4):
        for core in (c, other):
            if k or core is other:
                t = me.rank(k, core)
                late.append(send.local(cot_all.at[t], cotv.at[t]))
    from_sib = []

    def hand_over(i):
        for copy in arrivals[i]:
            copy.wait_recv()
        now = []
        for d in (1, -1, 2):
            block = tokens_of(obv.at[me.rank(d, c)], order[i])
            now.append(send(block, block, me.sibling()))
        from_sib.append(now)

    o_sib = []
    for n, k in enumerate((0, 1, -1)):
        loads[n].wait()
        o_sib.append(send(spread(ow, k), spread(ow, k), me.sibling()))
    hand_over(0)
    send_tokens(2)
    o_far.end()
    o_sib.append(send(spread(ow, 2), spread(ow, 2), me.sibling()))
    hand_over(1)
    send_tokens(3)
    for copy in late:
        copy.wait()

    @pl.loop(0, 4)
    def _(i):
        cot = jnp.concatenate([cotv[2 * i], cotv[2 * i + 1]], axis=0)
        gh = mm_nt(cot, dw[...].reshape(part, width))
        ghs[2 * i], ghs[2 * i + 1] = gh[:TOK], gh[TOK:]

    own_ob.wait()
    own_sib.wait_recv()
    for copy in loads[:4]:
        copy.wait()
    for copy in o_sib:
        copy.wait_recv()

    g2 = gains[1:2]
    sums = Scatter(me, send, lambda k, at: mine[k, at], sib, mid, far, near)
    w_gu = lambda: guw[...].reshape(width, 2 * part)
    w_down = lambda: dw[...].reshape(part, width)
    w_out = lambda: ow[...].reshape(width, width)

    def feed(i, between=None):
        k = order[i] % 4
        for copy in from_sib[i]:
            copy.wait_recv()
        ranks = (me.rank(k, c), me.rank(k, other))
        heads = []
        for s in range(NT):
            blocks = [obv[s, t // 4, lax.rem(t // 2, 2), lax.rem(t, 2)] for t in ranks]
            heads.append(
                jnp.concatenate([unpack(block, TOK)[:, : 2 * HD] for block in blocks], axis=0)
            )
        heads = jnp.concatenate(heads, axis=1)
        x = jnp.concatenate([tokv[t] for t in ranks], axis=0).astype(F32) + mm(heads, w_out())
        if k == 0:
            x2_out[...] = x[:TOK]
        h = x * lax.rsqrt(jnp.mean(x * x, axis=1, keepdims=True) + NORM_EPS)
        h = (h * g2).astype(BF)
        if i == 0:
            gu_far.end()
            for copy in loads[4:]:
                copy.wait()
        if between is not None:
            between()
        gu = mm(h, w_gu())
        gate, up = gu[:, :part], gu[:, part:]
        sigmoid = 1.0 / (1.0 + jnp.exp(-gate))
        silu = gate * sigmoid
        hidden = (silu * up).astype(BF)
        gh = jnp.concatenate([ghs[t] for t in ranks], axis=0)
        ggate = (gh * up * sigmoid * (1.0 + gate * (1.0 - sigmoid))).astype(BF)
        gup = (gh * silu).astype(BF)
        both = jnp.concatenate([ggate, gup], axis=1)
        gh2 = mm_nt(both, w_gu()).astype(BF)
        mine[k], tosib[k] = gh2[:TOK], gh2[TOK:]
        sums.hand(k, tosib.at[k])
        y = mm(hidden, w_down()).astype(BF)
        for n, t in enumerate(ranks):
            rows = slice(n * TOK, (n + 1) * TOK)
            obx[t], h2[t], hid[t], ggu[t], y_buf[t] = (
                heads[rows], h[rows], hidden[rows], both[rows], y[rows],
            )

    feed(0)
    hand_over(2)
    feed(1)
    hand_over(3)
    sums.step2()
    feed(2, sums.step1)
    sums.step0(0)

    def third_block():
        sums.step3()
        sums.step0(1)

    feed(3, third_block)
    send.local(y_buf, y_out)
    gh2 = sums.end()
    x = x2_out[...]
    r2 = lax.rsqrt(jnp.mean(x * x, axis=1, keepdims=True) + NORM_EPS)
    n2 = x * r2
    gm = gh2 * g2
    gain_out[...] = jnp.sum(gh2 * n2, axis=0, keepdims=True)
    gx2 = r2 * (gm - n2 * jnp.mean(gm * n2, axis=1, keepdims=True)) + cotv[me.t].astype(F32)
    gx2_out[...] = gx2
    gav = tokv
    gav[me.t] = gx2.astype(BF)
    back = Gather(send, me.along_y, lambda k: gav.at[me.rank(k, c)], halves)
    back_sib = [send(gav.at[me.t], gav.at[me.t], me.sibling())]

    @pl.loop(0, 3)
    def _(n):
        cols = pl.ds(pl.multiple_of(n * CHUNK, CHUNK), CHUNK)
        cot = cotv[:, :, cols].reshape(GROUP_ROWS, CHUNK)
        value = mm_tn(hid[...].reshape(GROUP_ROWS, part), cot).astype(BF)
        grad_down[:, :, cols] = value.reshape(4, TOK, CHUNK)

    down_sum = RingSum(
        send, me.along_x, lambda k: down_spread(grad_down, k), (d_far, d_direct, d_summed, d_mid)
    )
    down_sum.begin()

    def grad_columns(k):
        z = me.z_at(k)
        cols = pl.ds(pl.multiple_of(z * 4 * HD, TOK), 4 * HD)
        h = h2[:, :, cols].reshape(GROUP_ROWS, 4 * HD)
        value = mm_tn(h, ggu[...].reshape(GROUP_ROWS, 2 * part)).astype(BF)
        for n in range(4):
            for j in range(8):
                grad_gu[z, n, j * HD : (j + 1) * HD] = value[
                    n * HD : (n + 1) * HD, j * TOK : (j + 1) * TOK
                ]

    pl.loop(0, 1)(grad_columns)
    back.forward()
    back_sib += [
        send(gav.at[me.rank(k, c)], gav.at[me.rank(k, c)], me.sibling()) for k in (-1, 1)
    ]
    pl.loop(1, 3)(grad_columns)
    down_sum.middle()
    pl.loop(3, 4)(grad_columns)
    send.local(grad_gu, u_out)

    w_own = ow[me.t // 2, lax.rem(me.t, 2)].reshape(2 * HD, width)

    def attention_gradient(k):
        ranks = (me.rank(k, c), me.rank(k, other))
        ga = jnp.concatenate([gav[t] for t in ranks], axis=0)
        go_both = mm_nt(ga, w_own)
        for n, t in enumerate(ranks):
            place = places_of(me, t, (TOK, 2 * HD), 0)
            _, end = starts_of(lengths, place)
            go = jnp.where(place < end, go_both[n * TOK : (n + 1) * TOK], 0.0).astype(BF)
            both = jnp.concatenate([go[:, h * HD : (h + 1) * HD] for h in range(2)], axis=0)
            delta = jnp.sum(both.astype(F32) * o_in[t], axis=1, keepdims=True)
            delta_out[t] = jnp.transpose(jnp.broadcast_to(delta, (QROWS, TOK)))[:1]
            before, after = jnp.zeros((QROWS, HD), BF), jnp.zeros((QROWS, 2 * TOK - 2 * HD), BF)
            go_out[t] = jnp.concatenate([before, both, after], axis=1)

    for copy in back_sib:
        copy.wait_recv()
    attention_gradient(0)
    attention_gradient(1)
    attention_gradient(-1)
    back.end()
    last = send(gav.at[me.rank(2, c)], gav.at[me.rank(2, c)], me.sibling())
    down_sum.end(d_sum)
    last.wait_recv()
    attention_gradient(2)
    ga_half = gav[:, :, pl.ds(pl.multiple_of(me.yh * half, half), half)].reshape(GROUP_ROWS, half)
    for z in range(4):
        block = obx[:, :, z * 4 * HD : (z + 1) * 4 * HD].reshape(GROUP_ROWS, 4 * HD)
        o_buf[...] = mm_tn(block, ga_half)
        at = pl.multiple_of((me.yl * 2 + c) * HD, 8)
        value = o_buf[pl.ds(at, HD)].astype(BF)
        for j in range(6):
            grad_o[z, j * HD : (j + 1) * HD] = value[:, j * TOK : (j + 1) * TOK]
        grad_o[z, 6 * HD :] = jnp.zeros_like(grad_o[z, 6 * HD :])
    send.finish()


def middle(lengths, ob, tok_all, cot_all, cot, o_w, gu_w, down_w, gains, o):
    def like(*shape, dtype=BF):
        return jax.ShapeDtypeStruct(shape, dtype)

    def vmem(*shape, dtype=BF):
        return pltpu.VMEM(shape, dtype)

    width = o_w.shape[-1]
    part = gu_w.shape[-1] // 2
    grad_u = (4, 4, 2 * part * HD // TOK, TOK)
    outs = (
        (like(NT, QROWS, 2 * TOK), VM),
        (like(NT, 1, QROWS, dtype=F32), VM),
        (like(TOK, width, dtype=F32), VM),
        (like(TOK, width, dtype=F32), VM),
        (like(NT, TOK, width), ANY),
        (like(*grad_u), ANY),
        (like(4, TOK // 4, width), VM),
        (like(4, 6 * HD + 64, TOK), VM),
        (like(1, width, dtype=F32), VM),
    )
    return pl.pallas_call(
        middle_kernel,
        out_shape=tuple(o[0] for o in outs),
        in_specs=[SM] + [ANY] * 7 + [VM, VM],
        out_specs=tuple(o[1] for o in outs),
        scratch_shapes=[
            vmem(NT, 2, 2, 2, TOK * 3 // 2, TOK),
            vmem(NT, TOK, width),
            vmem(*o_w.shape),
            vmem(*gu_w.shape),
            vmem(4, TOK, width),
            vmem(NT, TOK, width),
            vmem(NT, TOK, width),
            vmem(NT, TOK, width),
            vmem(NT, TOK, part),
            vmem(NT, TOK, 2 * part),
            vmem(NT, TOK, part, dtype=F32),
            vmem(4, TOK, width),
            vmem(4, TOK, width),
            vmem(4, TOK, width),
            vmem(4, TOK, width),
            vmem(2, TOK // 2, width),
            vmem(2, TOK, width),
            vmem(NT, TOK, width),
            vmem(*grad_u),
            vmem(4, TOK, width),
            *[vmem(2, 2, TOK // 4, width)] * 4,
            vmem(4 * HD, width // 2, dtype=F32),
            pltpu.SemaphoreType.DMA((80,)),
            pltpu.SemaphoreType.DMA((80,)),
            pltpu.SemaphoreType.DMA((24,)),
        ],
        compiler_params=pltpu.CompilerParams(
            collective_id=1, has_side_effects=True, vmem_limit_bytes=63 * 2**20
        ),
        name="middle",
    )(lengths, ob, tok_all, cot_all, cot, o_w, gu_w, down_w, gains, o)


class Exchange:
    def __init__(self, me, send, block, from_sib, slots):
        self.me, self.send, self.block, self.from_sib, self.slots = me, send, block, from_sib, slots
        other = 1 - me.c
        self.first = [
            send(block.at[yl * 2 + other], from_sib.at[yl], me.sibling()) for yl in range(2)
        ]

    def second(self):
        me = self.me
        for copy in self.first:
            copy.wait_recv()
        mine, theirs = me.t, me.rank(0, 1 - me.c)
        self.copies = []
        for k, yl in ((1, 1 - me.yl), (-1, 1 - me.yl), (2, me.yl)):
            for src, t in ((self.block.at[yl * 2 + me.c], mine), (self.from_sib.at[yl], theirs)):
                self.copies.append(self.send(src, self.slots.at[t], me.along_y(k)))
        self.slots[mine] = self.block[me.yl * 2 + me.c]
        self.slots[theirs] = self.from_sib[me.yl]

    def end(self):
        for copy in self.copies:
            copy.wait_recv()


def back_kernel(
    lengths, freq, kv, q_in, go_in, lse, delta, y_hbm, gu_hbm, d_sum, grad_o,
    h1_hbm, tok_hbm, qkv_hbm, gx2, x2_own, gains, gain2,
    layer_out, tokens_grad, all_gu, all_q, all_down, all_o,
    y_mine, grad_gu, u_far, u_direct, h1, tokv, qkv_w,
    keyv, gkv, gq, staged, kv_far, kv_direct, kv_summed, kv_mid, g_query, g_pair, gain_part, starts,
    y_sib, y_mid, y_far, y_near, mine, tosib, sib, mid, far, near, grad_q,
    u_summed, u_mid, o_far, o_direct, o_summed, o_mid, q_far, q_direct, q_summed, q_mid,
    u_sum, o_sum, q_sum,
    ux_far, ux_direct, ux_summed, ux_mid, d_far, d_direct, d_summed, d_mid,
    ox_far, ox_direct, ox_summed, ox_mid, qx_far, qx_direct, qx_summed, qx_mid,
    u_mine, q_mine, u_from, q_from,
    send_sem, recv_sem, local_sem,
):
    me = Place()
    me.greet(
        tuple(me.along_x(k) for k in (1, -1, 2))
        + (me.along_z(1), me.along_z(-1), me.along_y(2))
    )
    send = Copies(send_sem, recv_sem, local_sem)
    c, other = me.c, 1 - me.c
    rows = HD

    def over_z(ref, buffers):
        return RingSum(send, me.along_z, lambda k: ref.at[me.z_at(k)], buffers)

    def quarters(ref, size, leading):
        def block(k):
            at = pl.ds(pl.multiple_of(me.x_at(k) * size, 16), size)
            return ref.at[:, at] if leading else ref.at[at]

        return block

    ys = Scatter(me, send, lambda k, at: y_mine[k, at], y_sib, y_mid, y_far, y_near)
    for k in (2, 1, 3, 0):
        ys.hand(k, y_hbm.at[me.rank(k, other)])
    down_z = over_z(d_sum, (d_far, d_direct, d_summed, d_mid))
    down_z.begin()
    out_z = over_z(grad_o, (o_far, o_direct, o_summed, o_mid))
    out_z.begin()
    loads = [send.local(y_hbm.at[me.rank(k, c)], y_mine.at[k]) for k in range(4)]
    loads += [send.local(gu_hbm.at[me.z_at(k)], grad_gu.at[me.z_at(k)]) for k in (1, 3, 0)]
    late = [send.local(qkv_hbm, qkv_w), send.local(h1_hbm, h1), send.local(tok_hbm, tokv)]

    def over_x(ref):
        return Gather(send, me.along_x, lambda k: ref.at[me.x_at(k)], halves)

    for t in range(NT):
        starts[t], _ = starts_of(lengths, places_of(me, t, (1, TOK), 1))
    gq[...] = jnp.zeros_like(gq)
    lane = lax.broadcasted_iota(jnp.int32, (1, 2 * TOK), 1)
    lane_scale = jnp.where(lane < HD, LN2, 1.0)

    def source(k):
        x = me.x_at(k)
        keyv[...] = unpack(kv[x], GROUP_ROWS)
        gkv[...] = jnp.zeros_like(gkv)
        row = lax.broadcasted_iota(jnp.int32, (TOK, QROWS), 0)
        for t in range(NT):
            n = (t + 1) * TOK
            q, go = q_in[t], go_in[t]
            start = jnp.concatenate([starts[t]] * 2, axis=1)
            p = jnp.exp2(mm_nt(keyv[:n, :TOK], q) - lse[t])
            kept = []
            for b in range(t + 1):
                key = row + (b * CHUNK + x * TOK)
                keep = key >= start
                if b == t:
                    column = lax.broadcasted_iota(jnp.int32, (TOK, QROWS), 1)
                    keep = keep & (key <= lax.rem(column, TOK) + (t * CHUNK + me.x * TOK))
                kept.append(jnp.where(keep, p[b * TOK : (b + 1) * TOK], 0.0))
            p = jnp.concatenate(kept, axis=0) if t else kept[0]
            gp = mm_nt(keyv[:n], go)
            gs = (p * (gp - delta[t])).astype(BF)
            gkv[:n] += mm(p.astype(BF), go)
            gkv[:n, :TOK] += mm(gs, q)
            gq[t] += mm_tn(gs, keyv[:n, :TOK])

    def stage(n):
        value = (gkv[...] * lane_scale).astype(BF)
        staged[n, :GROUP_ROWS] = value[:, :TOK]
        for t in range(NT):
            at = GROUP_ROWS + t * (TOK // 2)
            tail = value[t * TOK : (t + 1) * TOK, TOK : TOK + TOK // 2]
            staged[n, at : at + TOK // 2] = pack_tail(tail)

    kv_sum = RingSum(
        send,
        me.along_x,
        lambda k: staged.at[(None, 1, 0, 2)[k]],
        (kv_far, kv_direct, kv_summed, kv_mid),
    )
    source(2)
    stage(0)
    kv_sum.begin_far()
    down_z.middle()
    out_z.middle()
    over_z(gu_hbm, (u_far, u_direct, u_summed, u_mid)).begin()
    gu_first = send.all[-4:]
    gu_z = over_z(grad_gu, (u_far, u_direct, u_summed, u_mid))
    gu_z.first, gu_z.near = gu_first[:2], gu_first[2:]
    for copy in loads[:4]:
        copy.wait()
    ys.step2()
    ys.step1()

    @pl.loop(0, 2)
    def _(n):
        source(2 * n + 1)
        stage(n + 1)

    kv_sum.begin_near()
    kv_sum.middle()
    down_z.end(all_down.at[me.x, me.yh])
    down_y = send(all_down.at[me.x, me.yh], all_down.at[me.x, me.yh], me.along_y(2))
    out_z.end(o_sum)
    out_x = RingSum(
        send,
        me.along_x,
        quarters(o_sum, o_sum.shape[0] // 4, False),
        (ox_far, ox_direct, ox_summed, ox_mid),
    )
    out_x.begin()
    ys.step3()
    ys.step0(0)
    ys.step0(1)
    source(0)
    for copy in loads[4:] + late:
        copy.wait()

    def back_angles(i):
        place = places_of(me, 2 * i, (QROWS, HD), 0)
        start, _ = starts_of(lengths, place)
        angle = (place - start).astype(F32) * freq[...]
        return jnp.cos(angle), -jnp.sin(angle)

    span = 4 * rows
    h_of = lambda z: h1[:, :, z * span : (z + 1) * span].reshape(GROUP_ROWS, span)
    w_of = lambda z: qkv_w[z * span : (z + 1) * span].astype(F32)
    for i in range(4):
        cosine, sine = back_angles(i)
        at = slice(i * QROWS, (i + 1) * QROWS)
        parts = []
        for h in range(2):
            of = slice(h * TOK, (h + 1) * TOK)
            g = jnp.concatenate([gq[2 * i, of, :HD], gq[2 * i + 1, of, :HD]], axis=0)
            parts.append(turn(g * SCALE, cosine, sine))
        g_query[at] = jnp.concatenate(parts, axis=1).astype(BF)
    for z in range(4):
        g = mm_tn(h_of(z), g_query[...])
        gain_part[z] = jnp.sum(g * w_of(z)[:, : 2 * HD], axis=1, keepdims=True)
        g = g.astype(BF)
        for n in range(4):
            part = slice(n * rows, (n + 1) * rows)
            grad_q[z, n, :rows] = g[part, :TOK]
            grad_q[z, n, rows : 2 * rows, : TOK // 2] = g[part, TOK:]
    out_x.middle()
    down_y.wait_recv()
    for i in range(2):
        kv_sum.near[1 - i].wait_recv()
        kv_sum.last[i].wait_recv()
    others = [kv_direct[1 - i].astype(F32) + kv_summed[i].astype(F32) for i in range(2)]
    gkv[...] = gkv[...] * lane_scale + unpack(jnp.concatenate(others, axis=0), GROUP_ROWS)
    gu_z.middle()
    down_all = over_x(all_down)
    out_x.end(all_o.at[me.x, me.yh])
    out_y = send(all_o.at[me.x, me.yh], all_o.at[me.x, me.yh], me.along_y(2))

    g1 = gains[0:1]
    for i in range(4):
        cosine, sine = back_angles(i)
        at = slice(i * QROWS, (i + 1) * QROWS)
        parts = [turn(gkv[at, :HD], cosine, sine), gkv[at, HD : 2 * HD]]
        g_pair[at] = jnp.concatenate(parts, axis=1).astype(BF)
    for z in range(4):
        g = mm_tn(h_of(z), g_pair[...])
        of_gain = gain_part[z] + jnp.sum(g * w_of(z)[:, 2 * HD :], axis=1, keepdims=True)
        g = g.astype(BF)
        for n in range(4):
            part = slice(n * rows, (n + 1) * rows)
            grad_q[z, n, rows : 2 * rows, TOK // 2 :] = g[part, : TOK // 2]
            grad_q[z, n, 2 * rows : 3 * rows] = g[part, TOK // 2 :]
            at = slice(z * span + n * rows, z * span + (n + 1) * rows)
            first = jnp.transpose(jnp.broadcast_to(of_gain[part], (rows, TOK)))[:1] / g1[:, at]
            extra = jnp.concatenate([first, gain2[:, at]], axis=0)
            extra = jnp.concatenate([extra, jnp.zeros((30, rows), F32)], axis=0)
            extra = jnp.concatenate([extra, jnp.zeros((32, TOK - rows), F32)], axis=1)
            grad_q[z, n, 3 * rows :] = extra.astype(BF)
    q_z = over_z(grad_q, (q_far, q_direct, q_summed, q_mid))
    q_z.begin()
    down_all.forward()
    out_y.wait_recv()
    out_all = over_x(all_o)

    h_sums = Scatter(me, send, lambda k, at: mine[k, at], sib, mid, far, near)

    def feed(k):
        ranks = (me.rank(k, c), me.rank(k, other))
        g = [
            jnp.concatenate([ref[pl.ds(pl.multiple_of(t * TOK, TOK), TOK)] for ref in (g_query, g_pair)], axis=1)
            for t in ranks
        ]
        low = mm_nt(jnp.concatenate(g, axis=0), qkv_w[...]).astype(BF)
        mine[k], tosib[k] = low[:TOK], low[TOK:]
        h_sums.hand(k, tosib.at[k])

    feed(2)
    gu_z.end(u_sum)
    gu_x = RingSum(
        send,
        me.along_x,
        quarters(u_sum, u_sum.shape[1] // 4, True),
        (ux_far, ux_direct, ux_summed, ux_mid),
    )
    gu_x.begin()
    feed(1)
    h_sums.step2()
    feed(3)
    h_sums.step1()
    out_all.forward()
    q_z.middle()
    gu_x.middle()
    feed(0)
    h_sums.step3()
    gu_x.end(u_mine)
    u_rows = Exchange(me, send, u_mine, u_from, all_gu.at[me.x])
    layer_out[...] = (x2_own[...] + ys.end()).astype(BF)
    h_sums.step0(0)
    h_sums.step0(1)
    u_rows.second()
    q_z.end(q_sum)
    q_x = RingSum(
        send,
        me.along_x,
        quarters(q_sum, q_sum.shape[1] // 4, True),
        (qx_far, qx_direct, qx_summed, qx_mid),
    )
    q_x.begin()
    q_x.middle()
    q_x.end(q_mine)
    q_rows = Exchange(me, send, q_mine, q_from, all_q.at[me.x])
    u_rows.end()
    gu_all = over_x(all_gu)
    q_rows.second()
    gh1 = h_sums.end()
    x = tokv[...].astype(F32)
    r1 = lax.rsqrt(jnp.mean(x * x, axis=1, keepdims=True) + NORM_EPS)
    n1 = x * r1
    gn = gh1 * g1
    gx = gx2[...] + r1 * (gn - n1 * jnp.mean(gn * n1, axis=1, keepdims=True))
    tokens_grad[...] = gx.astype(BF)
    q_rows.end()
    q_all = over_x(all_q)
    gu_all.hand_on()
    q_all.forward()
    send.finish()


def back(*args):
    lengths = args[0]
    grad_gu, grad_o, qkv_w = args[7], args[9], args[12]
    half_u = (2, 2) + grad_gu.shape[2:]
    freq = jnp.asarray(np.tile(frequency_table(HD), 2)[None])
    width = qkv_w.shape[0]
    u_rows, o_rows = grad_gu.shape[2], grad_o.shape[1]
    q_rows = 3 * HD + 32

    def like(*shape, dtype=BF):
        return jax.ShapeDtypeStruct(shape, dtype)

    def vmem(*shape, dtype=BF):
        return pltpu.VMEM(shape, dtype)

    def ring(*shape):
        half = (shape[0] // 2,) + shape[1:]
        return [vmem(2, *half)] * 4

    def group(mine):
        head = [vmem(4, TOK, width)] * (4 if mine else 2)
        return head + [vmem(2, TOK // 2, width), vmem(2, TOK, width)]

    outs = (
        like(TOK, width),
        like(TOK, width),
        like(4, NT, u_rows // 4, TOK),
        like(4, NT, q_rows // 4, TOK),
        like(4, 2, TOK // 4, width),
        like(4, 2, o_rows // 4, TOK),
    )
    return pl.pallas_call(
        back_kernel,
        out_shape=outs,
        in_specs=[SM] + [VM] * 6 + [ANY] * 2 + [VM] * 2 + [ANY] * 3 + [VM] * 4,
        out_specs=(VM,) * len(outs),
        scratch_shapes=[
            vmem(4, TOK, width),
            vmem(*grad_gu.shape),
            vmem(*half_u),
            vmem(*half_u),
            vmem(NT, TOK, width),
            vmem(TOK, width),
            vmem(*qkv_w.shape),
            vmem(GROUP_ROWS, 2 * TOK),
            vmem(GROUP_ROWS, 2 * TOK, dtype=F32),
            vmem(NT, QROWS, TOK, dtype=F32),
            vmem(3, PACKED, TOK),
            *[vmem(2, PACKED // 2, TOK)] * 4,
            vmem(GROUP_ROWS, 2 * HD),
            vmem(GROUP_ROWS, 2 * HD),
            vmem(4, 4 * HD, 1, dtype=F32),
            vmem(NT, 1, TOK, dtype=jnp.int32),
            *group(False),
            *group(True),
            vmem(4, 4, q_rows, TOK),
            vmem(*half_u),
            vmem(*half_u),
            *ring(o_rows, TOK),
            *ring(4, q_rows, TOK),
            vmem(4, u_rows, TOK),
            vmem(o_rows, TOK),
            vmem(4, q_rows, TOK),
            *ring(4, u_rows // 4, TOK),
            *ring(TOK // 4, width),
            *ring(o_rows // 4, TOK),
            *ring(4, q_rows // 4, TOK),
            vmem(4, u_rows // 4, TOK),
            vmem(4, q_rows // 4, TOK),
            vmem(2, u_rows // 4, TOK),
            vmem(2, q_rows // 4, TOK),
            pltpu.SemaphoreType.DMA((128,)),
            pltpu.SemaphoreType.DMA((128,)),
            pltpu.SemaphoreType.DMA((16,)),
        ],
        compiler_params=pltpu.CompilerParams(
            collective_id=2, has_side_effects=True, vmem_limit_bytes=63 * 2**20
        ),
        name="back",
    )(lengths, freq, *args[1:])


def finish_kernel(
    layer_hbm, tokens_hbm, gu_hbm, q_hbm, down_hbm, o_hbm,
    layer_to, tokens_to, q_to, k_to, v_to, o_to, gate_to, up_to, down_to, to_gain1, to_gain2,
    all_gu, all_q, all_down, all_o, layer, tok, to_q, to_k, to_v, to_o, to_gate, to_up, to_down, sem,
):
    pairs = (
        (gu_hbm, all_gu), (down_hbm, all_down), (o_hbm, all_o), (q_hbm, all_q),
        (layer_hbm, layer), (tokens_hbm, tok),
    )
    reads = [pltpu.make_async_copy(a, b, sem.at[i]) for i, (a, b) in enumerate(pairs)]
    for copy in reads:
        copy.start()
    writes = []

    def leave(src, dst):
        copy = pltpu.make_async_copy(src, dst, sem.at[len(pairs) + len(writes)])
        copy.start()
        writes.append(copy)

    reads[0].wait()
    for j in range(8):
        to, at = (to_gate, to_up)[j // 4], (j % 4) * 2 * CHUNK
        for t in range(NT):
            tile = all_gu[j // 2, t, (j % 2) * HD : (j % 2 + 1) * HD].astype(F32)
            to[:, at + t * TOK : at + (t + 1) * TOK] = tile
        if j == 3:
            leave(to_gate, gate_to)
    leave(to_up, up_to)
    reads[1].wait()
    size = all_down.shape[2]
    for yh in range(2):
        for x in range(4):
            at = yh * TOK + x * size
            to_down[at : at + size] = all_down[x, yh].astype(F32)
    leave(to_down, down_to)
    reads[2].wait()
    for yh in range(2):
        value = jnp.concatenate([all_o[x, yh] for x in range(4)], axis=0).astype(F32)
        for j in range(6):
            at = (yh * 6 + j) * TOK
            to_o[:, at : at + TOK] = value[j * HD : (j + 1) * HD]
    leave(to_o, o_to)
    reads[3].wait()
    gains = jnp.zeros((2, TOK), F32)
    heads = []
    for t in range(NT):
        value = jnp.concatenate([all_q[x, t] for x in range(4)], axis=0).astype(F32)
        tiles = [value[j * HD : (j + 1) * HD] for j in range(3)]
        heads.append(jnp.concatenate(tiles, axis=1))
        gains += value[3 * HD : 3 * HD + 2]
    to_q[...] = jnp.concatenate([h[:, : 2 * HD] for h in heads], axis=1)
    leave(to_q, q_to)
    to_k[...] = jnp.concatenate([h[:, 2 * HD : 3 * HD] for h in heads], axis=1)
    leave(to_k, k_to)
    to_v[...] = jnp.concatenate([h[:, 3 * HD :] for h in heads], axis=1)
    leave(to_v, v_to)
    to_gain1[...] = gains[0, :HD]
    to_gain2[...] = gains[1, :HD]
    reads[4].wait()
    leave(layer, layer_to.at[0])
    reads[5].wait()
    leave(tok, tokens_to.at[0])
    for copy in writes:
        copy.wait()


def finish(layer_out, tokens_grad, all_gu, all_q, all_down, all_o):
    rows, width = layer_out.shape
    part = all_gu.shape[2] * 4 // HD * TOK // 2
    shapes = [
        ((1, rows, width), BF),
        ((1, rows, width), BF),
        ((HD, width), F32),
        ((HD, width // 2), F32),
        ((HD, width // 2), F32),
        ((HD, width), F32),
        ((HD, NT * part), F32),
        ((HD, NT * part), F32),
        ((2 * TOK, width), F32),
        ((HD,), F32),
        ((HD,), F32),
    ]
    return pl.pallas_call(
        finish_kernel,
        out_shape=tuple(jax.ShapeDtypeStruct(*s) for s in shapes),
        in_specs=[ANY] * 6,
        out_specs=(ANY,) * 9 + (VM, VM),
        scratch_shapes=[pltpu.VMEM(a.shape, BF) for a in (all_gu, all_q, all_down, all_o)]
        + [pltpu.VMEM((rows, width), BF)] * 2
        + [pltpu.VMEM(*s) for s in shapes[2:9]]
        + [pltpu.SemaphoreType.DMA((16,))],
        compiler_params=pltpu.CompilerParams(vmem_limit_bytes=63 * 2**20),
        name="finish",
    )(layer_out, tokens_grad, all_gu, all_q, all_down, all_o)


def body(
    tokens,
    doc_lengths,
    w_query,
    w_key,
    w_value,
    w_output,
    w_gate,
    w_up,
    w_down,
    gain_attn,
    gain_mlp,
    cotangent,
):
    tok_all, cot_all, h1, gu_w, o_w, down_w, kv, q, o, lse, ob, gains, qkv_w = front(
        doc_lengths,
        tokens[0],
        cotangent[0],
        w_query,
        w_key,
        w_value,
        w_gate,
        w_up,
        w_output,
        w_down,
        gain_attn.reshape(1, -1),
        gain_mlp.reshape(1, -1),
    )
    ob = ob.reshape((2, 2, 2) + ob.shape[1:])
    go, delta, gx2, own, y_part, grad_gu, d_sum, grad_o, gain2 = middle(
        doc_lengths, ob, tok_all, cot_all, cotangent[0], o_w, gu_w, down_w, gains, o
    )
    sums = back(
        doc_lengths, kv, q, go, lse, delta, y_part, grad_gu, d_sum, grad_o, h1, tokens[0], qkv_w,
        gx2, own, gains, gain2,
    )
    return finish(*sums)


def solution(mesh):
    fine = Mesh(mesh.devices.reshape(4, 2, 2, 2, 4), AXES)
    by_token = P("z", ("yl", "c", "yh", "x"), None)
    by_row = P(("z", "yl", "c"), None)
    by_feature = P(("z", "yl", "c"))
    return jax.shard_map(
        body,
        mesh=fine,
        in_specs=(by_token, P("z", None))
        + (by_row,) * 7
        + (by_feature, by_feature, by_token),
        out_specs=(by_token, by_token) + (by_row,) * 7 + (by_feature, by_feature),
        check_vma=False,
    )
```
